32 devices in a mesh: dp: 8 (over z, y), seq: 4 (over x, core).
Axes of the slice: x: 2, y: 2, z: 4, core: 2. Of those that a mesh axis runs over, the one named last changes fastest.
Arguments:
- inputs: bfloat16 [4, 4096, 768], P(None, ('dp', 'seq')), may hold values from -6 to 6
- time_table: bfloat16 [1000, 768], P(None, ('dp', 'seq')), may hold values from -3 to 3
- w_qkv: bfloat16 [768, 2304], P(None, ('dp', 'seq')), may hold values from -0.21875 to 0.21875
- w_out: bfloat16 [768, 768], P(None, ('dp', 'seq')), may hold values from -1.25 to 1.25
- w_up: bfloat16 [768, 3072], P(None, ('dp', 'seq')), may hold values from -0.21875 to 0.21875
- w_down: bfloat16 [3072, 768], P(None, ('dp', 'seq')), may hold values from -0.109375 to 0.109375
- norm_gains: bfloat16 [2, 768], P(None, ('dp', 'seq')), may hold values from 0.5 to 1.5
- norm_shifts: bfloat16 [2, 768], P(None, ('dp', 'seq')), may hold values from -4 to 4
- biases: bfloat16 [4, 768], P(None, ('dp', 'seq')), may hold values from -4 to 4
- up_bias: bfloat16 [1, 3072], P(None, ('dp', 'seq')), may hold values from -4 to 4
- timesteps: int32 [96], replicated, may hold values from 0 to 999
- item_map: int32 [96], P('dp'), may hold values from 0 to 95, each once
- lengths: int32 [32, 3], P('dp'), may hold values from 1 to 256, 512 in all within a row
- cotangent: bfloat16 [4, 4096, 768], P(None, ('dp', 'seq')), may hold values from -6 to 6
Outputs:
- output: bfloat16 [4, 4096, 768], P(None, ('dp', 'seq'))
- input_grad: bfloat16 [4, 4096, 768], P(None, ('dp', 'seq'))
- table_grad: float32 [1000, 768], P(None, ('dp', 'seq'))
- qkv_grad: float32 [768, 2304], P(None, ('dp', 'seq'))
- out_grad: float32 [768, 768], P(None, ('dp', 'seq'))
- up_grad: float32 [768, 3072], P(None, ('dp', 'seq'))
- down_grad: float32 [3072, 768], P(None, ('dp', 'seq'))
- gains_grad: float32 [2, 768], P(None, ('dp', 'seq'))
- shifts_grad: float32 [2, 768], P(None, ('dp', 'seq'))
- biases_grad: float32 [4, 768], P(None, ('dp', 'seq'))
- up_bias_grad: float32 [1, 3072], P(None, ('dp', 'seq'))
The draws below stay inside these ranges and needn't reach their ends.
Inputs may be any that keep to these rules, and one draw needn't show every extreme that they name: Each row of lengths sums to 512, and its largest entry is exactly 256. item_map holds each of the 96 items once.
All inputs are finite; a program needn't handle non-finite values.
Results may differ from the reference program's by a relative error of at most 0.0085.
Values may be sent and summed in bfloat16 or wider, within the bound.
A program may use at most 256 MiB of HBM per device.

```python
import math
import jax
import jax.numpy as jnp
import numpy as np
from jax import lax

D = 768
HEADS = 12
HEAD_DIM = 64
FF = 3072
STEPS = 1000
MICRO = 4
ITEM_MAX = 256
SEQ_LEN = 512
TOKENS = 4096
ROWS = 32
ITEMS_ROW = 3
ITEMS = 96
N_DP = 8


def set_ends(values, key, low, top_value):
    shape = values.shape
    spot = [jax.random.randint(jax.random.fold_in(key, axis), (), 0, shape[axis]) for axis in range(len(shape))]
    values = values.at[tuple(spot)].set(low)
    longest = shape.index(max(shape))
    spot[longest] = (spot[longest] + 1) % shape[longest]
    return values.at[tuple(spot)].set(top_value)


def strengthened(values, rng, source, target, parts, factor):
    def block_of(dim):
        return (jnp.arange(values.shape[dim]) // (values.shape[dim] // parts)).reshape((-1,) + (1,) * (values.ndim - 1 - dim))

    first = jax.random.permutation(rng, parts)[block_of(target)]
    far = (block_of(target) + parts // 2) % parts
    return jnp.where((block_of(source) == first) | (block_of(source) == far), factor * values, values)


def block_scale(key, extent, cuts, least, top_value):
    def one(position, parts):
        steps = jax.random.uniform(jax.random.fold_in(jax.random.fold_in(key, 6), position), (parts,), jnp.float32, least / len(cuts), top_value / len(cuts))
        return jnp.repeat(jnp.exp(steps), extent[position] // parts).reshape((-1,) + (1,) * (len(extent) - position - 1))

    level = one(*cuts[0])
    for cut in cuts[1:]:
        level = level * one(*cut)
    return level


def profile(number_of, total, limit, skew):
    weights = [(1 << 20) // math.isqrt(rank ** skew) + 1 for rank in range(2, number_of + 1)]
    spare, counts = total - limit - (number_of - 1), [1] * (number_of - 1)
    while spare > 0:
        candidates = [i for i in range(number_of - 1) if counts[i] < limit]
        mass, remaining = sum([weights[i] for i in candidates]), spare
        for i in candidates:
            extra = min(limit - counts[i], max(1, remaining * weights[i] // mass), spare)
            counts[i] = counts[i] + extra
            spare = spare - extra
    return np.array([limit] + counts)


def ragged(rng, amount, total, reach, lean):
    if amount == 2:
        one = jax.random.randint(rng, (), max(1, total - reach), min(reach, total - 1) + 1)
        return jnp.stack([one, total - one])
    sizes = jnp.asarray(profile(amount, total, reach, lean), jnp.int32)
    twos = (amount - 1) // 2
    giver, receiver = sizes[1:1 + 2 * twos:2], sizes[2:2 + 2 * twos:2]
    room = jnp.minimum(giver - 1, reach - receiver)
    moved = jax.random.randint(jax.random.fold_in(rng, 1), (twos,), 0, 1 << 20) % (room + 1)
    sizes = sizes.at[1:1 + 2 * twos:2].set(giver - moved).at[2:2 + 2 * twos:2].set(receiver + moved)
    return sizes[jax.random.permutation(jax.random.fold_in(rng, 2), amount)]


def scatter_about(rng, extent, width, most, cuts=(), kind=jnp.bfloat16):
    level = block_scale(rng, extent, cuts, -0.22, 0.18) if cuts else 1.0
    drawn = jax.random.normal(rng, extent, jnp.float32) * width * level
    return jnp.minimum(jnp.maximum(drawn, -most), most).astype(kind)


def bell_draw_with(own_key, dims, width, bound, shards, heavy, held_as=jnp.bfloat16):
    array = width * jax.random.normal(own_key, dims, jnp.float32)
    if shards:
        array = array * block_scale(own_key, dims, shards, -0.22, 0.18)
    return jnp.clip(strengthened(array, jax.random.fold_in(own_key, 3), *heavy), -bound, bound).astype(held_as)


def setup_inputs(seed: int = 0) -> dict:
    seeds = jax.random.split(jax.random.key(seed), 15)
    inputs = scatter_about(seeds[0], (MICRO, TOKENS, D), 1.0, 6.0, ((1, 32),))
    time_table = scatter_about(seeds[1], (STEPS, D), 0.5, 3.0, ((1, 32),))
    w_qkv = scatter_about(seeds[2], (D, 3 * D), D ** -0.5, 0.21875, ((1, 32),))
    w_out = scatter_about(seeds[3], (D, D), (D // 32) ** -0.5, 1.25, ((1, 32),))
    w_up = scatter_about(seeds[4], (D, FF), D ** -0.5, 0.21875, ((1, 32),))
    w_down = scatter_about(seeds[5], (FF, D), FF ** -0.5, 0.109375, ((1, 32),))
    norm_gains = jnp.clip(1.0 + 0.1 * jax.random.normal(seeds[6], (2, D), jnp.float32), 0.5, 1.5).astype(jnp.bfloat16)
    norm_shifts = scatter_about(seeds[7], (2, D), 0.3, 4.0, ((1, 32),))
    biases = scatter_about(seeds[8], (4, D), 0.3, 4.0, ((1, 32),))
    up_bias = scatter_about(seeds[9], (1, FF), 0.3, 4.0, ((1, 32),))
    timesteps = set_ends(jax.random.randint(seeds[10], (ITEMS,), 0, STEPS), jax.random.fold_in(seeds[10], 1), 0, STEPS - 1).astype(jnp.int32)
    item_map = jax.random.permutation(seeds[11], ITEMS).astype(jnp.int32)
    lengths = jax.vmap(lambda own: ragged(own, ITEMS_ROW, SEQ_LEN, ITEM_MAX, 1))(jax.random.split(seeds[12], ROWS)).reshape((ROWS, ITEMS_ROW)).astype(jnp.int32)
    cotangent = bell_draw_with(seeds[13], (MICRO, TOKENS, D), 1.0, 6.0, ((1, 32),), (1, 2, 32, 2.75))
    return dict(inputs=inputs, time_table=time_table, w_qkv=w_qkv, w_out=w_out, w_up=w_up, w_down=w_down, norm_gains=norm_gains, norm_shifts=norm_shifts, biases=biases, up_bias=up_bias, timesteps=timesteps, item_map=item_map, lengths=lengths, cotangent=cotangent)


@jax.custom_vjp
def low(v):
    return lax.optimization_barrier(v.astype(jnp.bfloat16)).astype(jnp.float32)

@jax.custom_vjp
def low_back(v):
    return v

def low_keep(v):
    return (low(v), None)

def low_pass(kept, grad):
    return (grad,)

def back_keep(v):
    return (v, None)

def back_low(kept, grad):
    return (low(grad),)
low.defvjp(low_keep, low_pass)
low_back.defvjp(back_keep, back_low)
HIGHEST = lax.Precision.HIGHEST
EPS = 1e-05

def rounded_both(field):
    return low_back(low(field))

def norm_rows(field, gain, offset):
    mean = lax.optimization_barrier(jnp.mean(field, axis=-1, keepdims=True))
    centred = field - mean
    spread = lax.optimization_barrier(jnp.mean(centred * centred, axis=-1, keepdims=True))
    return centred * lax.rsqrt(spread + EPS) * gain + offset

def attend(queries, keys, values, segment):
    length = queries.shape[0]
    block = min(512, length)
    count = length // block
    scale = HEAD_DIM ** (-0.5)
    query_blocks = queries.reshape(count, block, HEADS, HEAD_DIM)
    segment_blocks = segment.reshape(count, block)

    def one_block(pair):
        query_part, segment_part = pair
        raw = low_back(scale * jnp.einsum('qhd,khd->hqk', query_part, keys, precision=HIGHEST))
        keep = segment_part[None, :, None] == segment[None, None, :]
        probs = jax.nn.softmax(jnp.where(keep, raw, -1e+30), axis=-1)
        return jnp.einsum('hqk,khd->qhd', low(probs), values, precision=HIGHEST)
    result = lax.map(jax.checkpoint(one_block), (query_blocks, segment_blocks))
    return result.reshape(length, HEADS * HEAD_DIM)

def layer(table, w_qkv, w_out, w_up, w_down, gains, offsets, biases, up_bias, row_in, row_steps, row_segment):
    length = row_in.shape[0]
    embedded = row_in + table[row_steps]
    first_normed = low(norm_rows(embedded, gains[0], offsets[0]))
    projected = jnp.dot(first_normed, w_qkv, precision=HIGHEST)
    queries = rounded_both(projected[:, 0:D] + biases[0])
    keys = rounded_both(projected[:, D:2 * D])
    values = rounded_both(projected[:, 2 * D:3 * D] + biases[1])
    attended = rounded_both(attend(queries.reshape(length, HEADS, HEAD_DIM), keys.reshape(length, HEADS, HEAD_DIM), values.reshape(length, HEADS, HEAD_DIM), row_segment))
    mid = embedded + low_back(jnp.dot(attended, w_out, precision=HIGHEST) + biases[2])
    second_normed = low(norm_rows(mid, gains[1], offsets[1]))
    inner = low_back(jnp.dot(second_normed, w_up, precision=HIGHEST) + up_bias[0])
    activated = low(jax.nn.gelu(inner, approximate=False))
    return mid + low_back(jnp.dot(activated, w_down, precision=HIGHEST) + biases[3])

def reference(inputs, time_table, w_qkv, w_out, w_up, w_down, norm_gains, norm_shifts, biases, up_bias, timesteps, item_map, lengths, cotangent):
    params = tuple((a.astype(jnp.float32) for a in (time_table, w_qkv, w_out, w_up, w_down, norm_gains, norm_shifts, biases, up_bias)))
    row_count = N_DP * MICRO

    def to_rows(field):
        shaped = field.astype(jnp.float32).reshape(MICRO, N_DP, SEQ_LEN, D)
        return jnp.transpose(shaped, (1, 0, 2, 3)).reshape(row_count, SEQ_LEN, D)

    def from_rows(field):
        shaped = field.reshape(N_DP, MICRO, SEQ_LEN, D)
        return jnp.transpose(shaped, (1, 0, 2, 3)).reshape(MICRO, N_DP * SEQ_LEN, D)
    slot_steps = jnp.take(timesteps, item_map).reshape(row_count, ITEMS_ROW).astype(jnp.int32)
    ends = jnp.cumsum(lengths, axis=1).astype(jnp.int32)
    places = jnp.arange(SEQ_LEN, dtype=jnp.int32)
    segment = lax.optimization_barrier(jnp.sum((ends[:, None, :] <= places[None, :, None]).astype(jnp.int32), axis=2)).astype(jnp.int32)
    token_steps = jnp.take_along_axis(slot_steps, segment, axis=1).astype(jnp.int32)

    def one_row(carry, row):
        row_in, row_steps, row_segment, row_grad = row

        def apply(*pieces):
            return layer(*pieces, row_steps, row_segment)
        result, pull = jax.vjp(apply, *params, row_in)
        grads = pull(row_grad)
        totals = tuple((c + g for c, g in zip(carry, grads[:-1])))
        return (totals, (result.astype(jnp.bfloat16), grads[-1].astype(jnp.bfloat16)))
    begin = tuple((jnp.zeros_like(p) for p in params))
    totals, (results, grads_in) = lax.scan(one_row, begin, (to_rows(inputs), token_steps, segment, to_rows(cotangent)))
    return (from_rows(results), from_rows(grads_in), totals[0], totals[1], totals[2], totals[3], totals[4], totals[5], totals[6], totals[7], totals[8])
```

```python
import functools

import jax
import jax.numpy as jnp
from jax import lax
from jax.experimental import pallas as pl
from jax.experimental.pallas import tpu as pltpu
from jax.sharding import PartitionSpec as P

HEADS = 12
HEAD_DIM = 64


EPS = 1e-05


def norm_rows(field, gain, offset):
    mean = jnp.mean(field, axis=-1, keepdims=True)
    centred = field - mean
    spread = jnp.mean(centred * centred, axis=-1, keepdims=True)
    return centred * lax.rsqrt(spread + EPS) * gain + offset


def gelu_exact(field):
    return jax.nn.gelu(field, approximate=False)


def scores_block(query_part, keys, query_segment, key_segment, scale):
    raw = scale * jnp.einsum("qhd,khd->hqk", query_part, keys, preferred_element_type=jnp.float32)
    keep = query_segment[None, :, None] == key_segment[None, None, :]
    return jnp.where(keep, raw, -1e30)


def attend_forward(queries, keys, values, segment, scale):
    score = scores_block(queries, keys, segment, segment, scale)
    top = jnp.max(score, axis=-1, keepdims=True)
    expo = jnp.exp(score - top)
    denom = jnp.sum(expo, axis=-1, keepdims=True)
    probs = (expo / denom).astype(jnp.bfloat16)
    results = jnp.einsum("hqk,khd->qhd", probs, values, preferred_element_type=jnp.float32).astype(
        jnp.bfloat16
    )
    log_totals = [top + jnp.log(denom)]
    return (results, log_totals)


def attend_backward(queries, keys, values, segment, log_totals, grad_out, scale):
    length = queries.shape[0]
    block = min(512, length)
    grad_keys = jnp.zeros(keys.shape, jnp.float32)
    grad_values = jnp.zeros(values.shape, jnp.float32)
    grad_queries = []
    for index, begin in enumerate(range(0, length, block)):
        score = scores_block(queries, keys, segment, segment, scale)
        probs = jnp.exp(score - log_totals[index])
        grad_values = jnp.einsum(
            "hqk,qhd->khd", probs.astype(jnp.bfloat16), grad_out, preferred_element_type=jnp.float32
        )
        grad_probs = jnp.einsum(
            "qhd,khd->hqk", grad_out, values, preferred_element_type=jnp.float32
        )
        centre = jnp.sum(probs * grad_probs, axis=-1, keepdims=True)
        grad_score = (probs * (grad_probs - centre)).astype(jnp.bfloat16)
        grad_queries.append(
            (
                scale
                * jnp.einsum("hqk,khd->qhd", grad_score, keys, preferred_element_type=jnp.float32)
            ).astype(jnp.bfloat16)
        )
        grad_keys = scale * jnp.einsum(
            "hqk,qhd->khd", grad_score, queries, preferred_element_type=jnp.float32
        )
    return (grad_queries[0], grad_keys.astype(jnp.bfloat16), grad_values.astype(jnp.bfloat16))


def spread_out(
    inputs,
    time_table,
    w_qkv,
    w_out,
    w_up,
    w_down,
    norm_gains,
    norm_shifts,
    biases,
    up_bias,
    timesteps,
    item_map,
    lengths,
    cotangent,
):
    micro = inputs.shape[0]
    local = inputs.shape[1]
    width = inputs.shape[2]
    groups = lax.axis_size("seq")
    data_count = lax.axis_size("dp")
    seq_len = local * groups
    items_row = lengths.shape[1]
    heads_dev = HEADS // groups
    group_width = width // groups
    scale = HEAD_DIM ** (-0.5)
    my_start = lax.axis_index("seq") * local
    places = jnp.arange(seq_len, dtype=jnp.int32)
    slot_index = jnp.arange(items_row, dtype=jnp.int32)
    step_index = jnp.arange(time_table.shape[0], dtype=jnp.int32)
    totals = None
    results = []
    input_grads = []
    for index in range(micro):
        gathered = (
            lax.all_gather(time_table, ("dp", "seq"), axis=1, tiled=True),
            lax.all_gather(w_qkv, ("dp", "seq"), axis=1, tiled=True),
            lax.all_gather(w_out, ("dp", "seq"), axis=1, tiled=True),
            lax.all_gather(w_up, ("dp", "seq"), axis=1, tiled=True),
            lax.all_gather(w_down, ("dp", "seq"), axis=1, tiled=True),
            lax.all_gather(norm_gains, ("dp", "seq"), axis=1, tiled=True),
            lax.all_gather(norm_shifts, ("dp", "seq"), axis=1, tiled=True),
            lax.all_gather(biases, ("dp", "seq"), axis=1, tiled=True),
            lax.all_gather(up_bias, ("dp", "seq"), axis=1, tiled=True),
        )
        (
            full_table,
            full_qkv,
            full_out,
            full_up,
            full_down,
            full_gains,
            full_shifts,
            full_biases,
            full_up_bias,
        ) = gathered
        gains = full_gains.astype(jnp.float32)
        offsets = full_shifts.astype(jnp.float32)
        bias_rows = full_biases.astype(jnp.float32)
        up_row = full_up_bias.astype(jnp.float32)[0]
        if totals is None:
            totals = [jnp.zeros(a.shape, jnp.float32) for a in gathered]
        ends = jnp.cumsum(lengths[index])
        segment = jnp.sum((ends[None, :] <= places[:, None]).astype(jnp.int32), axis=1)
        my_segment = lax.dynamic_slice_in_dim(segment, my_start, local)
        slot_steps = jnp.take(timesteps, item_map[index * items_row : (index + 1) * items_row])
        token_slot = (my_segment[:, None] == slot_index[None, :]).astype(jnp.bfloat16)
        step_hot = (slot_steps[:, None] == step_index[None, :]).astype(jnp.bfloat16)
        slot_rows = jnp.dot(step_hot, full_table, preferred_element_type=jnp.float32).astype(
            jnp.bfloat16
        )
        embedded = inputs[index].astype(jnp.float32) + jnp.dot(
            token_slot, slot_rows, preferred_element_type=jnp.float32
        )
        first_normed = norm_rows(embedded, gains[0], offsets[0]).astype(jnp.bfloat16)
        projected = jnp.dot(first_normed, full_qkv, preferred_element_type=jnp.float32)
        queries = (projected[:, 0:width] + bias_rows[0]).astype(jnp.bfloat16)
        keys = projected[:, width : 2 * width].astype(jnp.bfloat16)
        values = (projected[:, 2 * width : 3 * width] + bias_rows[1]).astype(jnp.bfloat16)
        head_queries, head_keys, head_values = (
            lax.all_to_all(
                queries.reshape(local, groups, group_width),
                "seq",
                split_axis=1,
                concat_axis=0,
                tiled=True,
            ),
            lax.all_to_all(
                keys.reshape(local, groups, group_width),
                "seq",
                split_axis=1,
                concat_axis=0,
                tiled=True,
            ),
            lax.all_to_all(
                values.reshape(local, groups, group_width),
                "seq",
                split_axis=1,
                concat_axis=0,
                tiled=True,
            ),
        )
        head_queries = head_queries.reshape(seq_len, heads_dev, HEAD_DIM)
        head_keys = head_keys.reshape(seq_len, heads_dev, HEAD_DIM)
        head_values = head_values.reshape(seq_len, heads_dev, HEAD_DIM)
        head_out, log_totals = attend_forward(head_queries, head_keys, head_values, segment, scale)
        attended = lax.all_to_all(
            head_out.reshape(seq_len, 1, group_width),
            "seq",
            split_axis=0,
            concat_axis=1,
            tiled=True,
        ).reshape(local, width)
        mid = (
            embedded
            + jnp.dot(attended, full_out, preferred_element_type=jnp.float32)
            + bias_rows[2]
        )
        second_normed = norm_rows(mid, gains[1], offsets[1]).astype(jnp.bfloat16)
        inner = jnp.dot(second_normed, full_up, preferred_element_type=jnp.float32) + up_row
        activated = gelu_exact(inner).astype(jnp.bfloat16)
        results.append(
            (
                mid
                + jnp.dot(activated, full_down, preferred_element_type=jnp.float32)
                + bias_rows[3]
            ).astype(jnp.bfloat16)
        )
        grad_output = cotangent[index]
        grad_down = jnp.einsum(
            "tf,td->fd", activated, grad_output, preferred_element_type=jnp.float32
        )
        bias_down = jnp.sum(grad_output.astype(jnp.float32), axis=0)
        grad_act = jnp.einsum(
            "td,fd->tf", grad_output, full_down, preferred_element_type=jnp.float32
        )
        unused, gelu_pull = jax.vjp(gelu_exact, inner)
        grad_inner = gelu_pull(grad_act)[0].astype(jnp.bfloat16)
        grad_up = jnp.einsum(
            "td,tf->df", second_normed, grad_inner, preferred_element_type=jnp.float32
        )
        grad_up_bias = jnp.sum(grad_inner.astype(jnp.float32), axis=0)
        upstream = jnp.einsum("tf,df->td", grad_inner, full_up, preferred_element_type=jnp.float32)
        unused, norm_pull = jax.vjp(norm_rows, mid, gains[1], offsets[1])
        back_mid, gain_second, shift_second = norm_pull(upstream)
        grad_mid = grad_output.astype(jnp.float32) + back_mid
        grad_branch = grad_mid.astype(jnp.bfloat16)
        grad_out_weight = jnp.einsum(
            "te,td->ed", attended, grad_branch, preferred_element_type=jnp.float32
        )
        bias_attend = jnp.sum(grad_branch.astype(jnp.float32), axis=0)
        grad_attended = jnp.einsum(
            "td,ed->te", grad_branch, full_out, preferred_element_type=jnp.float32
        ).astype(jnp.bfloat16)
        head_grad = lax.all_to_all(
            grad_attended.reshape(local, groups, group_width),
            "seq",
            split_axis=1,
            concat_axis=0,
            tiled=True,
        ).reshape(seq_len, heads_dev, HEAD_DIM)
        grad_q_heads, grad_k_heads, grad_v_heads = attend_backward(
            head_queries, head_keys, head_values, segment, log_totals, head_grad, scale
        )
        grad_queries, grad_keys, grad_values = (
            lax.all_to_all(
                grad_q_heads.reshape(seq_len, 1, group_width),
                "seq",
                split_axis=0,
                concat_axis=1,
                tiled=True,
            ),
            lax.all_to_all(
                grad_k_heads.reshape(seq_len, 1, group_width),
                "seq",
                split_axis=0,
                concat_axis=1,
                tiled=True,
            ),
            lax.all_to_all(
                grad_v_heads.reshape(seq_len, 1, group_width),
                "seq",
                split_axis=0,
                concat_axis=1,
                tiled=True,
            ),
        )
        grad_projected = jnp.concatenate(
            (
                grad_queries.reshape(local, width),
                grad_keys.reshape(local, width),
                grad_values.reshape(local, width),
            ),
            axis=1,
        )
        grad_qkv = jnp.einsum(
            "td,tc->dc", first_normed, grad_projected, preferred_element_type=jnp.float32
        )
        bias_query = jnp.sum(grad_queries.reshape(local, width).astype(jnp.float32), axis=0)
        bias_value = jnp.sum(grad_values.reshape(local, width).astype(jnp.float32), axis=0)
        upstream_first = jnp.einsum(
            "tc,dc->td", grad_projected, full_qkv, preferred_element_type=jnp.float32
        )
        unused, first_pull = jax.vjp(norm_rows, embedded, gains[0], offsets[0])
        back_first, gain_first, shift_first = first_pull(upstream_first)
        grad_embedded = grad_mid + back_first
        input_grads.append(grad_embedded.astype(jnp.bfloat16))
        slot_sums = jnp.einsum(
            "ts,td->sd",
            token_slot.astype(jnp.float32),
            grad_embedded,
            precision=lax.Precision.HIGHEST,
        )
        grad_table = jnp.einsum(
            "si,sd->id", step_hot.astype(jnp.float32), slot_sums, precision=lax.Precision.HIGHEST
        )
        grad_gains = jnp.stack((gain_first, gain_second), axis=0)
        grad_shifts = jnp.stack((shift_first, shift_second), axis=0)
        grad_biases = jnp.stack((bias_query, bias_value, bias_attend, bias_down), axis=0)
        grad_up_row = grad_up_bias[None, :]
        fresh = (
            grad_table,
            grad_qkv,
            grad_out_weight,
            grad_up,
            grad_down,
            grad_gains,
            grad_shifts,
            grad_biases,
            grad_up_row,
        )
        totals = [a + b for a, b in zip(totals, fresh)]

    def spread(grad):
        return grad.reshape(
            grad.shape[0], data_count, groups, grad.shape[1] // (data_count * groups)
        )

    parts = [spread(a) for a in totals]
    folded = (
        lax.all_to_all(
            parts[0].astype(jnp.bfloat16), "seq", split_axis=2, concat_axis=2, tiled=True
        ).astype(jnp.float32),
        lax.all_to_all(
            parts[1].astype(jnp.bfloat16), "seq", split_axis=2, concat_axis=2, tiled=True
        ).astype(jnp.float32),
        lax.all_to_all(
            parts[2].astype(jnp.bfloat16), "seq", split_axis=2, concat_axis=2, tiled=True
        ).astype(jnp.float32),
        lax.all_to_all(
            parts[3].astype(jnp.bfloat16), "seq", split_axis=2, concat_axis=2, tiled=True
        ).astype(jnp.float32),
        lax.all_to_all(
            parts[4].astype(jnp.bfloat16), "seq", split_axis=2, concat_axis=2, tiled=True
        ).astype(jnp.float32),
        lax.all_to_all(
            parts[5].astype(jnp.bfloat16), "seq", split_axis=2, concat_axis=2, tiled=True
        ).astype(jnp.float32),
        lax.all_to_all(
            parts[6].astype(jnp.bfloat16), "seq", split_axis=2, concat_axis=2, tiled=True
        ).astype(jnp.float32),
        lax.all_to_all(
            parts[7].astype(jnp.bfloat16), "seq", split_axis=2, concat_axis=2, tiled=True
        ).astype(jnp.float32),
        lax.all_to_all(
            parts[8].astype(jnp.bfloat16), "seq", split_axis=2, concat_axis=2, tiled=True
        ).astype(jnp.float32),
    )
    merged = [jnp.sum(f, axis=2, keepdims=True) for f in folded]
    owners = (
        lax.psum_scatter(merged[0], "dp", scatter_dimension=1, tiled=True),
        lax.psum_scatter(merged[1], "dp", scatter_dimension=1, tiled=True),
        lax.psum_scatter(merged[2], "dp", scatter_dimension=1, tiled=True),
        lax.psum_scatter(merged[3], "dp", scatter_dimension=1, tiled=True),
        lax.psum_scatter(merged[4], "dp", scatter_dimension=1, tiled=True),
        lax.psum_scatter(merged[5], "dp", scatter_dimension=1, tiled=True),
        lax.psum_scatter(merged[6], "dp", scatter_dimension=1, tiled=True),
        lax.psum_scatter(merged[7], "dp", scatter_dimension=1, tiled=True),
        lax.psum_scatter(merged[8], "dp", scatter_dimension=1, tiled=True),
    )
    owned = [o.reshape(o.shape[0], o.shape[3]) for o in owners]
    return (
        jnp.stack(results, axis=0),
        jnp.stack(input_grads, axis=0),
        owned[0],
        owned[1],
        owned[2],
        owned[3],
        owned[4],
        owned[5],
        owned[6],
        owned[7],
        owned[8],
    )


F32 = jnp.float32
BF16 = jnp.bfloat16
MESH = pl.DeviceIdType.MESH
VMEM = pl.BlockSpec(memory_space=pltpu.VMEM)
ANY = pl.BlockSpec(memory_space=pl.ANY)
ALL = slice(None)
ORDER_FIRST = "zxy"
ORDERS_SECOND = ("zxy", "zyx", "yxz")


class Place:
    def __init__(self):
        row, column = lax.axis_index("dp"), lax.axis_index("seq")
        self.at = {"z": row // 2, "y": row % 2, "x": column // 2}
        self.core = column % 2
        self.column = column
        self.depth = lax.axis_size("dp") // 2

    def device(self, core=None, **moved):
        at = {**self.at, **moved}
        core = self.core if core is None else core
        return (at["z"] * 2 + at["y"], at["x"] * 2 + core)

    def other(self, axis):
        return 1 - self.at[axis]

    def around(self, step):
        return (self.at["z"] + step) % self.depth

    def sibling(self):
        return self.device(core=1 - self.core)

    def partners(self):
        found = [self.sibling(), self.device(x=self.other("x")), self.device(y=self.other("y"))]
        found.append(self.device(core=1 - self.core, x=self.other("x")))
        found += [self.device(z=self.around(step)) for step in range(1, self.depth)]
        return found


def meet(place):
    barrier = pltpu.get_barrier_semaphore()
    partners = place.partners()
    for partner in partners:
        pl.semaphore_signal(barrier, inc=1, device_id=partner, device_id_type=MESH)
    pl.semaphore_wait(barrier, len(partners))


def remote(source, target, send, receive, device):
    return pltpu.make_async_remote_copy(
        src_ref=source,
        dst_ref=target,
        send_sem=send,
        recv_sem=receive,
        device_id=device,
        device_id_type=MESH,
    )


def order_of(core, unit):
    return ORDER_FIRST if core == 0 else ORDERS_SECOND[unit % len(ORDERS_SECOND)]


def on_core(place, core):
    return pl.when(place.core == core)


class Gather:
    def __init__(self, place, unit, view, send, receive):
        self.place, self.unit, self.view = place, unit, view
        self.send, self.receive = send, receive

    def index(self, order, stage):
        return {a: (ALL if a in order[:stage] else self.place.at[a]) for a in "zyx"}

    def part(self, core, index):
        return self.view(index["z"], index["y"], index["x"], core)

    def copies(self, core, stage):
        order = order_of(core, self.unit)
        if stage == 3:
            whole = self.view(ALL, ALL, ALL, core)
            slot = self.place.depth + 1
            return [remote(whole, whole, self.send.at[self.unit, slot], self.receive.at[self.unit, slot], self.place.sibling())]
        axis, index = order[stage], self.index(order, stage)
        mine = self.part(core, index)
        if axis != "z":
            slot = self.place.depth - 1 + sum(a != "z" for a in order[:stage])
            device = self.place.device(**{axis: self.place.other(axis)})
            return [remote(mine, mine, self.send.at[self.unit, slot], self.receive.at[self.unit, slot], device)]
        return [
            remote(
                mine,
                mine,
                self.send.at[self.unit, step - 1],
                self.receive.at[self.unit, step - 1],
                self.place.device(z=self.place.around(step)),
            )
            for step in range(1, self.place.depth)
        ]

    def start(self, stage):
        for core in range(2):

            @on_core(self.place, core)
            def _():
                for copy in self.copies(core, stage):
                    copy.start()

    def arrived(self, stage):
        for core in range(2):

            @on_core(self.place, core)
            def _():
                for copy in self.copies(core, stage):
                    copy.wait_recv()

    def sibling_arrived(self):
        for core in range(2):

            @on_core(self.place, core)
            def _():
                for copy in self.copies(1 - core, 3):
                    copy.wait_recv()

    def sent(self):
        for core in range(2):

            @on_core(self.place, core)
            def _():
                for stage in range(4):
                    for copy in self.copies(core, stage):
                        copy.wait_send()


class Scatter:
    def __init__(self, place, unit, view, first, landings, send, receive):
        self.place, self.unit, self.view = place, unit, view
        self.first, self.landings = first, landings
        self.send, self.receive = send, receive

    def own(self, core, index):
        return self.view(index["z"], index["y"], index["x"], core)

    def sibling_copy(self, core):
        theirs = self.view(ALL, ALL, ALL, 1 - core)
        slot = self.place.depth + 1
        return remote(theirs, self.first, self.send.at[self.unit, slot], self.receive.at[self.unit, slot], self.place.sibling())

    def stage_copies(self, core, stage):
        order = order_of(core, self.unit)[::-1]
        axis = order[stage]
        index = {a: (self.place.at[a] if a in order[:stage] else ALL) for a in "zyx"}
        mine = self.own(core, {**index, axis: self.place.at[axis]})
        landing = self.landings(order)[stage]
        if axis != "z":
            slot = self.place.depth - 1 + sum(a != "z" for a in order[:stage])
            gone = self.own(core, {**index, axis: self.place.other(axis)})
            device = self.place.device(**{axis: self.place.other(axis)})
            copy = remote(gone, landing, self.send.at[self.unit, slot], self.receive.at[self.unit, slot], device)
            return [(copy, mine, landing)]
        found = []
        for step in range(1, self.place.depth):
            gone = self.own(core, {**index, "z": self.place.around(step)})
            copy = remote(
                gone,
                landing.at[step - 1],
                self.send.at[self.unit, step - 1],
                self.receive.at[self.unit, step - 1],
                self.place.device(z=self.place.around(step)),
            )
            found.append((copy, mine, landing.at[step - 1]))
        return found

    def start_sibling(self):
        for core in range(2):

            @on_core(self.place, core)
            def _():
                self.sibling_copy(core).start()

    def add_sibling(self):
        for core in range(2):

            @on_core(self.place, core)
            def _():
                self.sibling_copy(core).wait_recv()
                mine = self.view(ALL, ALL, ALL, core)
                mine[...] = (mine[...].astype(F32) + self.first[...].astype(F32)).astype(BF16)

    def start(self, stage):
        for core in range(2):

            @on_core(self.place, core)
            def _():
                for copy, _, _ in self.stage_copies(core, stage):
                    copy.start()

    def add(self, stage, result=None):
        for core in range(2):

            @on_core(self.place, core)
            def _():
                found = self.stage_copies(core, stage)
                for copy, _, _ in found:
                    copy.wait_recv()
                mine = found[0][1]
                total = mine[...].astype(F32)
                for _, _, landing in found:
                    total = total + landing[...].astype(F32)
                if stage == 2:
                    result(core)[...] = total
                else:
                    mine[...] = total.astype(BF16)

    def sent(self):
        for core in range(2):

            @on_core(self.place, core)
            def _():
                self.sibling_copy(core).wait_send()
                for stage in range(3):
                    for copy, _, _ in self.stage_copies(core, stage):
                        copy.wait_send()


class Sizes:
    def __init__(self, width, ff, devices, depth):
        self.width, self.ff, self.devices, self.depth = width, ff, devices, depth
        self.half = width // 2
        self.rows = 2 * width // devices
        self.n_qkv, self.n_ff = 3, ff // width
        self.small = 128
        self.units = 1 + self.n_qkv + 1 + 2 * self.n_ff
        self.chips = (depth, 2, 2)

    def weights(self):
        return [
            (*self.chips, self.rows, 2 * self.small),
            (*self.chips, self.n_qkv, self.rows, self.width),
            (*self.chips, self.rows, self.width),
            (*self.chips, self.n_ff, self.rows, self.width),
            (*self.chips, self.rows, self.ff),
        ]

    def views(self, refs):
        small, qkv, out, up, down = refs
        half = self.half

        def columns(core, base=0, width=half):
            return pl.ds(base + core * width, width)

        found = [lambda z, y, x, core: small.at[z, y, x, :, columns(core, 0, self.small)]]
        for unit in range(self.n_qkv):
            found.append(lambda z, y, x, core, unit=unit: qkv.at[z, y, x, unit, :, columns(core)])
        found.append(lambda z, y, x, core: out.at[z, y, x, :, columns(core)])
        for unit in range(self.n_ff):
            found.append(lambda z, y, x, core, unit=unit: up.at[z, y, x, unit, :, columns(core)])
        for unit in range(self.n_ff):
            found.append(lambda z, y, x, core, unit=unit: down.at[z, y, x, :, columns(core, unit * self.width)])
        return found


def transposed(block):
    size = block.shape[0]
    eye = (
        lax.broadcasted_iota(jnp.int32, (size, size), 0) == lax.broadcasted_iota(jnp.int32, (size, size), 1)
    ).astype(BF16)
    return lax.dot_general(block, eye, (((0,), (0,)), ((), ())), preferred_element_type=F32)


def gather_kernel(
    sizes, inputs, cotangent, table, qkv, out, up, down, vectors, steps,
    full_small, full_qkv, full_out, full_up, full_down, rows_in, rows_cot,
    own_small, own_qkv, own_out, own_up, own_down,
    sib_small, sib_qkv, sib_out, sib_up, sib_down,
    send, receive, raw_send, raw_receive, row_send, row_receive, row_local,
):
    place = Place()
    half = sizes.half
    own = [own_small, own_qkv, own_out, own_up, own_down]
    sib = [sib_small, sib_qkv, sib_out, sib_up, sib_down]
    count = table.shape[0]
    hot = (lax.broadcasted_iota(jnp.int32, (count, sizes.small), 0) == steps[...]).astype(BF16)
    own_small[:, 0 : sizes.small] = lax.dot_general(
        table[...], hot, (((0,), (0,)), ((), ())), preferred_element_type=F32
    )
    own_small[:, sizes.small :] = transposed(vectors[...])
    for ref, target in ((qkv, own_qkv), (out, own_out), (up, own_up), (down, own_down)):
        for begin in range(0, ref.shape[0], half):
            target[:, begin : begin + half] = transposed(ref[begin : begin + half, :])
    meet(place)
    local = inputs.shape[1]
    groups = inputs.shape[0]
    me = place.column

    def row_copies():
        found = []
        for which, (source, target) in enumerate(((inputs, rows_in), (cotangent, rows_cot))):
            for step in range(1, groups):
                peer = (me + step) % groups
                found.append(
                    remote(
                        source.at[peer],
                        target.at[me],
                        row_send.at[which, step - 1],
                        row_receive.at[which, step - 1],
                        (lax.axis_index("dp"), peer),
                    )
                )
        return found

    def local_copies():
        return [
            pltpu.make_async_copy(source.at[me], target.at[me], row_local.at[which])
            for which, (source, target) in enumerate(((inputs, rows_in), (cotangent, rows_cot)))
        ]

    def raw_copies(core):
        found = []
        for slot, (mine, theirs) in enumerate(zip(own, sib)):
            width = sizes.small if slot == 0 else half
            for part in range(mine.shape[1] // (2 * width)):
                found.append(
                    remote(
                        mine.at[:, pl.ds((2 * part + 1 - core) * width, width)],
                        theirs.at[:, pl.ds(part * width, width)],
                        raw_send.at[slot, part],
                        raw_receive.at[slot, part],
                        place.sibling(),
                    )
                )
        return found

    refs = [full_small, full_qkv, full_out, full_up, full_down]
    for core in range(2):

        @on_core(place, core)
        def _():
            for copy in raw_copies(core):
                copy.start()

    for copy in row_copies() + local_copies():
        copy.start()

    for core in range(2):

        @on_core(place, core)
        def _():
            copies = raw_copies(core)
            index = 0
            for slot, (mine, theirs) in enumerate(zip(own, sib)):
                width = sizes.small if slot == 0 else half
                for part in range(mine.shape[1] // (2 * width)):
                    copies[index].wait_recv()
                    index += 1
                    here = mine[:, (2 * part + core) * width : (2 * part + core + 1) * width]
                    there = theirs[:, part * width : (part + 1) * width]
                    block = jnp.concatenate([here, there] if core == 0 else [there, here], axis=0).astype(BF16)
                    lanes = pl.ds((2 * part + core) * width, width)
                    z, y, x = (place.at[a] for a in "zyx")
                    if refs[slot].ndim == 6:
                        for unit in range(refs[slot].shape[3]):
                            refs[slot][z, y, x, unit, :, lanes] = block[unit * sizes.rows : (unit + 1) * sizes.rows]
                    else:
                        refs[slot][z, y, x, :, lanes] = block

    units = [Gather(place, unit, view, send, receive) for unit, view in enumerate(sizes.views(refs))]
    count = len(units)
    for beat in range(count + 3):
        for stage in (3, 2, 1, 0):
            unit = beat - stage
            if 0 <= unit < count:
                if stage:
                    units[unit].arrived(stage - 1)
                units[unit].start(stage)
    for unit in units:
        unit.sibling_arrived()
    for unit in units:
        unit.sent()
    for core in range(2):

        @on_core(place, core)
        def _():
            for copy in raw_copies(core):
                copy.wait_send()

    for copy in row_copies():
        copy.wait()
    for copy in local_copies():
        copy.wait()


def scatter_kernel(
    sizes, grad_small, grad_qkv, grad_out, grad_up, grad_down, rows_out, rows_grad,
    end_small, end_qkv, end_out, end_up, end_down, result, input_grad,
    g_small, g_qkv, g_out, g_up, g_down,
    f_small, f_qkv, f_out, f_up, f_down,
    first_small, near_small, far_small, deep_small, first, near, far, deep, cross_far, cross_near, cross_last,
    send, receive, end_send, end_receive, row_send, row_receive, row_local, loads,
):
    place = Place()
    half = sizes.half
    grads = [g_small, g_qkv, g_out, g_up, g_down]
    finals = [f_small, f_qkv, f_out, f_up, f_down]
    ends = [end_small, end_qkv, end_out, end_up, end_down]
    copies = [
        pltpu.make_async_copy(source, target, loads.at[i])
        for i, (source, target) in enumerate(zip((grad_small, grad_qkv, grad_out, grad_up, grad_down), grads))
    ]
    for copy in copies:
        copy.start()
    for copy in copies:
        copy.wait()
    meet(place)
    me = place.column
    groups = result.shape[0]

    def row_copies():
        found = []
        for which, (source, target) in enumerate(((rows_out, result), (rows_grad, input_grad))):
            for step in range(1, groups):
                peer = (me + step) % groups
                found.append(
                    remote(
                        source.at[peer],
                        target.at[me],
                        row_send.at[which, step - 1],
                        row_receive.at[which, step - 1],
                        (lax.axis_index("dp"), peer),
                    )
                )
        return found

    def local_copies():
        return [
            pltpu.make_async_copy(source.at[me], target.at[me], row_local.at[which])
            for which, (source, target) in enumerate(((rows_out, result), (rows_grad, input_grad)))
        ]

    for copy in row_copies() + local_copies():
        copy.start()

    views = sizes.views(grads)
    spots = [(0, 0)] + [(1, u) for u in range(sizes.n_qkv)] + [(2, 0)]
    spots += [(3, u) for u in range(sizes.n_ff)] + [(4, u) for u in range(sizes.n_ff)]
    units = []
    for unit, view in enumerate(views):
        if unit == 0:
            places = (near_small.at[0], far_small.at[0], deep_small.at[0])
            units.append(Scatter(place, unit, view, first_small.at[0], lambda order, p=places: p, send, receive))
            continue
        slot = unit - 1
        plain = (near.at[slot], far.at[slot], deep.at[slot])
        cross = (cross_far.at[slot // 3], cross_near.at[slot // 3], cross_last.at[slot // 3])
        units.append(
            Scatter(
                place, unit, view, first.at[slot], lambda order, p=plain, c=cross: c if order[0] == "z" else p, send, receive
            )
        )

    def final(unit):
        slot, part = spots[unit]
        if slot == 4:
            return lambda core: finals[slot].at[:, pl.ds(part * half, half)]
        return lambda core: finals[slot].at[pl.ds(part * sizes.rows, sizes.rows), :]

    def end_copies(core, slot):
        width = sizes.small if slot == 0 else half
        rows = ends[slot].shape[0]
        found = []
        for part in range(finals[slot].shape[1] // width):
            source = finals[slot].at[pl.ds((1 - core) * rows, rows), pl.ds(part * width, width)]
            target = ends[slot].at[:, pl.ds((2 * part + core) * width, width)]
            found.append(remote(source, target, end_send.at[slot, part], end_receive.at[slot, part], place.sibling()))
        return found

    def close(slot):
        width = sizes.small if slot == 0 else half
        rows = ends[slot].shape[0]
        for core in range(2):

            @on_core(place, core)
            def _():
                for copy in end_copies(core, slot):
                    copy.start()
                for part in range(finals[slot].shape[1] // width):
                    ends[slot][:, (2 * part + core) * width : (2 * part + core + 1) * width] = finals[slot][
                        core * rows : (core + 1) * rows, part * width : (part + 1) * width
                    ]

    turn = list(range(len(units)))[::-1]
    last = {spots[unit][0]: unit for unit in turn}
    for unit in turn:
        units[unit].start_sibling()
    for beat in range(len(turn) + 3):
        for stage in (3, 2, 1, 0):
            at = beat - stage
            if 0 <= at < len(turn):
                unit = units[turn[at]]
                if stage == 0:
                    unit.add_sibling()
                else:
                    unit.add(stage - 1, final(turn[at]))
                if stage < 3:
                    unit.start(stage)
                else:
                    slot = spots[turn[at]][0]
                    if last[slot] == turn[at]:
                        close(slot)
    for unit in units:
        unit.sent()
    for slot in range(5):
        for core in range(2):

            @on_core(place, core)
            def _():
                for copy in end_copies(core, slot):
                    copy.wait_send()
                for copy in end_copies(1 - core, slot):
                    copy.wait_recv()

    for copy in row_copies():
        copy.wait()
    for copy in local_copies():
        copy.wait()


def row_by_row(
    inputs, time_table, w_qkv, w_out, w_up, w_down, norm_gains, norm_shifts, biases, up_bias,
    timesteps, item_map, lengths, cotangent,
):
    groups = lax.axis_size("seq")
    width = inputs.shape[2]
    local = inputs.shape[1]
    seq_len = local * groups
    devices = lax.axis_size("dp") * groups
    ff = w_down.shape[0]
    depth = lax.axis_size("dp") // 2
    sizes = Sizes(width, ff, devices, depth)
    items = timesteps.shape[0]
    per_up = ff // width
    me = lax.axis_index("seq")

    vectors = jnp.concatenate((norm_gains, norm_shifts, biases, up_bias.reshape(per_up, -1)), axis=0)
    vectors = jnp.pad(vectors, ((0, sizes.small - vectors.shape[0]), (0, 0)))
    steps = jnp.pad(timesteps, (0, sizes.small - items), constant_values=-1)[None, :]
    table = jnp.pad(time_table, ((0, -time_table.shape[0] % 128), (0, 0)))

    blocks = [jax.ShapeDtypeStruct(shape, BF16) for shape in sizes.weights()]
    rows_shape = jax.ShapeDtypeStruct((groups, local, width), BF16)
    owns = [2 * sizes.small, width, width, width, ff]
    own_rows = [sizes.rows // 2 * n for n in (1, sizes.n_qkv, 1, sizes.n_ff, 1)]
    unit_sems = pltpu.SemaphoreType.DMA((sizes.units, depth + 2))
    gathered = pl.pallas_call(
        functools.partial(gather_kernel, sizes),
        out_shape=(*blocks, rows_shape, rows_shape),
        in_specs=[ANY, ANY] + [VMEM] * 7,
        out_specs=(VMEM,) * 5 + (ANY, ANY),
        scratch_shapes=[pltpu.VMEM((r, c), F32) for r, c in zip(own_rows, owns)]
        + [pltpu.VMEM((r, c // 2), F32) for r, c in zip(own_rows, owns)]
        + [
            unit_sems,
            unit_sems,
            pltpu.SemaphoreType.DMA((5, per_up)),
            pltpu.SemaphoreType.DMA((5, per_up)),
            pltpu.SemaphoreType.DMA((2, groups - 1)),
            pltpu.SemaphoreType.DMA((2, groups - 1)),
            pltpu.SemaphoreType.DMA((2,)),
        ],
        compiler_params=pltpu.CompilerParams(collective_id=0, has_side_effects=True, vmem_limit_bytes=56 << 20),
    )(inputs, cotangent, table, w_qkv, w_out, w_up, w_down, vectors, steps)
    small, qkv_t, out_t, up_t, down_t, rows_in, rows_cot = gathered
    small = small.reshape(width, 2 * sizes.small)
    full_qkv, full_out, full_up, full_down = (
        qkv_t.reshape(3 * width, width),
        out_t.reshape(width, width),
        up_t.reshape(ff, width),
        down_t.reshape(width, ff),
    )
    row_in = rows_in.reshape(seq_len, width)
    row_cot = rows_cot.reshape(seq_len, width)
    lines = small[:, sizes.small :].T.astype(F32)
    gains, shifts, bias_rows = lines[0:2], lines[2:4], lines[4:8]
    up_row = (
        lines[8 : 8 + per_up].reshape(per_up, devices, width // devices).transpose(1, 0, 2).reshape(ff)
    )
    items_row = lengths.shape[1]
    my_lengths = lax.dynamic_index_in_dim(lengths, me, 0, keepdims=False)
    ends = jnp.cumsum(my_lengths)
    places = jnp.arange(seq_len, dtype=jnp.int32)
    segment = jnp.sum((ends[None, :] <= places[:, None]).astype(jnp.int32), axis=1)
    my_items = lax.dynamic_slice_in_dim(item_map, me * items_row, items_row)
    token_item = jnp.sum(jnp.where(segment[:, None] == jnp.arange(items_row)[None, :], my_items[None, :], 0), axis=1)
    token_hot = (token_item[:, None] == jnp.arange(sizes.small, dtype=jnp.int32)[None, :]).astype(BF16)

    scale = HEAD_DIM ** (-0.5)
    nt = functools.partial(jnp.einsum, "tk,nk->tn", preferred_element_type=F32)
    nn = functools.partial(jnp.einsum, "tn,nk->tk", preferred_element_type=F32)
    tn = functools.partial(jnp.einsum, "tn,tk->nk", preferred_element_type=F32)
    embedded = row_in.astype(F32) + nt(token_hot, small[:, 0 : sizes.small])
    first_normed = norm_rows(embedded, gains[0], shifts[0]).astype(BF16)
    projected = nt(first_normed, full_qkv)
    queries = (projected[:, 0:width] + bias_rows[0]).astype(BF16).reshape(seq_len, HEADS, HEAD_DIM)
    keys = projected[:, width : 2 * width].astype(BF16).reshape(seq_len, HEADS, HEAD_DIM)
    values = (projected[:, 2 * width :] + bias_rows[1]).astype(BF16).reshape(seq_len, HEADS, HEAD_DIM)
    head_out, log_totals = attend_forward(queries, keys, values, segment, scale)
    attended = head_out.reshape(seq_len, width)
    mid = embedded + nt(attended, full_out) + bias_rows[2]
    second_normed = norm_rows(mid, gains[1], shifts[1]).astype(BF16)
    inner = nt(second_normed, full_up) + up_row
    activated = gelu_exact(inner).astype(BF16)
    output = (mid + nt(activated, full_down) + bias_rows[3]).astype(BF16)

    grad_down = tn(row_cot, activated).astype(BF16)
    bias_down = jnp.sum(row_cot.astype(F32), axis=0)
    _, gelu_pull = jax.vjp(gelu_exact, inner)
    grad_inner = gelu_pull(nn(row_cot, full_down))[0].astype(BF16)
    grad_up = tn(grad_inner, second_normed).astype(BF16)
    grad_up_bias = jnp.sum(grad_inner.astype(F32), axis=0)
    _, norm_pull = jax.vjp(norm_rows, mid, gains[1], shifts[1])
    back_mid, gain_second, shift_second = norm_pull(nn(grad_inner, full_up))
    grad_mid = row_cot.astype(F32) + back_mid
    grad_branch = grad_mid.astype(BF16)
    grad_out = tn(grad_branch, attended).astype(BF16)
    bias_attend = jnp.sum(grad_branch.astype(F32), axis=0)
    grad_attended = nn(grad_branch, full_out).astype(BF16).reshape(seq_len, HEADS, HEAD_DIM)
    grads = attend_backward(queries, keys, values, segment, log_totals, grad_attended, scale)
    grad_projected = jnp.concatenate([g.reshape(seq_len, width) for g in grads], axis=1)
    grad_qkv = tn(grad_projected, first_normed).astype(BF16)
    bias_qkv = jnp.sum(grad_projected.astype(F32), axis=0)
    _, first_pull = jax.vjp(norm_rows, embedded, gains[0], shifts[0])
    back_first, gain_first, shift_first = first_pull(nn(grad_projected, full_qkv))
    grad_embedded = grad_mid + back_first
    row_grad = grad_embedded.astype(BF16)
    item_sums = jnp.einsum("td,ti->di", grad_embedded, token_hot.astype(F32), precision=lax.Precision.HIGHEST)
    up_lines = grad_up_bias.reshape(devices, per_up, width // devices).transpose(1, 0, 2).reshape(per_up, width)
    grad_lines = jnp.concatenate(
        (
            jnp.stack(
                (
                    gain_first, gain_second, shift_first, shift_second,
                    bias_qkv[0:width], bias_qkv[2 * width :], bias_attend, bias_down,
                )
            ),
            up_lines,
        )
    )
    grad_lines = jnp.pad(grad_lines, ((0, sizes.small - grad_lines.shape[0]), (0, 0)))
    grad_small = jnp.concatenate((item_sums, grad_lines.T), axis=1).astype(BF16)

    full_grads = [
        g.reshape(shape) for g, shape in zip((grad_small, grad_qkv, grad_out, grad_up, grad_down), sizes.weights())
    ]
    n_big = sizes.units - 1
    n_cross = -(-n_big // 3)
    rows, half, tiny = sizes.rows, sizes.half, sizes.small
    unit_shape = (rows, half)
    result_shape = jax.ShapeDtypeStruct((groups, local, width), BF16)
    final_shapes = [(rows, tiny), (rows * 3, half), (rows, half), (rows * sizes.n_ff, half), (rows, ff // 2)]
    scattered = pl.pallas_call(
        functools.partial(scatter_kernel, sizes),
        out_shape=tuple(jax.ShapeDtypeStruct((r, c), F32) for r, c in zip(own_rows, owns)) + (result_shape, result_shape),
        in_specs=[ANY] * 7,
        out_specs=(VMEM,) * 5 + (ANY, ANY),
        scratch_shapes=[pltpu.VMEM(shape, BF16) for shape in sizes.weights()]
        + [pltpu.VMEM(shape, F32) for shape in final_shapes]
        + [
            pltpu.VMEM((1, *sizes.chips, rows, tiny), BF16),
            pltpu.VMEM((1, depth, 2, rows, tiny), BF16),
            pltpu.VMEM((1, depth, rows, tiny), BF16),
            pltpu.VMEM((1, depth - 1, rows, tiny), BF16),
            pltpu.VMEM((n_big, *sizes.chips, *unit_shape), BF16),
            pltpu.VMEM((n_big, depth, 2, *unit_shape), BF16),
            pltpu.VMEM((n_big, depth, *unit_shape), BF16),
            pltpu.VMEM((n_big, depth - 1, *unit_shape), BF16),
            pltpu.VMEM((n_cross, depth - 1, 2, 2, *unit_shape), BF16),
            pltpu.VMEM((n_cross, 2, *unit_shape), BF16),
            pltpu.VMEM((n_cross, *unit_shape), BF16),
            unit_sems,
            unit_sems,
            pltpu.SemaphoreType.DMA((5, per_up)),
            pltpu.SemaphoreType.DMA((5, per_up)),
            pltpu.SemaphoreType.DMA((2, groups - 1)),
            pltpu.SemaphoreType.DMA((2, groups - 1)),
            pltpu.SemaphoreType.DMA((2,)),
            pltpu.SemaphoreType.DMA((5,)),
        ],
        compiler_params=pltpu.CompilerParams(collective_id=1, has_side_effects=True, vmem_limit_bytes=56 << 20),
    )(*full_grads, output.reshape(groups, local, width), row_grad.reshape(groups, local, width))
    end_small, end_qkv, end_out, end_up, end_down, result, input_grad = scattered
    step_hot = (jnp.arange(time_table.shape[0], dtype=jnp.int32)[:, None] == timesteps[None, :]).astype(F32)
    table_grad = jnp.einsum("si,di->sd", step_hot, end_small[:, 0:items], precision=lax.Precision.HIGHEST)
    end_lines = end_small[:, tiny:].T
    return (
        result,
        input_grad,
        table_grad,
        end_qkv.T,
        end_out.T,
        end_up.T,
        end_down.T,
        end_lines[0:2],
        end_lines[2:4],
        end_lines[4:8],
        end_lines[8 : 8 + per_up].reshape(1, -1),
    )


def on_device(*arrays):
    inputs, w_out, w_down, timesteps = arrays[0], arrays[3], arrays[5], arrays[10]
    width, ff = inputs.shape[2], w_down.shape[0]
    own = w_out.shape[1]
    fits = (
        lax.axis_size("seq") == 4
        and inputs.shape[0] == 4
        and lax.axis_size("dp") % 2 == 0
        and own % 8 == 0
        and ff % width == 0
        and width % 256 == 0
        and timesteps.shape[0] <= 128
    )
    return row_by_row(*arrays) if fits else spread_out(*arrays)


def solution(mesh):
    return jax.shard_map(
        on_device,
        mesh=mesh,
        in_specs=(
            P(None, ("dp", "seq"), None),
            P(None, ("dp", "seq")),
            P(None, ("dp", "seq")),
            P(None, ("dp", "seq")),
            P(None, ("dp", "seq")),
            P(None, ("dp", "seq")),
            P(None, ("dp", "seq")),
            P(None, ("dp", "seq")),
            P(None, ("dp", "seq")),
            P(None, ("dp", "seq")),
            P(),
            P("dp"),
            P("dp", None),
            P(None, ("dp", "seq"), None),
        ),
        out_specs=(
            P(None, ("dp", "seq"), None),
            P(None, ("dp", "seq"), None),
            P(None, ("dp", "seq")),
            P(None, ("dp", "seq")),
            P(None, ("dp", "seq")),
            P(None, ("dp", "seq")),
            P(None, ("dp", "seq")),
            P(None, ("dp", "seq")),
            P(None, ("dp", "seq")),
            P(None, ("dp", "seq")),
            P(None, ("dp", "seq")),
        ),
        check_vma=False,
    )
```

```python
import functools

import jax
import jax.numpy as jnp
from jax import lax
from jax.experimental import pallas as pl
from jax.experimental.pallas import tpu as pltpu
from jax.sharding import PartitionSpec as P

HEADS = 12
HEAD_DIM = 64


EPS = 1e-05


def norm_rows(field, gain, offset):
    mean = jnp.mean(field, axis=-1, keepdims=True)
    centred = field - mean
    spread = jnp.mean(centred * centred, axis=-1, keepdims=True)
    return centred * lax.rsqrt(spread + EPS) * gain + offset


def gelu_exact(field):
    return jax.nn.gelu(field, approximate=False)


def scores_block(query_part, keys, query_segment, key_segment, scale):
    raw = scale * jnp.einsum("qhd,khd->hqk", query_part, keys, preferred_element_type=jnp.float32)
    keep = query_segment[None, :, None] == key_segment[None, None, :]
    return jnp.where(keep, raw, -1e30)


def attend_forward(queries, keys, values, segment, scale):
    score = scores_block(queries, keys, segment, segment, scale)
    top = jnp.max(score, axis=-1, keepdims=True)
    expo = jnp.exp(score - top)
    denom = jnp.sum(expo, axis=-1, keepdims=True)
    probs = (expo / denom).astype(jnp.bfloat16)
    results = jnp.einsum("hqk,khd->qhd", probs, values, preferred_element_type=jnp.float32).astype(
        jnp.bfloat16
    )
    log_totals = [top + jnp.log(denom)]
    return (results, log_totals)


def attend_backward(queries, keys, values, segment, log_totals, grad_out, scale):
    length = queries.shape[0]
    block = min(512, length)
    grad_keys = jnp.zeros(keys.shape, jnp.float32)
    grad_values = jnp.zeros(values.shape, jnp.float32)
    grad_queries = []
    for index, begin in enumerate(range(0, length, block)):
        score = scores_block(queries, keys, segment, segment, scale)
        probs = jnp.exp(score - log_totals[index])
        grad_values = jnp.einsum(
            "hqk,qhd->khd", probs.astype(jnp.bfloat16), grad_out, preferred_element_type=jnp.float32
        )
        grad_probs = jnp.einsum(
            "qhd,khd->hqk", grad_out, values, preferred_element_type=jnp.float32
        )
        centre = jnp.sum(probs * grad_probs, axis=-1, keepdims=True)
        grad_score = (probs * (grad_probs - centre)).astype(jnp.bfloat16)
        grad_queries.append(
            (
                scale
                * jnp.einsum("hqk,khd->qhd", grad_score, keys, preferred_element_type=jnp.float32)
            ).astype(jnp.bfloat16)
        )
        grad_keys = scale * jnp.einsum(
            "hqk,qhd->khd", grad_score, queries, preferred_element_type=jnp.float32
        )
    return (grad_queries[0], grad_keys.astype(jnp.bfloat16), grad_values.astype(jnp.bfloat16))


def spread_out(
    inputs,
    time_table,
    w_qkv,
    w_out,
    w_up,
    w_down,
    norm_gains,
    norm_shifts,
    biases,
    up_bias,
    timesteps,
    item_map,
    lengths,
    cotangent,
):
    micro = inputs.shape[0]
    local = inputs.shape[1]
    width = inputs.shape[2]
    groups = lax.axis_size("seq")
    data_count = lax.axis_size("dp")
    seq_len = local * groups
    items_row = lengths.shape[1]
    heads_dev = HEADS // groups
    group_width = width // groups
    scale = HEAD_DIM ** (-0.5)
    my_start = lax.axis_index("seq") * local
    places = jnp.arange(seq_len, dtype=jnp.int32)
    slot_index = jnp.arange(items_row, dtype=jnp.int32)
    step_index = jnp.arange(time_table.shape[0], dtype=jnp.int32)
    totals = None
    results = []
    input_grads = []
    for index in range(micro):
        gathered = (
            lax.all_gather(time_table, ("dp", "seq"), axis=1, tiled=True),
            lax.all_gather(w_qkv, ("dp", "seq"), axis=1, tiled=True),
            lax.all_gather(w_out, ("dp", "seq"), axis=1, tiled=True),
            lax.all_gather(w_up, ("dp", "seq"), axis=1, tiled=True),
            lax.all_gather(w_down, ("dp", "seq"), axis=1, tiled=True),
            lax.all_gather(norm_gains, ("dp", "seq"), axis=1, tiled=True),
            lax.all_gather(norm_shifts, ("dp", "seq"), axis=1, tiled=True),
            lax.all_gather(biases, ("dp", "seq"), axis=1, tiled=True),
            lax.all_gather(up_bias, ("dp", "seq"), axis=1, tiled=True),
        )
        (
            full_table,
            full_qkv,
            full_out,
            full_up,
            full_down,
            full_gains,
            full_shifts,
            full_biases,
            full_up_bias,
        ) = gathered
        gains = full_gains.astype(jnp.float32)
        offsets = full_shifts.astype(jnp.float32)
        bias_rows = full_biases.astype(jnp.float32)
        up_row = full_up_bias.astype(jnp.float32)[0]
        if totals is None:
            totals = [jnp.zeros(a.shape, jnp.float32) for a in gathered]
        ends = jnp.cumsum(lengths[index])
        segment = jnp.sum((ends[None, :] <= places[:, None]).astype(jnp.int32), axis=1)
        my_segment = lax.dynamic_slice_in_dim(segment, my_start, local)
        slot_steps = jnp.take(timesteps, item_map[index * items_row : (index + 1) * items_row])
        token_slot = (my_segment[:, None] == slot_index[None, :]).astype(jnp.bfloat16)
        step_hot = (slot_steps[:, None] == step_index[None, :]).astype(jnp.bfloat16)
        slot_rows = jnp.dot(step_hot, full_table, preferred_element_type=jnp.float32).astype(
            jnp.bfloat16
        )
        embedded = inputs[index].astype(jnp.float32) + jnp.dot(
            token_slot, slot_rows, preferred_element_type=jnp.float32
        )
        first_normed = norm_rows(embedded, gains[0], offsets[0]).astype(jnp.bfloat16)
        projected = jnp.dot(first_normed, full_qkv, preferred_element_type=jnp.float32)
        queries = (projected[:, 0:width] + bias_rows[0]).astype(jnp.bfloat16)
        keys = projected[:, width : 2 * width].astype(jnp.bfloat16)
        values = (projected[:, 2 * width : 3 * width] + bias_rows[1]).astype(jnp.bfloat16)
        head_queries, head_keys, head_values = (
            lax.all_to_all(
                queries.reshape(local, groups, group_width),
                "seq",
                split_axis=1,
                concat_axis=0,
                tiled=True,
            ),
            lax.all_to_all(
                keys.reshape(local, groups, group_width),
                "seq",
                split_axis=1,
                concat_axis=0,
                tiled=True,
            ),
            lax.all_to_all(
                values.reshape(local, groups, group_width),
                "seq",
                split_axis=1,
                concat_axis=0,
                tiled=True,
            ),
        )
        head_queries = head_queries.reshape(seq_len, heads_dev, HEAD_DIM)
        head_keys = head_keys.reshape(seq_len, heads_dev, HEAD_DIM)
        head_values = head_values.reshape(seq_len, heads_dev, HEAD_DIM)
        head_out, log_totals = attend_forward(head_queries, head_keys, head_values, segment, scale)
        attended = lax.all_to_all(
            head_out.reshape(seq_len, 1, group_width),
            "seq",
            split_axis=0,
            concat_axis=1,
            tiled=True,
        ).reshape(local, width)
        mid = (
            embedded
            + jnp.dot(attended, full_out, preferred_element_type=jnp.float32)
            + bias_rows[2]
        )
        second_normed = norm_rows(mid, gains[1], offsets[1]).astype(jnp.bfloat16)
        inner = jnp.dot(second_normed, full_up, preferred_element_type=jnp.float32) + up_row
        activated = gelu_exact(inner).astype(jnp.bfloat16)
        results.append(
            (
                mid
                + jnp.dot(activated, full_down, preferred_element_type=jnp.float32)
                + bias_rows[3]
            ).astype(jnp.bfloat16)
        )
        grad_output = cotangent[index]
        grad_down = jnp.einsum(
            "tf,td->fd", activated, grad_output, preferred_element_type=jnp.float32
        )
        bias_down = jnp.sum(grad_output.astype(jnp.float32), axis=0)
        grad_act = jnp.einsum(
            "td,fd->tf", grad_output, full_down, preferred_element_type=jnp.float32
        )
        unused, gelu_pull = jax.vjp(gelu_exact, inner)
        grad_inner = gelu_pull(grad_act)[0].astype(jnp.bfloat16)
        grad_up = jnp.einsum(
            "td,tf->df", second_normed, grad_inner, preferred_element_type=jnp.float32
        )
        grad_up_bias = jnp.sum(grad_inner.astype(jnp.float32), axis=0)
        upstream = jnp.einsum("tf,df->td", grad_inner, full_up, preferred_element_type=jnp.float32)
        unused, norm_pull = jax.vjp(norm_rows, mid, gains[1], offsets[1])
        back_mid, gain_second, shift_second = norm_pull(upstream)
        grad_mid = grad_output.astype(jnp.float32) + back_mid
        grad_branch = grad_mid.astype(jnp.bfloat16)
        grad_out_weight = jnp.einsum(
            "te,td->ed", attended, grad_branch, preferred_element_type=jnp.float32
        )
        bias_attend = jnp.sum(grad_branch.astype(jnp.float32), axis=0)
        grad_attended = jnp.einsum(
            "td,ed->te", grad_branch, full_out, preferred_element_type=jnp.float32
        ).astype(jnp.bfloat16)
        head_grad = lax.all_to_all(
            grad_attended.reshape(local, groups, group_width),
            "seq",
            split_axis=1,
            concat_axis=0,
            tiled=True,
        ).reshape(seq_len, heads_dev, HEAD_DIM)
        grad_q_heads, grad_k_heads, grad_v_heads = attend_backward(
            head_queries, head_keys, head_values, segment, log_totals, head_grad, scale
        )
        grad_queries, grad_keys, grad_values = (
            lax.all_to_all(
                grad_q_heads.reshape(seq_len, 1, group_width),
                "seq",
                split_axis=0,
                concat_axis=1,
                tiled=True,
            ),
            lax.all_to_all(
                grad_k_heads.reshape(seq_len, 1, group_width),
                "seq",
                split_axis=0,
                concat_axis=1,
                tiled=True,
            ),
            lax.all_to_all(
                grad_v_heads.reshape(seq_len, 1, group_width),
                "seq",
                split_axis=0,
                concat_axis=1,
                tiled=True,
            ),
        )
        grad_projected = jnp.concatenate(
            (
                grad_queries.reshape(local, width),
                grad_keys.reshape(local, width),
                grad_values.reshape(local, width),
            ),
            axis=1,
        )
        grad_qkv = jnp.einsum(
            "td,tc->dc", first_normed, grad_projected, preferred_element_type=jnp.float32
        )
        bias_query = jnp.sum(grad_queries.reshape(local, width).astype(jnp.float32), axis=0)
        bias_value = jnp.sum(grad_values.reshape(local, width).astype(jnp.float32), axis=0)
        upstream_first = jnp.einsum(
            "tc,dc->td", grad_projected, full_qkv, preferred_element_type=jnp.float32
        )
        unused, first_pull = jax.vjp(norm_rows, embedded, gains[0], offsets[0])
        back_first, gain_first, shift_first = first_pull(upstream_first)
        grad_embedded = grad_mid + back_first
        input_grads.append(grad_embedded.astype(jnp.bfloat16))
        slot_sums = jnp.einsum(
            "ts,td->sd",
            token_slot.astype(jnp.float32),
            grad_embedded,
            precision=lax.Precision.HIGHEST,
        )
        grad_table = jnp.einsum(
            "si,sd->id", step_hot.astype(jnp.float32), slot_sums, precision=lax.Precision.HIGHEST
        )
        grad_gains = jnp.stack((gain_first, gain_second), axis=0)
        grad_shifts = jnp.stack((shift_first, shift_second), axis=0)
        grad_biases = jnp.stack((bias_query, bias_value, bias_attend, bias_down), axis=0)
        grad_up_row = grad_up_bias[None, :]
        fresh = (
            grad_table,
            grad_qkv,
            grad_out_weight,
            grad_up,
            grad_down,
            grad_gains,
            grad_shifts,
            grad_biases,
            grad_up_row,
        )
        totals = [a + b for a, b in zip(totals, fresh)]

    def spread(grad):
        return grad.reshape(
            grad.shape[0], data_count, groups, grad.shape[1] // (data_count * groups)
        )

    parts = [spread(a) for a in totals]
    folded = (
        lax.all_to_all(
            parts[0].astype(jnp.bfloat16), "seq", split_axis=2, concat_axis=2, tiled=True
        ).astype(jnp.float32),
        lax.all_to_all(
            parts[1].astype(jnp.bfloat16), "seq", split_axis=2, concat_axis=2, tiled=True
        ).astype(jnp.float32),
        lax.all_to_all(
            parts[2].astype(jnp.bfloat16), "seq", split_axis=2, concat_axis=2, tiled=True
        ).astype(jnp.float32),
        lax.all_to_all(
            parts[3].astype(jnp.bfloat16), "seq", split_axis=2, concat_axis=2, tiled=True
        ).astype(jnp.float32),
        lax.all_to_all(
            parts[4].astype(jnp.bfloat16), "seq", split_axis=2, concat_axis=2, tiled=True
        ).astype(jnp.float32),
        lax.all_to_all(
            parts[5].astype(jnp.bfloat16), "seq", split_axis=2, concat_axis=2, tiled=True
        ).astype(jnp.float32),
        lax.all_to_all(
            parts[6].astype(jnp.bfloat16), "seq", split_axis=2, concat_axis=2, tiled=True
        ).astype(jnp.float32),
        lax.all_to_all(
            parts[7].astype(jnp.bfloat16), "seq", split_axis=2, concat_axis=2, tiled=True
        ).astype(jnp.float32),
        lax.all_to_all(
            parts[8].astype(jnp.bfloat16), "seq", split_axis=2, concat_axis=2, tiled=True
        ).astype(jnp.float32),
    )
    merged = [jnp.sum(f, axis=2, keepdims=True) for f in folded]
    owners = (
        lax.psum_scatter(merged[0], "dp", scatter_dimension=1, tiled=True),
        lax.psum_scatter(merged[1], "dp", scatter_dimension=1, tiled=True),
        lax.psum_scatter(merged[2], "dp", scatter_dimension=1, tiled=True),
        lax.psum_scatter(merged[3], "dp", scatter_dimension=1, tiled=True),
        lax.psum_scatter(merged[4], "dp", scatter_dimension=1, tiled=True),
        lax.psum_scatter(merged[5], "dp", scatter_dimension=1, tiled=True),
        lax.psum_scatter(merged[6], "dp", scatter_dimension=1, tiled=True),
        lax.psum_scatter(merged[7], "dp", scatter_dimension=1, tiled=True),
        lax.psum_scatter(merged[8], "dp", scatter_dimension=1, tiled=True),
    )
    owned = [o.reshape(o.shape[0], o.shape[3]) for o in owners]
    return (
        jnp.stack(results, axis=0),
        jnp.stack(input_grads, axis=0),
        owned[0],
        owned[1],
        owned[2],
        owned[3],
        owned[4],
        owned[5],
        owned[6],
        owned[7],
        owned[8],
    )


F32 = jnp.float32
BF16 = jnp.bfloat16
MESH = pl.DeviceIdType.MESH
VMEM_LIMIT = 63 << 20
VMEM = pl.BlockSpec(memory_space=pltpu.VMEM)
ANY = pl.BlockSpec(memory_space=pl.ANY)
ALL = slice(None)
ORDER_FIRST = "zxy"
ORDERS_SECOND = ("zxy", "zyx", "yxz")


class Place:
    def __init__(self):
        row, column = lax.axis_index("dp"), lax.axis_index("seq")
        self.at = {"z": row // 2, "y": row % 2, "x": column // 2}
        self.core = column % 2
        self.column = column
        self.depth = lax.axis_size("dp") // 2

    def device(self, core=None, **moved):
        at = {**self.at, **moved}
        core = self.core if core is None else core
        return (at["z"] * 2 + at["y"], at["x"] * 2 + core)

    def other(self, axis):
        return 1 - self.at[axis]

    def around(self, step):
        return (self.at["z"] + step) % self.depth

    def sibling(self):
        return self.device(core=1 - self.core)

    def partners(self):
        found = [self.sibling(), self.device(x=self.other("x")), self.device(y=self.other("y"))]
        found.append(self.device(core=1 - self.core, x=self.other("x")))
        found += [self.device(z=self.around(step)) for step in range(1, self.depth)]
        return found


def meet(place):
    barrier = pltpu.get_barrier_semaphore()
    partners = place.partners()
    for partner in partners:
        pl.semaphore_signal(barrier, inc=1, device_id=partner, device_id_type=MESH)
    pl.semaphore_wait(barrier, len(partners))


def remote(source, target, send, receive, device):
    return pltpu.make_async_remote_copy(
        src_ref=source,
        dst_ref=target,
        send_sem=send,
        recv_sem=receive,
        device_id=device,
        device_id_type=MESH,
    )


def order_of(core, unit):
    return ORDER_FIRST if core == 0 else ORDERS_SECOND[unit % len(ORDERS_SECOND)]


def on_core(place, core):
    return pl.when(place.core == core)


class Gather:
    def __init__(self, place, unit, view, send, receive):
        self.place, self.unit, self.view = place, unit, view
        self.send, self.receive = send, receive

    def index(self, order, stage):
        return {a: (ALL if a in order[:stage] else self.place.at[a]) for a in "zyx"}

    def part(self, core, index):
        return self.view(index["z"], index["y"], index["x"], core)

    def copies(self, core, stage):
        order = order_of(core, self.unit)
        if stage == 3:
            whole = self.view(ALL, ALL, ALL, core)
            slot = self.place.depth + 1
            return [remote(whole, whole, self.send.at[self.unit, slot], self.receive.at[self.unit, slot], self.place.sibling())]
        axis, index = order[stage], self.index(order, stage)
        mine = self.part(core, index)
        if axis != "z":
            slot = self.place.depth - 1 + sum(a != "z" for a in order[:stage])
            device = self.place.device(**{axis: self.place.other(axis)})
            return [remote(mine, mine, self.send.at[self.unit, slot], self.receive.at[self.unit, slot], device)]
        return [
            remote(
                mine,
                mine,
                self.send.at[self.unit, step - 1],
                self.receive.at[self.unit, step - 1],
                self.place.device(z=self.place.around(step)),
            )
            for step in range(1, self.place.depth)
        ]

    def start(self, stage):
        for core in range(2):

            @on_core(self.place, core)
            def _():
                for copy in self.copies(core, stage):
                    copy.start()

    def arrived(self, stage):
        for core in range(2):

            @on_core(self.place, core)
            def _():
                for copy in self.copies(core, stage):
                    copy.wait_recv()

    def sibling_arrived(self):
        for core in range(2):

            @on_core(self.place, core)
            def _():
                for copy in self.copies(1 - core, 3):
                    copy.wait_recv()

    def sent(self):
        for core in range(2):

            @on_core(self.place, core)
            def _():
                for stage in range(4):
                    for copy in self.copies(core, stage):
                        copy.wait_send()


class Scatter:
    def __init__(self, place, unit, view, first, landings, send, receive):
        self.place, self.unit, self.view = place, unit, view
        self.first, self.landings = first, landings
        self.send, self.receive = send, receive

    def own(self, core, index):
        return self.view(index["z"], index["y"], index["x"], core)

    def sibling_copy(self, core):
        theirs = self.view(ALL, ALL, ALL, 1 - core)
        slot = self.place.depth + 1
        return remote(theirs, self.first, self.send.at[self.unit, slot], self.receive.at[self.unit, slot], self.place.sibling())

    def stage_copies(self, core, stage):
        order = order_of(core, self.unit)[::-1]
        axis = order[stage]
        index = {a: (self.place.at[a] if a in order[:stage] else ALL) for a in "zyx"}
        mine = self.own(core, {**index, axis: self.place.at[axis]})
        landing = self.landings(order)[stage]
        if axis != "z":
            slot = self.place.depth - 1 + sum(a != "z" for a in order[:stage])
            gone = self.own(core, {**index, axis: self.place.other(axis)})
            device = self.place.device(**{axis: self.place.other(axis)})
            copy = remote(gone, landing, self.send.at[self.unit, slot], self.receive.at[self.unit, slot], device)
            return [(copy, mine, landing)]
        found = []
        for step in range(1, self.place.depth):
            gone = self.own(core, {**index, "z": self.place.around(step)})
            copy = remote(
                gone,
                landing.at[step - 1],
                self.send.at[self.unit, step - 1],
                self.receive.at[self.unit, step - 1],
                self.place.device(z=self.place.around(step)),
            )
            found.append((copy, mine, landing.at[step - 1]))
        return found

    def start_sibling(self):
        for core in range(2):

            @on_core(self.place, core)
            def _():
                self.sibling_copy(core).start()

    def add_sibling(self):
        for core in range(2):

            @on_core(self.place, core)
            def _():
                self.sibling_copy(core).wait_recv()
                mine = self.view(ALL, ALL, ALL, core)
                mine[...] = (mine[...].astype(F32) + self.first[...].astype(F32)).astype(BF16)

    def start(self, stage):
        for core in range(2):

            @on_core(self.place, core)
            def _():
                for copy, _, _ in self.stage_copies(core, stage):
                    copy.start()

    def add(self, stage, result=None):
        for core in range(2):

            @on_core(self.place, core)
            def _():
                found = self.stage_copies(core, stage)
                for copy, _, _ in found:
                    copy.wait_recv()
                mine = found[0][1]
                total = mine[...].astype(F32)
                for _, _, landing in found:
                    total = total + landing[...].astype(F32)
                if stage == 2:
                    result(core)[...] = total
                else:
                    mine[...] = total.astype(BF16)

    def sent(self):
        for core in range(2):

            @on_core(self.place, core)
            def _():
                self.sibling_copy(core).wait_send()
                for stage in range(3):
                    for copy, _, _ in self.stage_copies(core, stage):
                        copy.wait_send()


class Sizes:
    def __init__(self, width, ff, devices, depth, items):
        self.width, self.ff, self.devices, self.depth, self.items = width, ff, devices, depth, items
        self.half = width // 2
        self.own = width // devices
        self.rows = 2 * self.own
        self.n_qkv, self.n_ff = 3, ff // width
        self.small = 128
        self.units = 1 + self.n_qkv + 1 + 2 * self.n_ff
        self.chips = (depth, 2, 2)

    def weights(self):
        return [
            (*self.chips, self.rows, 2 * self.small),
            (*self.chips, self.n_qkv, self.rows, self.width),
            (*self.chips, self.rows, self.width),
            (*self.chips, self.n_ff, self.rows, self.width),
            (*self.chips, self.rows, self.ff),
        ]

    def own_shapes(self):
        widths = [2 * self.small, self.width, self.width, self.width, self.ff]
        return [(self.own * n, w) for n, w in zip((1, self.n_qkv, 1, self.n_ff, 1), widths)]

    def views(self, refs):
        small, qkv, out, up, down = refs
        half = self.half

        def columns(core, base=0, width=half):
            return pl.ds(base + core * width, width)

        found = [lambda z, y, x, core: small.at[z, y, x, :, columns(core, 0, self.small)]]
        for unit in range(self.n_qkv):
            found.append(lambda z, y, x, core, unit=unit: qkv.at[z, y, x, unit, :, columns(core)])
        found.append(out if callable(out) else lambda z, y, x, core: out.at[z, y, x, :, columns(core)])
        for unit in range(self.n_ff):
            found.append(lambda z, y, x, core, unit=unit: up.at[z, y, x, unit, :, columns(core)])
        for unit in range(self.n_ff):
            found.append(lambda z, y, x, core, unit=unit: down.at[z, y, x, :, columns(core, unit * self.width)])
        return found


def dot(a, b, ca, cb):
    return lax.dot_general(a, b, (((ca,), (cb,)), ((), ())), preferred_element_type=F32)


def iota(shape, axis):
    return lax.broadcasted_iota(jnp.int32, shape, axis)


def normalized(field):
    mean = jnp.mean(field, axis=-1, keepdims=True)
    centred = field - mean
    spread = jnp.mean(centred * centred, axis=-1, keepdims=True)
    rs = lax.rsqrt(spread + EPS)
    return centred * rs, rs


def loop(count, body):
    lax.fori_loop(0, count, lambda i, c: (body(i), c)[1], 0)


def span(i, size):
    return pl.ds(pl.multiple_of(i * size, size), size)


def flat(block, columns):
    return block.reshape(-1, columns)


TILE = 128


class Layer:
    def __init__(self, sizes, weights, grads, row_x, row_cot, scratch):
        self.s = sizes
        self.small, self.qkv_w, self.out_w, self.up_w, self.down_w = weights
        self.g_small, self.g_qkv, self.g_out, self.g_up, self.g_down = grads
        self.row_x, self.row_cot = row_x, row_cot
        (
            self.embedded, self.first, self.qkv, self.attended, self.log_total, self.mid, self.second,
            self.active, self.slope, self.result, self.total, self.branch, self.bias, self.token_hot,
            self.lines, self.qkv_bias, self.up_row, self.spread, self.grad_lines, self.up_sum,
        ) = scratch
        self.length = self.embedded.shape[0]


    def prepare(self, lengths, item_map, me):
        n, wide = self.length, self.s.small
        count = lengths.shape[1]
        ends = [lengths[me, 0]]
        for slot in range(1, count - 1):
            ends.append(ends[-1] + lengths[me, slot])
        items = [item_map[me * count + slot] for slot in range(count)]

        def segment(position):
            return sum((position >= end).astype(jnp.int32) for end in ends)

        columns = segment(iota((1, n), 1))

        def masks(i):
            rows = segment(iota((TILE, 1), 0) + i * TILE)
            self.bias[span(i, TILE), :] = jnp.where(rows == columns, 0.0, -1e30)
            item = jnp.full((TILE, 1), items[-1], jnp.int32)
            for slot in range(count - 1):
                item = jnp.where(rows == slot, items[slot], item)
            self.token_hot[span(i, TILE), :] = (item == iota((TILE, wide), 1)).astype(BF16)

        loop(n // TILE, masks)
        own, per = self.s.own, self.s.n_ff
        part = self.spread.shape[0]
        row, column = iota((part, 1), 0), iota((1, self.s.width), 1)
        same = (row // own == column // (per * own)) & (row % own == column % own)
        self.spread[...] = same.astype(BF16)

    def small_lines(self):
        s = self.s
        eye = (iota((16, s.small), 0) == iota((16, s.small), 1)).astype(BF16)
        lines = dot(eye, flat(self.small[:, :, :, :, s.small :], s.small), 1, 1)
        self.lines[...] = lines
        zero = jnp.zeros((1, s.width), F32)
        self.qkv_bias[...] = jnp.concatenate([lines[4:5], zero, lines[5:6]], axis=1)
        part = self.spread.shape[0]
        turn = (iota((1, s.width), 1) // s.own) % s.n_ff
        picked = turn == iota((s.n_ff, 1), 0)
        for tile in range(s.n_ff):
            seen = lines[8 : 8 + s.n_ff, tile * part : (tile + 1) * part].astype(BF16)
            moved = dot(seen, self.spread[...], 1, 0)
            self.up_row[:, tile * s.width : (tile + 1) * s.width] = jnp.sum(
                jnp.where(picked, moved, 0.0), axis=0, keepdims=True
            )
        self.grad_lines[...] = jnp.zeros_like(self.grad_lines)
        self.up_sum[...] = jnp.zeros_like(self.up_sum)

    def norm_first(self):
        gain, shift = self.lines[0:1, :], self.lines[2:3, :]
        items = flat(self.small[:, :, :, :, 0 : self.s.small], self.s.small)

        def body(i):
            field = self.row_x[i].astype(F32) + dot(self.token_hot[span(i, TILE), :], items, 1, 1)
            self.embedded[span(i, TILE), :] = field
            n, _ = normalized(field)
            self.first[span(i, TILE), :] = (n * gain + shift).astype(BF16)

        loop(self.length // TILE, body)

    def project(self, i):
        width = 2 * self.qkv_w.shape[1] * self.qkv_w.shape[2] * self.qkv_w.shape[3] * self.s.rows
        weight = flat(self.qkv_w[2 * i : 2 * i + 2], self.s.width)
        lanes = slice(i * width, (i + 1) * width)
        self.qkv[:, lanes] = (dot(self.first[...], weight, 1, 1) + self.qkv_bias[:, lanes]).astype(BF16)

    def heads(self, base, pair):
        return pl.ds(pl.multiple_of(base + pair * 2 * HEAD_DIM, 2 * HEAD_DIM), 2 * HEAD_DIM)

    def attend(self, low, high):
        width, block = self.s.width, 256
        lane = iota((1, 2 * HEAD_DIM), 1)
        mine = [lane < HEAD_DIM, lane >= HEAD_DIM]
        scale = HEAD_DIM ** (-0.5)

        def body(pair, carry):
            keys = self.qkv[:, self.heads(width, pair)]
            values = self.qkv[:, self.heads(2 * width, pair)]
            for part in range(self.length // block):
                rows = slice(part * block, (part + 1) * block)
                queries = self.qkv[rows, self.heads(0, pair)] * jnp.asarray(scale, BF16)
                logs = self.log_total[rows, :]
                found = []
                for head in range(2):
                    one = jnp.where(mine[head], queries, jnp.zeros_like(queries))
                    score = dot(one, keys, 1, 1) + self.bias[rows, :]
                    top = jnp.max(score, axis=-1, keepdims=True)
                    expo = jnp.exp(score - top)
                    denom = jnp.sum(expo, axis=-1, keepdims=True)
                    probs = (expo * (1.0 / denom)).astype(BF16)
                    found.append(dot(probs, values, 1, 0))
                    logs = jnp.where(lane == 2 * pair + head, top + jnp.log(denom), logs)
                self.log_total[rows, :] = logs
                self.attended[rows, self.heads(0, pair)] = jnp.where(mine[0], found[0], found[1]).astype(BF16)
            return carry

        lax.fori_loop(low, high, body, 0)

    def merge(self):
        width = self.s.width
        for i in range(2):
            weight = flat(self.out_w[2 * i : 2 * i + 2], width)
            lanes = slice(i * weight.shape[0], (i + 1) * weight.shape[0])
            self.mid[:, lanes] = self.embedded[:, lanes] + dot(self.attended[...], weight, 1, 1) + self.lines[6:7, lanes]

    def norm_second(self):
        gain, shift = self.lines[1:2, :], self.lines[3:4, :]

        def body(i):
            n, _ = normalized(self.mid[span(i, TILE), :])
            self.second[span(i, TILE), :] = (n * gain + shift).astype(BF16)

        loop(self.length // TILE, body)

    def activate(self, z):
        half = self.s.ff // (2 * self.s.depth)
        for y in range(2):
            lanes = slice((2 * z + y) * half, (2 * z + y + 1) * half)
            weight = flat(self.up_w[z, y], self.s.width)
            inner = dot(self.second[...], weight, 1, 1) + self.up_row[:, lanes]
            mass = 0.5 + 0.5 * lax.erf(inner * (0.5**0.5))
            self.active[:, lanes] = (inner * mass).astype(BF16)
            bell = jnp.exp(-0.5 * inner * inner) * 0.3989422804014327
            self.slope[:, lanes] = (mass + inner * bell).astype(BF16)

    def finish(self):
        width = self.s.width
        for i in range(2):
            weight = flat(self.down_w[2 * i : 2 * i + 2], self.s.ff)
            lanes = slice(i * weight.shape[0], (i + 1) * weight.shape[0])
            field = self.mid[:, lanes] + dot(self.active[...], weight, 1, 1) + self.lines[7:8, lanes]
            for part in range(self.length // TILE):
                self.result[part, :, lanes] = field[part * TILE : (part + 1) * TILE].astype(BF16)


    def cotangent(self):
        return flat(self.row_cot[...], self.s.width)

    def grad_down(self, unit):
        width = self.s.width
        lanes = slice(unit * width, (unit + 1) * width)
        grad = dot(self.cotangent(), self.active[:, lanes], 0, 0).astype(BF16)
        self.g_down[:, :, :, :, lanes] = grad.reshape(*self.s.chips, self.s.rows, width)

    def bias_down(self):
        self.grad_lines[7:8, :] = jnp.sum(self.cotangent().astype(F32), axis=0, keepdims=True)

    def back_active(self, unit):
        width = self.s.width
        for part in range(2):
            lanes = slice(unit * width + part * width // 2, unit * width + (part + 1) * width // 2)
            weight = flat(self.down_w[:, :, :, :, lanes], width // 2)
            grad = dot(self.cotangent(), weight, 1, 0)
            inner = (self.slope[:, lanes].astype(F32) * grad).astype(BF16)
            self.slope[:, lanes] = inner
            self.up_sum[:, lanes] = jnp.sum(inner.astype(F32), axis=0, keepdims=True)

    def grad_up(self, z):
        half = self.s.ff // (2 * self.s.depth)
        for y in range(2):
            lanes = slice((2 * z + y) * half, (2 * z + y + 1) * half)
            grad = dot(self.slope[:, lanes], self.second[...], 0, 0).astype(BF16)
            self.g_up[z, y] = grad.reshape(2, self.s.n_ff, self.s.rows, self.s.width)

    def back_up(self):
        half = self.s.half
        for part in range(2):
            lanes = slice(part * half, (part + 1) * half)
            weight = flat(self.up_w[:, :, :, :, :, lanes], half)
            self.total[:, lanes] = dot(self.slope[...], weight, 1, 0)

    def norm_second_back(self):
        gain = self.lines[1:2, :]
        zero = jnp.zeros((1, self.s.width), F32)

        def body(i, sums):
            upstream = self.total[span(i, TILE), :]
            n, rs = normalized(self.mid[span(i, TILE), :])
            u = upstream * gain
            back = rs * (u - jnp.mean(u, axis=-1, keepdims=True) - n * jnp.mean(u * n, axis=-1, keepdims=True))
            grad = self.row_cot[i].astype(F32) + back
            self.mid[span(i, TILE), :] = grad
            low = grad.astype(BF16)
            self.branch[span(i, TILE), :] = low
            fresh = (upstream * n, upstream, low.astype(F32))
            return tuple(a + jnp.sum(b, axis=0, keepdims=True) for a, b in zip(sums, fresh))

        sums = lax.fori_loop(0, self.length // TILE, body, (zero, zero, zero))
        self.grad_lines[1:2, :] = sums[0]
        self.grad_lines[3:4, :] = sums[1]
        self.grad_lines[6:7, :] = sums[2]

    def grad_out(self):
        grad = dot(self.branch[...], self.attended[...], 0, 0).astype(BF16)
        self.g_out[...] = grad.reshape(*self.s.chips, self.s.rows, self.s.width)

    def back_out(self):
        weight = flat(self.out_w[...], self.s.width)
        self.attended[...] = dot(self.branch[...], weight, 1, 0).astype(BF16)

    def attend_back(self, low, high):
        width, block = self.s.width, 256
        lane = iota((1, 2 * HEAD_DIM), 1)
        mine = [lane < HEAD_DIM, lane >= HEAD_DIM]
        scale = HEAD_DIM ** (-0.5)

        def body(pair, carry):
            queries = self.qkv[:, self.heads(0, pair)]
            keys = self.qkv[:, self.heads(width, pair)]
            values = self.qkv[:, self.heads(2 * width, pair)]
            grads = self.attended[:, self.heads(0, pair)]
            grad_keys, grad_values, grad_queries = [0.0, 0.0], [0.0, 0.0], []
            for part in range(self.length // block):
                rows = slice(part * block, (part + 1) * block)
                query, grad = queries[rows], grads[rows]
                scaled = query * jnp.asarray(scale, BF16)
                logs = self.log_total[rows, :]
                found = []
                for head in range(2):
                    one = jnp.where(mine[head], scaled, jnp.zeros_like(scaled))
                    own = jnp.where(mine[head], grad, jnp.zeros_like(grad))
                    log = jnp.sum(jnp.where(lane == 2 * pair + head, logs, 0.0), axis=-1, keepdims=True)
                    probs = jnp.exp(dot(one, keys, 1, 1) + self.bias[rows, :] - log)
                    grad_probs = dot(own, values, 1, 1)
                    centre = jnp.sum(probs * grad_probs, axis=-1, keepdims=True)
                    grad_score = (probs * (grad_probs - centre)).astype(BF16)
                    grad_values[head] += dot(probs.astype(BF16), grad, 0, 0)
                    grad_keys[head] += dot(grad_score, query, 0, 0)
                    found.append(dot(grad_score, keys, 1, 0))
                grad_queries.append(scale * jnp.where(mine[0], found[0], found[1]))
            for part, grad in enumerate(grad_queries):
                self.qkv[part * block : (part + 1) * block, self.heads(0, pair)] = grad.astype(BF16)
            self.qkv[:, self.heads(width, pair)] = (scale * jnp.where(mine[0], grad_keys[0], grad_keys[1])).astype(BF16)
            self.qkv[:, self.heads(2 * width, pair)] = jnp.where(mine[0], grad_values[0], grad_values[1]).astype(BF16)
            return carry

        lax.fori_loop(low, high, body, 0)

    def grad_qkv(self, i):
        width, half = self.s.width, self.s.half
        span_z = 2 * self.qkv_w.shape[1] * self.qkv_w.shape[2] * self.qkv_w.shape[3] * self.s.rows
        lanes = slice(i * span_z, (i + 1) * span_z)
        for part in range(2):
            columns = slice(part * half, (part + 1) * half)
            grad = dot(self.qkv[:, lanes], self.first[:, columns], 0, 0).astype(BF16)
            self.g_qkv[2 * i : 2 * i + 2, :, :, 0 : self.s.n_qkv, :, columns] = grad.reshape(
                2, 2, 2, self.s.n_qkv, self.s.rows, half
            )

    def back_qkv(self):
        half = self.s.half
        for part in range(2):
            lanes = slice(part * half, (part + 1) * half)
            weight = flat(self.qkv_w[:, :, :, :, :, lanes], half)
            self.total[:, lanes] = dot(self.qkv[...], weight, 1, 0)

    def norm_first_back(self):
        gain = self.lines[0:1, :]
        width = self.s.width
        zero = jnp.zeros((1, width), F32)

        def body(i, sums):
            upstream = self.total[span(i, TILE), :]
            n, rs = normalized(self.embedded[span(i, TILE), :])
            u = upstream * gain
            back = rs * (u - jnp.mean(u, axis=-1, keepdims=True) - n * jnp.mean(u * n, axis=-1, keepdims=True))
            grad = self.mid[span(i, TILE), :] + back
            self.row_x[i] = grad.astype(BF16)
            projected = self.qkv[span(i, TILE), :].astype(F32)
            fresh = (upstream * n, upstream, projected[:, 0:width], projected[:, 2 * width :])
            return tuple(a + jnp.sum(b, axis=0, keepdims=True) for a, b in zip(sums, fresh))

        sums = lax.fori_loop(0, self.length // TILE, body, (zero,) * 4)
        self.grad_lines[0:1, :] = sums[0]
        self.grad_lines[2:3, :] = sums[1]
        self.grad_lines[4:5, :] = sums[2]
        self.grad_lines[5:6, :] = sums[3]

    def grad_small(self):
        s = self.s
        part = self.spread.shape[0]
        turn = (iota((1, s.width), 1) // s.own) % s.n_ff
        picked = turn == iota((s.n_ff, 1), 0)
        for tile in range(s.n_ff):
            seen = self.up_sum[:, tile * s.width : (tile + 1) * s.width]
            moved = dot(jnp.where(picked, seen, 0.0).astype(BF16), self.spread[...], 1, 1)
            self.grad_lines[8 : 8 + s.n_ff, tile * part : (tile + 1) * part] = moved
        eye = (iota((16, s.small), 0) == iota((16, s.small), 1)).astype(BF16)
        lines = dot(self.grad_lines[...].astype(BF16), eye, 0, 0).astype(BF16)
        self.g_small[:, :, :, :, s.small :] = lines.reshape(*s.chips, s.rows, s.small)
        sums = dot(flat(self.row_x[...], s.width), self.token_hot[...], 0, 0).astype(BF16)
        self.g_small[:, :, :, :, 0 : s.small] = sums.reshape(*s.chips, s.rows, s.small)


LAG = 2


def layer_kernel(
    sizes, inputs, cotangent, table, qkv, out, up, down, vectors, steps, lengths, item_map,
    end_small, end_qkv, end_out, end_up, end_down, result, input_grad,
    w_small, w_qkv, w_out, w_up, w_down, g_small, g_up, g_down,
    own_small, own_qkv, own_out, own_up, own_down,
    sib_small, sib_qkv, sib_out, sib_up, sib_down,
    f_small, f_qkv, f_out, f_up, f_down,
    first_small, first_down, pool_small, pool, row_x, row_cot, *rest,
):
    scratch, sems = rest[:20], rest[20:]
    (
        send, receive, back_send, back_receive, raw_send, raw_receive, row_send, row_receive, row_local,
        end_send, end_receive, free,
    ) = sems
    place = Place()
    half, depth = sizes.half, sizes.depth
    me = place.column
    groups = inputs.shape[0]
    weights = [w_small, w_qkv, w_out, w_up, w_down]
    own = [own_small, own_qkv, own_out, own_up, own_down]
    sib = [sib_small, sib_qkv, sib_out, sib_up, sib_down]
    finals = [f_small, f_qkv, f_out, f_up, f_down]
    ends = [end_small, end_qkv, end_out, end_up, end_down]
    grad_out = w_up.at[:, :, :, sizes.n_qkv]
    layer = Layer(sizes, weights, [g_small, w_up, grad_out, g_up, g_down], row_x, row_cot, scratch)

    def width_of(slot):
        return sizes.small if slot == 0 else half

    hot = (steps[...] == iota((sizes.items, table.shape[1]), 1)).astype(BF16)
    own_small[...] = jnp.zeros_like(own_small)
    own_small[:, 0 : sizes.items] = dot(table[...], hot, 1, 1)
    eye = (iota((vectors.shape[0], sizes.small), 0) == iota((vectors.shape[0], sizes.small), 1)).astype(BF16)
    own_small[:, sizes.small :] = dot(vectors[...], eye, 0, 0)
    for source, target in ((qkv, own_qkv), (out, own_out), (up, own_up), (down, own_down)):
        target[...] = source[...].astype(F32)

    def row_copies(which, source, target):
        found = []
        for step in range(1, groups):
            peer = (me + step) % groups
            found.append(
                remote(
                    source.at[peer], target.at[me], row_send.at[which, step - 1], row_receive.at[which, step - 1],
                    (lax.axis_index("dp"), peer),
                )
            )
        return found, pltpu.make_async_copy(source.at[me], target.at[me], row_local.at[which])

    rows = [
        row_copies(0, inputs, row_x),
        row_copies(1, cotangent, row_cot),
        row_copies(2, layer.result, result),
        row_copies(3, row_x, input_grad),
    ]

    def start_rows(which):
        for copy in [*rows[which][0], rows[which][1]]:
            copy.start()

    def rows_arrived(which):
        for copy in rows[which][0]:
            copy.wait_recv()
        rows[which][1].wait()

    def rows_sent(which):
        for copy in rows[which][0]:
            copy.wait_send()

    def raw_copies(core):
        found = []
        for slot, (mine, theirs) in enumerate(zip(own, sib)):
            wide = width_of(slot)
            for part in range(mine.shape[1] // (2 * wide)):
                found.append(
                    remote(
                        mine.at[:, pl.ds((2 * part + 1 - core) * wide, wide)],
                        theirs.at[:, pl.ds(part * wide, wide)],
                        raw_send.at[slot, part],
                        raw_receive.at[slot, part],
                        place.sibling(),
                    )
                )
        return found

    def place_own(core):
        copies = raw_copies(core)
        index = 0
        z, y, x = (place.at[a] for a in "zyx")
        for slot, (mine, theirs) in enumerate(zip(own, sib)):
            wide = width_of(slot)
            for part in range(mine.shape[1] // (2 * wide)):
                copies[index].wait_recv()
                index += 1
                here = mine[:, (2 * part + core) * wide : (2 * part + core + 1) * wide]
                there = theirs[:, part * wide : (part + 1) * wide]
                block = jnp.concatenate([here, there] if core == 0 else [there, here], axis=0).astype(BF16)
                lanes = pl.ds((2 * part + core) * wide, wide)
                if weights[slot].ndim == 6:
                    for unit in range(weights[slot].shape[3]):
                        weights[slot][z, y, x, unit, :, lanes] = block[unit * sizes.rows : (unit + 1) * sizes.rows]
                else:
                    weights[slot][z, y, x, :, lanes] = block

    arriving = [Gather(place, unit, view, send, receive) for unit, view in enumerate(sizes.views(weights))]
    count = len(arriving)

    def gather_beat(beat):
        for stage in (3, 2, 1, 0):
            unit = beat - stage * LAG
            if 0 <= unit < count:
                if stage:
                    arriving[unit].arrived(stage - 1)
                    arriving[unit].start(stage)
                elif unit + 2 < count:
                    arriving[unit + 2].start(0)

    def whole(*units):
        for unit in units:
            arriving[unit].sibling_arrived()

    spots = [(0, 0)] + [(1, u) for u in range(sizes.n_qkv)] + [(2, 0)]
    spots += [(3, u) for u in range(sizes.n_ff)] + [(4, u) for u in range(sizes.n_ff)]
    views = sizes.views([g_small, w_up, lambda z, y, x, core: w_up.at[z, y, x, sizes.n_qkv, :, pl.ds(core * half, half)], g_up, g_down])
    down_unit = 1 + sizes.n_qkv + 1 + sizes.n_ff

    def landings(unit, order):
        here = (lambda *i: pool_small.at[i]) if unit == 0 else (lambda *i: pool.at[(unit - 1, *i)])
        some = pl.ds(0, depth - 1)
        if order[0] == "z":
            return here(some), here(depth - 1, ALL, 0), here(depth - 1, 0, 1)
        return here(ALL, 0), here(ALL, 1, 0), here(some, 1, 1)

    def first_landing(unit):
        if unit == 0:
            return first_small
        if unit >= down_unit:
            return first_down.at[unit - down_unit]
        return w_down.at[:, :, :, :, pl.ds((unit - 1) * half, half)]

    leaving = [
        Scatter(
            place, unit, view, first_landing(unit), functools.partial(landings, unit), back_send, back_receive
        )
        for unit, view in enumerate(views)
    ]

    def final(unit):
        slot, part = spots[unit]
        if slot == 4:
            return lambda core: finals[slot].at[:, pl.ds(part * half, half)]
        return lambda core: finals[slot].at[pl.ds(part * sizes.rows, sizes.rows), :]

    def end_copies(core, slot):
        wide = width_of(slot)
        count = ends[slot].shape[0]
        found = []
        for part in range(finals[slot].shape[1] // wide):
            source = finals[slot].at[pl.ds((1 - core) * count, count), pl.ds(part * wide, wide)]
            target = ends[slot].at[:, pl.ds((2 * part + core) * wide, wide)]
            found.append(remote(source, target, end_send.at[slot, part], end_receive.at[slot, part], place.sibling()))
        return found

    def close(slot):
        wide = width_of(slot)
        count = ends[slot].shape[0]
        for core in range(2):

            @on_core(place, core)
            def _():
                for copy in end_copies(core, slot):
                    copy.start()
                for part in range(finals[slot].shape[1] // wide):
                    ends[slot][:, (2 * part + core) * wide : (2 * part + core + 1) * wide] = finals[slot][
                        core * count : (core + 1) * count, part * wide : (part + 1) * wide
                    ]

    qkv_units = list(range(1, 1 + sizes.n_qkv))
    out_unit = 1 + sizes.n_qkv
    up_units = list(range(out_unit + 1, down_unit))
    down_units = list(range(down_unit, count))
    ready, born = [], {}
    state = {"beat": 0}

    def offer(unit):
        leaving[unit].start_sibling()
        ready.append(unit)

    def scatter_beat():
        beat = state["beat"]
        state["beat"] += 1
        fresh = [unit for unit in ready if unit not in born][:1]
        for unit in fresh:
            born[unit] = beat
        for unit in ready:
            if unit not in born or (beat - born[unit]) % LAG:
                continue
            stage = (beat - born[unit]) // LAG
            if stage > 3:
                continue
            if stage == 0:
                leaving[unit].add_sibling()
            else:
                leaving[unit].add(stage - 1, final(unit))
            if stage < 3:
                leaving[unit].start(stage)
            else:
                done.append(unit)
                slot = spots[unit][0]
                if all(other in done for other in range(count) if spots[other][0] == slot):
                    close(slot)

    done = []

    meet(place)
    for core in range(2):

        @on_core(place, core)
        def _():
            for copy in raw_copies(core):
                copy.start()

    start_rows(0)
    for core in range(2):

        @on_core(place, core)
        def _():
            place_own(core)

    arriving[0].start(0)
    arriving[1].start(0)
    gather_beat(0)
    start_rows(1)
    layer.prepare(lengths, item_map, me)
    for beat in range(1, 3 * LAG + 2):
        gather_beat(beat)
    whole(0)
    rows_arrived(0)
    layer.small_lines()
    layer.norm_first()
    for beat in range(3 * LAG + 2, 3 * LAG + 5):
        gather_beat(beat)
    whole(*qkv_units)
    layer.project(0)
    layer.project(1)
    beat = 3 * LAG + 5
    pairs = HEADS // 2
    for low in range(0, pairs, 2):
        layer.attend(low, low + 2)
        gather_beat(beat)
        beat += 1
    whole(out_unit)
    layer.merge()
    layer.norm_second()
    while beat < 3 * LAG + up_units[-1] + 2:
        gather_beat(beat)
        beat += 1
    whole(*up_units)
    for z in range(depth):
        layer.activate(z)
        if z % 2 and beat < count + 3 * LAG:
            gather_beat(beat)
            beat += 1
    rows_arrived(1)
    for index, unit in enumerate(down_units):
        layer.grad_down(index)
        offer(unit)
        if index % 2 and beat < count + 3 * LAG:
            gather_beat(beat)
            beat += 1
    while beat < count + 3 * LAG:
        gather_beat(beat)
        beat += 1
    layer.bias_down()
    scatter_beat()
    for index, unit in enumerate(down_units):
        whole(unit)
    for index in range(sizes.n_ff):
        layer.back_active(index)
        if index % 2:
            scatter_beat()
    layer.finish()
    start_rows(2)
    for unit in down_units:
        arriving[unit].sent()
    pl.semaphore_signal(free, inc=1, device_id=place.sibling(), device_id_type=MESH)
    for z in range(depth):
        layer.grad_up(z)
    pl.semaphore_wait(free, 1)
    for unit in up_units:
        offer(unit)
    scatter_beat()
    layer.back_up()
    layer.norm_second_back()
    scatter_beat()
    for unit in up_units:
        arriving[unit].sent()
    layer.grad_out()
    offer(out_unit)
    layer.back_out()
    scatter_beat()
    for low in range(0, pairs, 2):
        layer.attend_back(low, low + 1)
        scatter_beat()
        layer.attend_back(low + 1, low + 2)
        if low:
            scatter_beat()
    for i in range(depth // 2):
        layer.grad_qkv(i)
    for unit in qkv_units:
        offer(unit)
    scatter_beat()
    layer.back_qkv()
    layer.norm_first_back()
    start_rows(3)
    layer.grad_small()
    offer(0)
    while len(done) < count:
        scatter_beat()
    for unit in [0, *qkv_units, out_unit]:
        arriving[unit].sent()
    for unit in leaving:
        unit.sent()
    for slot in range(5):
        for core in range(2):

            @on_core(place, core)
            def _():
                for copy in end_copies(core, slot):
                    copy.wait_send()
                for copy in end_copies(1 - core, slot):
                    copy.wait_recv()

    for core in range(2):

        @on_core(place, core)
        def _():
            for copy in raw_copies(core):
                copy.wait_send()

    rows_sent(0)
    rows_sent(1)
    for which in (2, 3):
        rows_arrived(which)
        rows_sent(which)


def write_kernel(
    sizes, end_small, end_qkv, end_out, end_up, end_down, result, input_grad, steps,
    o_table, o_qkv, o_out, o_up, o_down, o_result, o_input, o_lines, sems,
):
    copies = [
        pltpu.make_async_copy(source, target, sems.at[i])
        for i, (source, target) in enumerate(
            (
                (end_qkv, o_qkv), (end_out, o_out), (end_up, o_up), (end_down, o_down),
                (result, o_result), (input_grad, o_input),
            )
        )
    ]
    for copy in copies:
        copy.start()
    hot = (steps[...] == iota((sizes.items, o_table.shape[1]), 1)).astype(BF16)
    o_table[...] = dot(end_small[:, 0 : sizes.items].astype(BF16), hot, 1, 0)
    own = sizes.own
    eye = (iota((own, own), 0) == iota((own, own), 1)).astype(F32)
    lines = lax.dot_general(
        end_small[:, sizes.small :], eye, (((0,), (0,)), ((), ())), precision=lax.Precision.HIGHEST, preferred_element_type=F32
    )
    o_lines[...] = lines[0 : o_lines.shape[0]]
    for copy in copies:
        copy.wait()


def row_by_row(
    inputs, time_table, w_qkv, w_out, w_up, w_down, norm_gains, norm_shifts, biases, up_bias,
    timesteps, item_map, lengths, cotangent,
):
    groups = lax.axis_size("seq")
    local, width = inputs.shape[1], inputs.shape[2]
    length = local * groups
    ff, items = w_down.shape[0], timesteps.shape[0]
    depth = lax.axis_size("dp") // 2
    sizes = Sizes(width, ff, lax.axis_size("dp") * groups, depth, items)
    half, rows, small, per = sizes.half, sizes.rows, sizes.small, sizes.n_ff

    vectors = jnp.concatenate((norm_gains, norm_shifts, biases, up_bias.reshape(per, -1)), axis=0)
    vectors = jnp.pad(vectors, ((0, 16 - vectors.shape[0]), (0, 0)))
    steps = timesteps.reshape(items, 1)
    shapes = sizes.weights()
    own_shapes = sizes.own_shapes()
    final_shapes = [(rows, small), (rows * 3, half), (rows, half), (rows * per, half), (rows, ff // 2)]
    row_shape = (groups, local, width)
    unit_sems = pltpu.SemaphoreType.DMA((sizes.units, depth + 2))
    smem = pl.BlockSpec(memory_space=pltpu.SMEM)
    scratch = (
        [pltpu.VMEM(shape, BF16) for shape in shapes]
        + [pltpu.VMEM(shapes[slot], BF16) for slot in (0, 3, 4)]
        + [pltpu.VMEM(shape, F32) for shape in own_shapes]
        + [pltpu.VMEM((r, c // 2), F32) for r, c in own_shapes]
        + [pltpu.VMEM(shape, F32) for shape in final_shapes]
        + [
            pltpu.VMEM((*sizes.chips, rows, small), BF16),
            pltpu.VMEM((per, *sizes.chips, rows, half), BF16),
            pltpu.VMEM((*sizes.chips, rows, small), BF16),
            pltpu.VMEM((sizes.units - 1, *sizes.chips, rows, half), BF16),
            pltpu.VMEM(row_shape, BF16),
            pltpu.VMEM(row_shape, BF16),
        ]
        + [
            pltpu.VMEM((length, width), F32),
            pltpu.VMEM((length, width), BF16),
            pltpu.VMEM((length, 3 * width), BF16),
            pltpu.VMEM((length, width), BF16),
            pltpu.VMEM((length, 2 * HEAD_DIM), F32),
            pltpu.VMEM((length, width), F32),
            pltpu.VMEM((length, width), BF16),
            pltpu.VMEM((length, ff), BF16),
            pltpu.VMEM((length, ff), BF16),
            pltpu.VMEM(row_shape, BF16),
            pltpu.VMEM((length, width), F32),
            pltpu.VMEM((length, width), BF16),
            pltpu.VMEM((length, length), F32),
            pltpu.VMEM((length, small), BF16),
            pltpu.VMEM((16, width), F32),
            pltpu.VMEM((1, 3 * width), F32),
            pltpu.VMEM((1, ff), F32),
            pltpu.VMEM((width // per, width), BF16),
            pltpu.VMEM((16, width), F32),
            pltpu.VMEM((1, ff), F32),
        ]
        + [unit_sems] * 4
        + [pltpu.SemaphoreType.DMA((5, per))] * 2
        + [pltpu.SemaphoreType.DMA((4, groups - 1))] * 2
        + [pltpu.SemaphoreType.DMA((4,))]
        + [pltpu.SemaphoreType.DMA((5, per))] * 2
        + [pltpu.SemaphoreType.REGULAR]
    )
    row_type = jax.ShapeDtypeStruct(row_shape, BF16)
    landed = pl.pallas_call(
        functools.partial(layer_kernel, sizes),
        out_shape=tuple(jax.ShapeDtypeStruct(shape, F32) for shape in own_shapes) + (row_type, row_type),
        in_specs=[ANY, ANY] + [VMEM] * 7 + [smem] * 2,
        out_specs=(VMEM,) * 5 + (ANY, ANY),
        scratch_shapes=scratch,
        compiler_params=pltpu.CompilerParams(collective_id=0, has_side_effects=True, vmem_limit_bytes=VMEM_LIMIT),
    )(inputs, cotangent, time_table.T, w_qkv.T, w_out.T, w_up.T, w_down.T, vectors, steps, lengths, item_map)
    steps_count = time_table.shape[0]
    own_types = [jax.ShapeDtypeStruct(shape, F32) for shape in own_shapes[1:]]
    line_count = 8 + per
    written = pl.pallas_call(
        functools.partial(write_kernel, sizes),
        out_shape=(
            jax.ShapeDtypeStruct((sizes.own, steps_count), F32),
            *own_types,
            row_type,
            row_type,
            jax.ShapeDtypeStruct((line_count, sizes.own), F32),
        ),
        in_specs=[VMEM] + [ANY] * 6 + [VMEM],
        out_specs=(VMEM,) + (ANY,) * 6 + (VMEM,),
        scratch_shapes=[pltpu.SemaphoreType.DMA((6,))],
    )(*landed, steps)
    table, qkv, out, up, down, result, input_grad, lines = written
    return (
        result,
        input_grad,
        table.T,
        qkv.T,
        out.T,
        up.T,
        down.T,
        lines[0:2],
        lines[2:4],
        lines[4:8],
        lines[8:].reshape(1, -1),
    )


def on_device(*arrays):
    inputs, w_out, w_down, timesteps = arrays[0], arrays[3], arrays[5], arrays[10]
    width, ff = inputs.shape[2], w_down.shape[0]
    own = w_out.shape[1]
    fits = (
        lax.axis_size("seq") == 4
        and inputs.shape[0] == 4
        and lax.axis_size("dp") % 4 == 0
        and own % 8 == 0
        and ff % width == 0
        and width % 256 == 0
        and timesteps.shape[0] <= 128
    )
    return row_by_row(*arrays) if fits else spread_out(*arrays)


def solution(mesh):
    return jax.shard_map(
        on_device,
        mesh=mesh,
        in_specs=(
            P(None, ("dp", "seq"), None),
            P(None, ("dp", "seq")),
            P(None, ("dp", "seq")),
            P(None, ("dp", "seq")),
            P(None, ("dp", "seq")),
            P(None, ("dp", "seq")),
            P(None, ("dp", "seq")),
            P(None, ("dp", "seq")),
            P(None, ("dp", "seq")),
            P(None, ("dp", "seq")),
            P(),
            P("dp"),
            P("dp", None),
            P(None, ("dp", "seq"), None),
        ),
        out_specs=(
            P(None, ("dp", "seq"), None),
            P(None, ("dp", "seq"), None),
            P(None, ("dp", "seq")),
            P(None, ("dp", "seq")),
            P(None, ("dp", "seq")),
            P(None, ("dp", "seq")),
            P(None, ("dp", "seq")),
            P(None, ("dp", "seq")),
            P(None, ("dp", "seq")),
            P(None, ("dp", "seq")),
            P(None, ("dp", "seq")),
        ),
        check_vma=False,
    )
```

```python
import functools

import jax
import jax.numpy as jnp
from jax import lax
from jax.experimental import pallas as pl
from jax.experimental.pallas import tpu as pltpu
from jax.sharding import PartitionSpec as P

HEADS = 12
HEAD_DIM = 64


EPS = 1e-05


def norm_rows(field, gain, offset):
    mean = jnp.mean(field, axis=-1, keepdims=True)
    centred = field - mean
    spread = jnp.mean(centred * centred, axis=-1, keepdims=True)
    return centred * lax.rsqrt(spread + EPS) * gain + offset


def gelu_exact(field):
    return jax.nn.gelu(field, approximate=False)


def scores_block(query_part, keys, query_segment, key_segment, scale):
    raw = scale * jnp.einsum("qhd,khd->hqk", query_part, keys, preferred_element_type=jnp.float32)
    keep = query_segment[None, :, None] == key_segment[None, None, :]
    return jnp.where(keep, raw, -1e30)


def attend_forward(queries, keys, values, segment, scale):
    score = scores_block(queries, keys, segment, segment, scale)
    top = jnp.max(score, axis=-1, keepdims=True)
    expo = jnp.exp(score - top)
    denom = jnp.sum(expo, axis=-1, keepdims=True)
    probs = (expo / denom).astype(jnp.bfloat16)
    results = jnp.einsum("hqk,khd->qhd", probs, values, preferred_element_type=jnp.float32).astype(
        jnp.bfloat16
    )
    log_totals = [top + jnp.log(denom)]
    return (results, log_totals)


def attend_backward(queries, keys, values, segment, log_totals, grad_out, scale):
    length = queries.shape[0]
    block = min(512, length)
    grad_keys = jnp.zeros(keys.shape, jnp.float32)
    grad_values = jnp.zeros(values.shape, jnp.float32)
    grad_queries = []
    for index, begin in enumerate(range(0, length, block)):
        score = scores_block(queries, keys, segment, segment, scale)
        probs = jnp.exp(score - log_totals[index])
        grad_values = jnp.einsum(
            "hqk,qhd->khd", probs.astype(jnp.bfloat16), grad_out, preferred_element_type=jnp.float32
        )
        grad_probs = jnp.einsum(
            "qhd,khd->hqk", grad_out, values, preferred_element_type=jnp.float32
        )
        centre = jnp.sum(probs * grad_probs, axis=-1, keepdims=True)
        grad_score = (probs * (grad_probs - centre)).astype(jnp.bfloat16)
        grad_queries.append(
            (
                scale
                * jnp.einsum("hqk,khd->qhd", grad_score, keys, preferred_element_type=jnp.float32)
            ).astype(jnp.bfloat16)
        )
        grad_keys = scale * jnp.einsum(
            "hqk,qhd->khd", grad_score, queries, preferred_element_type=jnp.float32
        )
    return (grad_queries[0], grad_keys.astype(jnp.bfloat16), grad_values.astype(jnp.bfloat16))


def spread_out(
    inputs,
    time_table,
    w_qkv,
    w_out,
    w_up,
    w_down,
    norm_gains,
    norm_shifts,
    biases,
    up_bias,
    timesteps,
    item_map,
    lengths,
    cotangent,
):
    micro = inputs.shape[0]
    local = inputs.shape[1]
    width = inputs.shape[2]
    groups = lax.axis_size("seq")
    data_count = lax.axis_size("dp")
    seq_len = local * groups
    items_row = lengths.shape[1]
    heads_dev = HEADS // groups
    group_width = width // groups
    scale = HEAD_DIM ** (-0.5)
    my_start = lax.axis_index("seq") * local
    places = jnp.arange(seq_len, dtype=jnp.int32)
    slot_index = jnp.arange(items_row, dtype=jnp.int32)
    step_index = jnp.arange(time_table.shape[0], dtype=jnp.int32)
    totals = None
    results = []
    input_grads = []
    for index in range(micro):
        gathered = (
            lax.all_gather(time_table, ("dp", "seq"), axis=1, tiled=True),
            lax.all_gather(w_qkv, ("dp", "seq"), axis=1, tiled=True),
            lax.all_gather(w_out, ("dp", "seq"), axis=1, tiled=True),
            lax.all_gather(w_up, ("dp", "seq"), axis=1, tiled=True),
            lax.all_gather(w_down, ("dp", "seq"), axis=1, tiled=True),
            lax.all_gather(norm_gains, ("dp", "seq"), axis=1, tiled=True),
            lax.all_gather(norm_shifts, ("dp", "seq"), axis=1, tiled=True),
            lax.all_gather(biases, ("dp", "seq"), axis=1, tiled=True),
            lax.all_gather(up_bias, ("dp", "seq"), axis=1, tiled=True),
        )
        (
            full_table,
            full_qkv,
            full_out,
            full_up,
            full_down,
            full_gains,
            full_shifts,
            full_biases,
            full_up_bias,
        ) = gathered
        gains = full_gains.astype(jnp.float32)
        offsets = full_shifts.astype(jnp.float32)
        bias_rows = full_biases.astype(jnp.float32)
        up_row = full_up_bias.astype(jnp.float32)[0]
        if totals is None:
            totals = [jnp.zeros(a.shape, jnp.float32) for a in gathered]
        ends = jnp.cumsum(lengths[index])
        segment = jnp.sum((ends[None, :] <= places[:, None]).astype(jnp.int32), axis=1)
        my_segment = lax.dynamic_slice_in_dim(segment, my_start, local)
        slot_steps = jnp.take(timesteps, item_map[index * items_row : (index + 1) * items_row])
        token_slot = (my_segment[:, None] == slot_index[None, :]).astype(jnp.bfloat16)
        step_hot = (slot_steps[:, None] == step_index[None, :]).astype(jnp.bfloat16)
        slot_rows = jnp.dot(step_hot, full_table, preferred_element_type=jnp.float32).astype(
            jnp.bfloat16
        )
        embedded = inputs[index].astype(jnp.float32) + jnp.dot(
            token_slot, slot_rows, preferred_element_type=jnp.float32
        )
        first_normed = norm_rows(embedded, gains[0], offsets[0]).astype(jnp.bfloat16)
        projected = jnp.dot(first_normed, full_qkv, preferred_element_type=jnp.float32)
        queries = (projected[:, 0:width] + bias_rows[0]).astype(jnp.bfloat16)
        keys = projected[:, width : 2 * width].astype(jnp.bfloat16)
        values = (projected[:, 2 * width : 3 * width] + bias_rows[1]).astype(jnp.bfloat16)
        head_queries, head_keys, head_values = (
            lax.all_to_all(
                queries.reshape(local, groups, group_width),
                "seq",
                split_axis=1,
                concat_axis=0,
                tiled=True,
            ),
            lax.all_to_all(
                keys.reshape(local, groups, group_width),
                "seq",
                split_axis=1,
                concat_axis=0,
                tiled=True,
            ),
            lax.all_to_all(
                values.reshape(local, groups, group_width),
                "seq",
                split_axis=1,
                concat_axis=0,
                tiled=True,
            ),
        )
        head_queries = head_queries.reshape(seq_len, heads_dev, HEAD_DIM)
        head_keys = head_keys.reshape(seq_len, heads_dev, HEAD_DIM)
        head_values = head_values.reshape(seq_len, heads_dev, HEAD_DIM)
        head_out, log_totals = attend_forward(head_queries, head_keys, head_values, segment, scale)
        attended = lax.all_to_all(
            head_out.reshape(seq_len, 1, group_width),
            "seq",
            split_axis=0,
            concat_axis=1,
            tiled=True,
        ).reshape(local, width)
        mid = (
            embedded
            + jnp.dot(attended, full_out, preferred_element_type=jnp.float32)
            + bias_rows[2]
        )
        second_normed = norm_rows(mid, gains[1], offsets[1]).astype(jnp.bfloat16)
        inner = jnp.dot(second_normed, full_up, preferred_element_type=jnp.float32) + up_row
        activated = gelu_exact(inner).astype(jnp.bfloat16)
        results.append(
            (
                mid
                + jnp.dot(activated, full_down, preferred_element_type=jnp.float32)
                + bias_rows[3]
            ).astype(jnp.bfloat16)
        )
        grad_output = cotangent[index]
        grad_down = jnp.einsum(
            "tf,td->fd", activated, grad_output, preferred_element_type=jnp.float32
        )
        bias_down = jnp.sum(grad_output.astype(jnp.float32), axis=0)
        grad_act = jnp.einsum(
            "td,fd->tf", grad_output, full_down, preferred_element_type=jnp.float32
        )
        unused, gelu_pull = jax.vjp(gelu_exact, inner)
        grad_inner = gelu_pull(grad_act)[0].astype(jnp.bfloat16)
        grad_up = jnp.einsum(
            "td,tf->df", second_normed, grad_inner, preferred_element_type=jnp.float32
        )
        grad_up_bias = jnp.sum(grad_inner.astype(jnp.float32), axis=0)
        upstream = jnp.einsum("tf,df->td", grad_inner, full_up, preferred_element_type=jnp.float32)
        unused, norm_pull = jax.vjp(norm_rows, mid, gains[1], offsets[1])
        back_mid, gain_second, shift_second = norm_pull(upstream)
        grad_mid = grad_output.astype(jnp.float32) + back_mid
        grad_branch = grad_mid.astype(jnp.bfloat16)
        grad_out_weight = jnp.einsum(
            "te,td->ed", attended, grad_branch, preferred_element_type=jnp.float32
        )
        bias_attend = jnp.sum(grad_branch.astype(jnp.float32), axis=0)
        grad_attended = jnp.einsum(
            "td,ed->te", grad_branch, full_out, preferred_element_type=jnp.float32
        ).astype(jnp.bfloat16)
        head_grad = lax.all_to_all(
            grad_attended.reshape(local, groups, group_width),
            "seq",
            split_axis=1,
            concat_axis=0,
            tiled=True,
        ).reshape(seq_len, heads_dev, HEAD_DIM)
        grad_q_heads, grad_k_heads, grad_v_heads = attend_backward(
            head_queries, head_keys, head_values, segment, log_totals, head_grad, scale
        )
        grad_queries, grad_keys, grad_values = (
            lax.all_to_all(
                grad_q_heads.reshape(seq_len, 1, group_width),
                "seq",
                split_axis=0,
                concat_axis=1,
                tiled=True,
            ),
            lax.all_to_all(
                grad_k_heads.reshape(seq_len, 1, group_width),
                "seq",
                split_axis=0,
                concat_axis=1,
                tiled=True,
            ),
            lax.all_to_all(
                grad_v_heads.reshape(seq_len, 1, group_width),
                "seq",
                split_axis=0,
                concat_axis=1,
                tiled=True,
            ),
        )
        grad_projected = jnp.concatenate(
            (
                grad_queries.reshape(local, width),
                grad_keys.reshape(local, width),
                grad_values.reshape(local, width),
            ),
            axis=1,
        )
        grad_qkv = jnp.einsum(
            "td,tc->dc", first_normed, grad_projected, preferred_element_type=jnp.float32
        )
        bias_query = jnp.sum(grad_queries.reshape(local, width).astype(jnp.float32), axis=0)
        bias_value = jnp.sum(grad_values.reshape(local, width).astype(jnp.float32), axis=0)
        upstream_first = jnp.einsum(
            "tc,dc->td", grad_projected, full_qkv, preferred_element_type=jnp.float32
        )
        unused, first_pull = jax.vjp(norm_rows, embedded, gains[0], offsets[0])
        back_first, gain_first, shift_first = first_pull(upstream_first)
        grad_embedded = grad_mid + back_first
        input_grads.append(grad_embedded.astype(jnp.bfloat16))
        slot_sums = jnp.einsum(
            "ts,td->sd",
            token_slot.astype(jnp.float32),
            grad_embedded,
            precision=lax.Precision.HIGHEST,
        )
        grad_table = jnp.einsum(
            "si,sd->id", step_hot.astype(jnp.float32), slot_sums, precision=lax.Precision.HIGHEST
        )
        grad_gains = jnp.stack((gain_first, gain_second), axis=0)
        grad_shifts = jnp.stack((shift_first, shift_second), axis=0)
        grad_biases = jnp.stack((bias_query, bias_value, bias_attend, bias_down), axis=0)
        grad_up_row = grad_up_bias[None, :]
        fresh = (
            grad_table,
            grad_qkv,
            grad_out_weight,
            grad_up,
            grad_down,
            grad_gains,
            grad_shifts,
            grad_biases,
            grad_up_row,
        )
        totals = [a + b for a, b in zip(totals, fresh)]

    def spread(grad):
        return grad.reshape(
            grad.shape[0], data_count, groups, grad.shape[1] // (data_count * groups)
        )

    parts = [spread(a) for a in totals]
    folded = (
        lax.all_to_all(
            parts[0].astype(jnp.bfloat16), "seq", split_axis=2, concat_axis=2, tiled=True
        ).astype(jnp.float32),
        lax.all_to_all(
            parts[1].astype(jnp.bfloat16), "seq", split_axis=2, concat_axis=2, tiled=True
        ).astype(jnp.float32),
        lax.all_to_all(
            parts[2].astype(jnp.bfloat16), "seq", split_axis=2, concat_axis=2, tiled=True
        ).astype(jnp.float32),
        lax.all_to_all(
            parts[3].astype(jnp.bfloat16), "seq", split_axis=2, concat_axis=2, tiled=True
        ).astype(jnp.float32),
        lax.all_to_all(
            parts[4].astype(jnp.bfloat16), "seq", split_axis=2, concat_axis=2, tiled=True
        ).astype(jnp.float32),
        lax.all_to_all(
            parts[5].astype(jnp.bfloat16), "seq", split_axis=2, concat_axis=2, tiled=True
        ).astype(jnp.float32),
        lax.all_to_all(
            parts[6].astype(jnp.bfloat16), "seq", split_axis=2, concat_axis=2, tiled=True
        ).astype(jnp.float32),
        lax.all_to_all(
            parts[7].astype(jnp.bfloat16), "seq", split_axis=2, concat_axis=2, tiled=True
        ).astype(jnp.float32),
        lax.all_to_all(
            parts[8].astype(jnp.bfloat16), "seq", split_axis=2, concat_axis=2, tiled=True
        ).astype(jnp.float32),
    )
    merged = [jnp.sum(f, axis=2, keepdims=True) for f in folded]
    owners = (
        lax.psum_scatter(merged[0], "dp", scatter_dimension=1, tiled=True),
        lax.psum_scatter(merged[1], "dp", scatter_dimension=1, tiled=True),
        lax.psum_scatter(merged[2], "dp", scatter_dimension=1, tiled=True),
        lax.psum_scatter(merged[3], "dp", scatter_dimension=1, tiled=True),
        lax.psum_scatter(merged[4], "dp", scatter_dimension=1, tiled=True),
        lax.psum_scatter(merged[5], "dp", scatter_dimension=1, tiled=True),
        lax.psum_scatter(merged[6], "dp", scatter_dimension=1, tiled=True),
        lax.psum_scatter(merged[7], "dp", scatter_dimension=1, tiled=True),
        lax.psum_scatter(merged[8], "dp", scatter_dimension=1, tiled=True),
    )
    owned = [o.reshape(o.shape[0], o.shape[3]) for o in owners]
    return (
        jnp.stack(results, axis=0),
        jnp.stack(input_grads, axis=0),
        owned[0],
        owned[1],
        owned[2],
        owned[3],
        owned[4],
        owned[5],
        owned[6],
        owned[7],
        owned[8],
    )


F32 = jnp.float32
BF16 = jnp.bfloat16
MESH = pl.DeviceIdType.MESH
VMEM_LIMIT = 63 << 20
VMEM = pl.BlockSpec(memory_space=pltpu.VMEM)
ANY = pl.BlockSpec(memory_space=pl.ANY)
ALL = slice(None)
KINDS = (("zy",), ("zy", "zx", "yz"))


class Place:
    def __init__(self):
        row, column = lax.axis_index("dp"), lax.axis_index("seq")
        self.at = {"z": row // 2, "y": row % 2, "x": column // 2}
        self.core = column % 2
        self.column = column
        self.depth = lax.axis_size("dp") // 2

    def device(self, core=None, **moved):
        at = {**self.at, **moved}
        core = self.core if core is None else core
        return (at["z"] * 2 + at["y"], at["x"] * 2 + core)

    def other(self, axis):
        return 1 - self.at[axis]

    def around(self, step):
        return (self.at["z"] + step) % self.depth

    def sibling(self):
        return self.device(core=1 - self.core)

    def partners(self):
        found = [self.sibling(), self.device(x=self.other("x")), self.device(y=self.other("y"))]
        found.append(self.device(core=1 - self.core, x=self.other("x")))
        found += [self.device(z=self.around(step)) for step in range(1, self.depth)]
        return found


def meet(place):
    barrier = pltpu.get_barrier_semaphore()
    partners = place.partners()
    for partner in partners:
        pl.semaphore_signal(barrier, inc=1, device_id=partner, device_id_type=MESH)
    pl.semaphore_wait(barrier, len(partners))


def remote(source, target, send, receive, device):
    return pltpu.make_async_remote_copy(
        src_ref=source,
        dst_ref=target,
        send_sem=send,
        recv_sem=receive,
        device_id=device,
        device_id_type=MESH,
    )


def on_core(place, core):
    return pl.when(place.core == core)


class Route:
    def __init__(self, place, unit, view, send, receive):
        self.place, self.unit, self.view = place, unit, view
        self.send, self.receive = send, receive

    def kind(self, core):
        found = KINDS[core][self.unit % len(KINDS[core])]
        z_first = found[0] == "z"
        late = found[1] if z_first else found[0]
        return z_first, late, "x" if late == "y" else "y"

    def part(self, core, **moved):
        at = {**self.place.at, **moved}
        return self.view(at["z"], at["y"], at["x"], core)

    def copy(self, slot, source, target, device):
        return remote(source, target, self.send.at[self.unit, slot], self.receive.at[self.unit, slot], device)

    def over(self, axis):
        return self.place.device(**{axis: self.place.other(axis)})

    def on_each_core(self, act):
        for core in range(2):

            @on_core(self.place, core)
            def _():
                act(core)


class Gather(Route):
    def copies(self, core, name):
        place, depth = self.place, self.place.depth
        z_first, late, early = self.kind(core)
        spread = ALL if z_first else place.at["z"]
        if name == "z":
            block = self.part(core) if z_first else self.part(core, x=ALL, y=ALL)
            return [
                self.copy(step - 1, block, block, place.device(z=place.around(step))) for step in range(1, depth)
            ]
        if name == "sibling":
            block = self.part(core, z=ALL, y=ALL, x=ALL)
            return [self.copy(depth + 2, block, block, place.sibling())]
        moved = {early: place.other(early)} if name == "diagonal" else {}
        block = self.part(core, z=spread, **moved)
        slot = {"late": depth - 1, "early": depth, "diagonal": depth + 1}[name]
        return [self.copy(slot, block, block, self.over(early if name == "early" else late))]

    def stages(self, core):
        if self.kind(core)[0]:
            return [((), ("z",)), (("z",), ("early", "late")), (("early",), ("diagonal",)), (("late", "diagonal"), ("sibling",))]
        return [((), ("early", "late")), (("early",), ("diagonal",)), (("late", "diagonal"), ("z",)), (("z",), ("sibling",))]

    def step(self, stage):
        def act(core):
            waits, starts = self.stages(core)[stage]
            for name in waits:
                for copy in self.copies(core, name):
                    copy.wait_recv()
            for name in starts:
                for copy in self.copies(core, name):
                    copy.start()

        self.on_each_core(act)

    def sibling_arrived(self):
        self.on_each_core(lambda core: self.copies(1 - core, "sibling")[0].wait_recv())

    def sent(self):
        def act(core):
            for name in ("z", "late", "early", "diagonal", "sibling"):
                for copy in self.copies(core, name):
                    copy.wait_send()

        self.on_each_core(act)


class Scatter(Route):
    def __init__(self, place, unit, view, first, landings, send, receive):
        super().__init__(place, unit, view, send, receive)
        self.first, self.landings = first, landings

    def sibling_copy(self, core):
        theirs = self.part(1 - core, z=ALL, y=ALL, x=ALL)
        return self.copy(self.place.depth + 2, theirs, self.first, self.place.sibling())

    def target(self, core, name):
        z_first, late, early = self.kind(core)
        if name == "z" and not z_first:
            return self.part(core, x=ALL, y=ALL)
        moved = {early: self.place.other(early)} if name == "diagonal" else {}
        if name != "z" and z_first:
            moved["z"] = ALL
        return self.part(core, **moved)

    def copies(self, core, name):
        place, depth = self.place, self.place.depth
        z_first, late, early = self.kind(core)
        z_land, diagonal, direct, near = self.landings(z_first)
        if name == "z":
            found = []
            rest = {} if z_first else {"x": ALL, "y": ALL}
            for step in range(1, depth):
                gone = self.part(core, z=place.around(step), **rest)
                landing = z_land.at[step - 1]
                found.append((self.copy(step - 1, gone, landing, place.device(z=place.around(step))), landing))
            return found
        moved = {"z": ALL} if z_first else {}
        if name != "near":
            moved[late] = place.other(late)
        if name != "direct":
            moved[early] = place.other(early)
        slot, landing = {
            "direct": (depth - 1, direct), "near": (depth, near), "diagonal": (depth + 1, diagonal)
        }[name]
        gone = self.part(core, **moved)
        return [(self.copy(slot, gone, landing, self.over(early if name == "near" else late)), landing)]

    def stages(self, core):
        if self.kind(core)[0]:
            return [((), ("diagonal", "direct")), (("diagonal",), ("near",)), (("near", "direct"), ("z",)), (("z",), ())]
        return [((), ("z",)), (("z",), ("diagonal", "direct")), (("diagonal",), ("near",)), (("near", "direct"), ())]

    def start_sibling(self):
        self.on_each_core(lambda core: self.sibling_copy(core).start())

    def step(self, stage, result):
        def act(core):
            waits, starts = self.stages(core)[stage]
            if stage == 0:
                self.sibling_copy(core).wait_recv()
                mine = self.part(core, z=ALL, y=ALL, x=ALL)
                mine[...] = (mine[...].astype(F32) + self.first[...].astype(F32)).astype(BF16)
            if waits:
                target = self.target(core, waits[0])
                total = target[...].astype(F32)
                for name in waits:
                    for copy, landing in self.copies(core, name):
                        copy.wait_recv()
                        total = total + landing[...].astype(F32)
                if stage == 3:
                    result(core)[...] = total
                else:
                    target[...] = total.astype(BF16)
            for name in starts:
                for copy, _ in self.copies(core, name):
                    copy.start()

        self.on_each_core(act)

    def sent(self):
        def act(core):
            self.sibling_copy(core).wait_send()
            for name in ("z", "direct", "near", "diagonal"):
                for copy, _ in self.copies(core, name):
                    copy.wait_send()

        self.on_each_core(act)


class Sizes:
    def __init__(self, width, ff, devices, depth, items):
        self.width, self.ff, self.devices, self.depth, self.items = width, ff, devices, depth, items
        self.half = width // 2
        self.own = width // devices
        self.rows = 2 * self.own
        self.n_qkv, self.n_ff = 3, ff // width
        self.small = 128
        self.units = 1 + self.n_qkv + 1 + 2 * self.n_ff
        self.chips = (depth, 2, 2)

    def weights(self):
        return [
            (*self.chips, self.rows, 2 * self.small),
            (*self.chips, self.n_qkv, self.rows, self.width),
            (*self.chips, self.rows, self.width),
            (*self.chips, self.n_ff, self.rows, self.width),
            (*self.chips, self.rows, self.ff),
        ]

    def own_shapes(self):
        widths = [2 * self.small, self.width, self.width, self.width, self.ff]
        return [(self.own * n, w) for n, w in zip((1, self.n_qkv, 1, self.n_ff, 1), widths)]

    def views(self, refs):
        small, qkv, out, up, down = refs
        half = self.half

        def columns(core, base=0, width=half):
            return pl.ds(base + core * width, width)

        found = [lambda z, y, x, core: small.at[z, y, x, :, columns(core, 0, self.small)]]
        for unit in range(self.n_qkv):
            found.append(lambda z, y, x, core, unit=unit: qkv.at[z, y, x, unit, :, columns(core)])
        found.append(out if callable(out) else lambda z, y, x, core: out.at[z, y, x, :, columns(core)])
        for unit in range(self.n_ff):
            found.append(lambda z, y, x, core, unit=unit: up.at[z, y, x, unit, :, columns(core)])
        for unit in range(self.n_ff):
            found.append(lambda z, y, x, core, unit=unit: down.at[z, y, x, :, columns(core, unit * self.width)])
        return found


def dot(a, b, ca, cb):
    return lax.dot_general(a, b, (((ca,), (cb,)), ((), ())), preferred_element_type=F32)


def iota(shape, axis):
    return lax.broadcasted_iota(jnp.int32, shape, axis)


def normalized(field):
    mean = jnp.mean(field, axis=-1, keepdims=True)
    centred = field - mean
    spread = jnp.mean(centred * centred, axis=-1, keepdims=True)
    rs = lax.rsqrt(spread + EPS)
    return centred * rs, rs


def loop(count, body):
    lax.fori_loop(0, count, lambda i, c: (body(i), c)[1], 0)


def span(i, size):
    return pl.ds(pl.multiple_of(i * size, size), size)


def flat(block, columns):
    return block.reshape(-1, columns)


TILE = 128


class Layer:
    def __init__(self, sizes, weights, grads, row_x, row_cot, scratch):
        self.s = sizes
        self.small, self.qkv_w, self.out_w, self.up_w, self.down_w = weights
        self.g_small, self.g_qkv, self.g_out, self.g_up, self.g_down = grads
        self.row_x, self.row_cot = row_x, row_cot
        (
            self.embedded, self.first, self.qkv, self.attended, self.log_total, self.mid, self.second,
            self.active, self.slope, self.result, self.total, self.branch, self.bias, self.token_hot,
            self.lines, self.qkv_bias, self.up_row, self.spread, self.grad_lines, self.up_sum,
        ) = scratch
        self.length = self.embedded.shape[0]


    def prepare(self, lengths, item_map, me):
        n, wide = self.length, self.s.small
        count = lengths.shape[1]
        ends = [lengths[me, 0]]
        for slot in range(1, count - 1):
            ends.append(ends[-1] + lengths[me, slot])
        items = [item_map[me * count + slot] for slot in range(count)]

        def segment(position):
            return sum((position >= end).astype(jnp.int32) for end in ends)

        columns = segment(iota((1, n), 1))

        def masks(i):
            rows = segment(iota((TILE, 1), 0) + i * TILE)
            self.bias[span(i, TILE), :] = jnp.where(rows == columns, 0.0, -1e30)
            item = jnp.full((TILE, 1), items[-1], jnp.int32)
            for slot in range(count - 1):
                item = jnp.where(rows == slot, items[slot], item)
            self.token_hot[span(i, TILE), :] = (item == iota((TILE, wide), 1)).astype(BF16)

        loop(n // TILE, masks)
        own, per = self.s.own, self.s.n_ff
        part = self.spread.shape[0]
        row, column = iota((part, 1), 0), iota((1, self.s.width), 1)
        same = (row // own == column // (per * own)) & (row % own == column % own)
        self.spread[...] = same.astype(BF16)

    def small_lines(self):
        s = self.s
        eye = (iota((16, s.small), 0) == iota((16, s.small), 1)).astype(BF16)
        lines = dot(eye, flat(self.small[:, :, :, :, s.small :], s.small), 1, 1)
        self.lines[...] = lines
        zero = jnp.zeros((1, s.width), F32)
        self.qkv_bias[...] = jnp.concatenate([lines[4:5], zero, lines[5:6]], axis=1)
        part = self.spread.shape[0]
        turn = (iota((1, s.width), 1) // s.own) % s.n_ff
        picked = turn == iota((s.n_ff, 1), 0)
        for tile in range(s.n_ff):
            seen = lines[8 : 8 + s.n_ff, tile * part : (tile + 1) * part].astype(BF16)
            moved = dot(seen, self.spread[...], 1, 0)
            self.up_row[:, tile * s.width : (tile + 1) * s.width] = jnp.sum(
                jnp.where(picked, moved, 0.0), axis=0, keepdims=True
            )
        self.grad_lines[...] = jnp.zeros_like(self.grad_lines)
        self.up_sum[...] = jnp.zeros_like(self.up_sum)

    def norm_first(self):
        gain, shift = self.lines[0:1, :], self.lines[2:3, :]
        items = flat(self.small[:, :, :, :, 0 : self.s.small], self.s.small)

        def body(i):
            field = self.row_x[i].astype(F32) + dot(self.token_hot[span(i, TILE), :], items, 1, 1)
            self.embedded[span(i, TILE), :] = field
            n, _ = normalized(field)
            self.first[span(i, TILE), :] = (n * gain + shift).astype(BF16)

        loop(self.length // TILE, body)

    def project(self, i):
        width = 2 * self.qkv_w.shape[1] * self.qkv_w.shape[2] * self.qkv_w.shape[3] * self.s.rows
        weight = flat(self.qkv_w[2 * i : 2 * i + 2], self.s.width)
        lanes = slice(i * width, (i + 1) * width)
        self.qkv[:, lanes] = (dot(self.first[...], weight, 1, 1) + self.qkv_bias[:, lanes]).astype(BF16)

    def heads(self, base, pair):
        return pl.ds(pl.multiple_of(base + pair * 2 * HEAD_DIM, 2 * HEAD_DIM), 2 * HEAD_DIM)

    def attend(self, low, high):
        width, block = self.s.width, 256
        lane = iota((1, 2 * HEAD_DIM), 1)
        mine = [lane < HEAD_DIM, lane >= HEAD_DIM]
        scale = HEAD_DIM ** (-0.5)

        def body(pair, carry):
            keys = self.qkv[:, self.heads(width, pair)]
            values = self.qkv[:, self.heads(2 * width, pair)]
            for part in range(self.length // block):
                rows = slice(part * block, (part + 1) * block)
                queries = self.qkv[rows, self.heads(0, pair)] * jnp.asarray(scale, BF16)
                logs = self.log_total[rows, :]
                found = []
                for head in range(2):
                    one = jnp.where(mine[head], queries, jnp.zeros_like(queries))
                    score = dot(one, keys, 1, 1) + self.bias[rows, :]
                    top = jnp.max(score, axis=-1, keepdims=True)
                    expo = jnp.exp(score - top)
                    denom = jnp.sum(expo, axis=-1, keepdims=True)
                    probs = (expo * (1.0 / denom)).astype(BF16)
                    found.append(dot(probs, values, 1, 0))
                    logs = jnp.where(lane == 2 * pair + head, top + jnp.log(denom), logs)
                self.log_total[rows, :] = logs
                self.attended[rows, self.heads(0, pair)] = jnp.where(mine[0], found[0], found[1]).astype(BF16)
            return carry

        lax.fori_loop(low, high, body, 0)

    def merge(self):
        width = self.s.width
        for i in range(2):
            weight = flat(self.out_w[2 * i : 2 * i + 2], width)
            lanes = slice(i * weight.shape[0], (i + 1) * weight.shape[0])
            self.mid[:, lanes] = self.embedded[:, lanes] + dot(self.attended[...], weight, 1, 1) + self.lines[6:7, lanes]

    def norm_second(self):
        gain, shift = self.lines[1:2, :], self.lines[3:4, :]

        def body(i):
            n, _ = normalized(self.mid[span(i, TILE), :])
            self.second[span(i, TILE), :] = (n * gain + shift).astype(BF16)

        loop(self.length // TILE, body)

    def activate(self, z):
        half = self.s.ff // (2 * self.s.depth)
        for y in range(2):
            lanes = slice((2 * z + y) * half, (2 * z + y + 1) * half)
            weight = flat(self.up_w[z, y], self.s.width)
            inner = dot(self.second[...], weight, 1, 1) + self.up_row[:, lanes]
            mass = 0.5 + 0.5 * lax.erf(inner * (0.5**0.5))
            self.active[:, lanes] = (inner * mass).astype(BF16)
            bell = jnp.exp(-0.5 * inner * inner) * 0.3989422804014327
            self.slope[:, lanes] = (mass + inner * bell).astype(BF16)

    def finish(self):
        width = self.s.width
        for i in range(2):
            weight = flat(self.down_w[2 * i : 2 * i + 2], self.s.ff)
            lanes = slice(i * weight.shape[0], (i + 1) * weight.shape[0])
            field = self.mid[:, lanes] + dot(self.active[...], weight, 1, 1) + self.lines[7:8, lanes]
            for part in range(self.length // TILE):
                self.result[part, :, lanes] = field[part * TILE : (part + 1) * TILE].astype(BF16)


    def cotangent(self):
        return flat(self.row_cot[...], self.s.width)

    def grad_down(self, unit):
        width = self.s.width
        lanes = slice(unit * width, (unit + 1) * width)
        grad = dot(self.cotangent(), self.active[:, lanes], 0, 0).astype(BF16)
        self.g_down[:, :, :, :, lanes] = grad.reshape(*self.s.chips, self.s.rows, width)

    def bias_down(self):
        self.grad_lines[7:8, :] = jnp.sum(self.cotangent().astype(F32), axis=0, keepdims=True)

    def back_active(self, unit):
        width = self.s.width
        for part in range(2):
            lanes = slice(unit * width + part * width // 2, unit * width + (part + 1) * width // 2)
            weight = flat(self.down_w[:, :, :, :, lanes], width // 2)
            grad = dot(self.cotangent(), weight, 1, 0)
            inner = (self.slope[:, lanes].astype(F32) * grad).astype(BF16)
            self.slope[:, lanes] = inner
            self.up_sum[:, lanes] = jnp.sum(inner.astype(F32), axis=0, keepdims=True)

    def grad_up(self, z):
        half = self.s.ff // (2 * self.s.depth)
        for y in range(2):
            lanes = slice((2 * z + y) * half, (2 * z + y + 1) * half)
            grad = dot(self.slope[:, lanes], self.second[...], 0, 0).astype(BF16)
            self.g_up[z, y] = grad.reshape(2, self.s.n_ff, self.s.rows, self.s.width)

    def back_up(self):
        half = self.s.half
        for part in range(2):
            lanes = slice(part * half, (part + 1) * half)
            weight = flat(self.up_w[:, :, :, :, :, lanes], half)
            self.total[:, lanes] = dot(self.slope[...], weight, 1, 0)

    def norm_second_back(self):
        gain = self.lines[1:2, :]
        zero = jnp.zeros((1, self.s.width), F32)

        def body(i, sums):
            upstream = self.total[span(i, TILE), :]
            n, rs = normalized(self.mid[span(i, TILE), :])
            u = upstream * gain
            back = rs * (u - jnp.mean(u, axis=-1, keepdims=True) - n * jnp.mean(u * n, axis=-1, keepdims=True))
            grad = self.row_cot[i].astype(F32) + back
            self.mid[span(i, TILE), :] = grad
            low = grad.astype(BF16)
            self.branch[span(i, TILE), :] = low
            fresh = (upstream * n, upstream, low.astype(F32))
            return tuple(a + jnp.sum(b, axis=0, keepdims=True) for a, b in zip(sums, fresh))

        sums = lax.fori_loop(0, self.length // TILE, body, (zero, zero, zero))
        self.grad_lines[1:2, :] = sums[0]
        self.grad_lines[3:4, :] = sums[1]
        self.grad_lines[6:7, :] = sums[2]

    def grad_out(self):
        grad = dot(self.branch[...], self.attended[...], 0, 0).astype(BF16)
        self.g_out[...] = grad.reshape(*self.s.chips, self.s.rows, self.s.width)

    def back_out(self):
        weight = flat(self.out_w[...], self.s.width)
        self.attended[...] = dot(self.branch[...], weight, 1, 0).astype(BF16)

    def attend_back(self, low, high):
        width, block = self.s.width, 256
        lane = iota((1, 2 * HEAD_DIM), 1)
        mine = [lane < HEAD_DIM, lane >= HEAD_DIM]
        scale = HEAD_DIM ** (-0.5)

        def body(pair, carry):
            queries = self.qkv[:, self.heads(0, pair)]
            keys = self.qkv[:, self.heads(width, pair)]
            values = self.qkv[:, self.heads(2 * width, pair)]
            grads = self.attended[:, self.heads(0, pair)]
            grad_keys, grad_values, grad_queries = [0.0, 0.0], [0.0, 0.0], []
            for part in range(self.length // block):
                rows = slice(part * block, (part + 1) * block)
                query, grad = queries[rows], grads[rows]
                scaled = query * jnp.asarray(scale, BF16)
                logs = self.log_total[rows, :]
                found = []
                for head in range(2):
                    one = jnp.where(mine[head], scaled, jnp.zeros_like(scaled))
                    own = jnp.where(mine[head], grad, jnp.zeros_like(grad))
                    log = jnp.sum(jnp.where(lane == 2 * pair + head, logs, 0.0), axis=-1, keepdims=True)
                    probs = jnp.exp(dot(one, keys, 1, 1) + self.bias[rows, :] - log)
                    grad_probs = dot(own, values, 1, 1)
                    centre = jnp.sum(probs * grad_probs, axis=-1, keepdims=True)
                    grad_score = (probs * (grad_probs - centre)).astype(BF16)
                    grad_values[head] += dot(probs.astype(BF16), grad, 0, 0)
                    grad_keys[head] += dot(grad_score, query, 0, 0)
                    found.append(dot(grad_score, keys, 1, 0))
                grad_queries.append(scale * jnp.where(mine[0], found[0], found[1]))
            for part, grad in enumerate(grad_queries):
                self.qkv[part * block : (part + 1) * block, self.heads(0, pair)] = grad.astype(BF16)
            self.qkv[:, self.heads(width, pair)] = (scale * jnp.where(mine[0], grad_keys[0], grad_keys[1])).astype(BF16)
            self.qkv[:, self.heads(2 * width, pair)] = jnp.where(mine[0], grad_values[0], grad_values[1]).astype(BF16)
            return carry

        lax.fori_loop(low, high, body, 0)

    def grad_qkv(self, i):
        width, half = self.s.width, self.s.half
        span_z = 2 * self.qkv_w.shape[1] * self.qkv_w.shape[2] * self.qkv_w.shape[3] * self.s.rows
        lanes = slice(i * span_z, (i + 1) * span_z)
        for part in range(2):
            columns = slice(part * half, (part + 1) * half)
            grad = dot(self.qkv[:, lanes], self.first[:, columns], 0, 0).astype(BF16)
            self.g_qkv[2 * i : 2 * i + 2, :, :, 0 : self.s.n_qkv, :, columns] = grad.reshape(
                2, 2, 2, self.s.n_qkv, self.s.rows, half
            )

    def back_qkv(self):
        half = self.s.half
        for part in range(2):
            lanes = slice(part * half, (part + 1) * half)
            weight = flat(self.qkv_w[:, :, :, :, :, lanes], half)
            self.total[:, lanes] = dot(self.qkv[...], weight, 1, 0)

    def norm_first_back(self):
        gain = self.lines[0:1, :]
        width = self.s.width
        zero = jnp.zeros((1, width), F32)

        def body(i, sums):
            upstream = self.total[span(i, TILE), :]
            n, rs = normalized(self.embedded[span(i, TILE), :])
            u = upstream * gain
            back = rs * (u - jnp.mean(u, axis=-1, keepdims=True) - n * jnp.mean(u * n, axis=-1, keepdims=True))
            grad = self.mid[span(i, TILE), :] + back
            self.row_x[i] = grad.astype(BF16)
            projected = self.qkv[span(i, TILE), :].astype(F32)
            fresh = (upstream * n, upstream, projected[:, 0:width], projected[:, 2 * width :])
            return tuple(a + jnp.sum(b, axis=0, keepdims=True) for a, b in zip(sums, fresh))

        sums = lax.fori_loop(0, self.length // TILE, body, (zero,) * 4)
        self.grad_lines[0:1, :] = sums[0]
        self.grad_lines[2:3, :] = sums[1]
        self.grad_lines[4:5, :] = sums[2]
        self.grad_lines[5:6, :] = sums[3]

    def grad_small(self):
        s = self.s
        part = self.spread.shape[0]
        turn = (iota((1, s.width), 1) // s.own) % s.n_ff
        picked = turn == iota((s.n_ff, 1), 0)
        for tile in range(s.n_ff):
            seen = self.up_sum[:, tile * s.width : (tile + 1) * s.width]
            moved = dot(jnp.where(picked, seen, 0.0).astype(BF16), self.spread[...], 1, 1)
            self.grad_lines[8 : 8 + s.n_ff, tile * part : (tile + 1) * part] = moved
        eye = (iota((16, s.small), 0) == iota((16, s.small), 1)).astype(BF16)
        lines = dot(self.grad_lines[...].astype(BF16), eye, 0, 0).astype(BF16)
        self.g_small[:, :, :, :, s.small :] = lines.reshape(*s.chips, s.rows, s.small)
        sums = dot(flat(self.row_x[...], s.width), self.token_hot[...], 0, 0).astype(BF16)
        self.g_small[:, :, :, :, 0 : s.small] = sums.reshape(*s.chips, s.rows, s.small)


LAG = 2


def layer_kernel(
    sizes, inputs, cotangent, table, qkv, out, up, down, vectors, steps, lengths, item_map,
    end_small, end_qkv, end_out, end_up, end_down, result, input_grad,
    w_small, w_qkv, w_out, w_up, w_down, g_small, g_up, g_down,
    own_small, own_qkv, own_out, own_up, own_down,
    sib_small, sib_qkv, sib_out, sib_up, sib_down,
    f_small, f_qkv, f_out, f_up, f_down,
    first_small, first_down, pool_small, pool, row_x, row_cot, *rest,
):
    scratch, sems = rest[:20], rest[20:]
    (
        send, receive, back_send, back_receive, raw_send, raw_receive, row_send, row_receive, row_local,
        end_send, end_receive, free,
    ) = sems
    place = Place()
    half, depth = sizes.half, sizes.depth
    me = place.column
    groups = inputs.shape[0]
    weights = [w_small, w_qkv, w_out, w_up, w_down]
    own = [own_small, own_qkv, own_out, own_up, own_down]
    sib = [sib_small, sib_qkv, sib_out, sib_up, sib_down]
    finals = [f_small, f_qkv, f_out, f_up, f_down]
    ends = [end_small, end_qkv, end_out, end_up, end_down]
    grad_out = w_up.at[:, :, :, sizes.n_qkv]
    layer = Layer(sizes, weights, [g_small, w_up, grad_out, g_up, g_down], row_x, row_cot, scratch)

    def width_of(slot):
        return sizes.small if slot == 0 else half

    hot = (steps[...] == iota((sizes.items, table.shape[1]), 1)).astype(BF16)
    own_small[...] = jnp.zeros_like(own_small)
    own_small[:, 0 : sizes.items] = dot(table[...], hot, 1, 1)
    eye = (iota((vectors.shape[0], sizes.small), 0) == iota((vectors.shape[0], sizes.small), 1)).astype(BF16)
    own_small[:, sizes.small :] = dot(vectors[...], eye, 0, 0)
    for source, target in ((qkv, own_qkv), (out, own_out), (up, own_up), (down, own_down)):
        target[...] = source[...].astype(F32)

    def row_copies(which, source, target):
        found = []
        for step in range(1, groups):
            peer = (me + step) % groups
            found.append(
                remote(
                    source.at[peer], target.at[me], row_send.at[which, step - 1], row_receive.at[which, step - 1],
                    (lax.axis_index("dp"), peer),
                )
            )
        return found, pltpu.make_async_copy(source.at[me], target.at[me], row_local.at[which])

    rows = [
        row_copies(0, inputs, row_x),
        row_copies(1, cotangent, row_cot),
        row_copies(2, layer.result, result),
        row_copies(3, row_x, input_grad),
    ]

    def start_rows(which):
        for copy in [*rows[which][0], rows[which][1]]:
            copy.start()

    def rows_arrived(which):
        for copy in rows[which][0]:
            copy.wait_recv()
        rows[which][1].wait()

    def rows_sent(which):
        for copy in rows[which][0]:
            copy.wait_send()

    def raw_copies(core):
        found = []
        for slot, (mine, theirs) in enumerate(zip(own, sib)):
            wide = width_of(slot)
            for part in range(mine.shape[1] // (2 * wide)):
                found.append(
                    remote(
                        mine.at[:, pl.ds((2 * part + 1 - core) * wide, wide)],
                        theirs.at[:, pl.ds(part * wide, wide)],
                        raw_send.at[slot, part],
                        raw_receive.at[slot, part],
                        place.sibling(),
                    )
                )
        return found

    def place_own(core):
        copies = raw_copies(core)
        index = 0
        z, y, x = (place.at[a] for a in "zyx")
        for slot, (mine, theirs) in enumerate(zip(own, sib)):
            wide = width_of(slot)
            for part in range(mine.shape[1] // (2 * wide)):
                copies[index].wait_recv()
                index += 1
                here = mine[:, (2 * part + core) * wide : (2 * part + core + 1) * wide]
                there = theirs[:, part * wide : (part + 1) * wide]
                block = jnp.concatenate([here, there] if core == 0 else [there, here], axis=0).astype(BF16)
                lanes = pl.ds((2 * part + core) * wide, wide)
                if weights[slot].ndim == 6:
                    for unit in range(weights[slot].shape[3]):
                        weights[slot][z, y, x, unit, :, lanes] = block[unit * sizes.rows : (unit + 1) * sizes.rows]
                else:
                    weights[slot][z, y, x, :, lanes] = block

    arriving = [Gather(place, unit, view, send, receive) for unit, view in enumerate(sizes.views(weights))]
    count = len(arriving)

    def gather_beat(beat):
        for stage in (3, 2, 1, 0):
            unit = beat - stage * LAG
            if 0 <= unit < count:
                if stage:
                    arriving[unit].step(stage)
                elif unit + 2 < count:
                    arriving[unit + 2].step(0)

    def whole(*units):
        for unit in units:
            arriving[unit].sibling_arrived()

    spots = [(0, 0)] + [(1, u) for u in range(sizes.n_qkv)] + [(2, 0)]
    spots += [(3, u) for u in range(sizes.n_ff)] + [(4, u) for u in range(sizes.n_ff)]
    views = sizes.views([g_small, w_up, lambda z, y, x, core: w_up.at[z, y, x, sizes.n_qkv, :, pl.ds(core * half, half)], g_up, g_down])
    down_unit = 1 + sizes.n_qkv + 1 + sizes.n_ff

    def landings(unit, z_first):
        here = (lambda *i: pool_small.at[i]) if unit == 0 else (lambda *i: pool.at[(unit - 1, *i)])
        some = pl.ds(0, depth - 1)
        if z_first:
            return here(some, 1, 1), here(ALL, 0, 0), here(ALL, 0, 1), here(ALL, 1, 0)
        return here(some), here(depth - 1, 0, 0), here(depth - 1, 0, 1), here(depth - 1, 1, 0)

    def first_landing(unit):
        if unit == 0:
            return first_small
        if unit >= down_unit:
            return first_down.at[unit - down_unit]
        return w_down.at[:, :, :, :, pl.ds((unit - 1) * half, half)]

    leaving = [
        Scatter(
            place, unit, view, first_landing(unit), functools.partial(landings, unit), back_send, back_receive
        )
        for unit, view in enumerate(views)
    ]

    def final(unit):
        slot, part = spots[unit]
        if slot == 4:
            return lambda core: finals[slot].at[:, pl.ds(part * half, half)]
        return lambda core: finals[slot].at[pl.ds(part * sizes.rows, sizes.rows), :]

    def end_copies(core, slot):
        wide = width_of(slot)
        count = ends[slot].shape[0]
        found = []
        for part in range(finals[slot].shape[1] // wide):
            source = finals[slot].at[pl.ds((1 - core) * count, count), pl.ds(part * wide, wide)]
            target = ends[slot].at[:, pl.ds((2 * part + core) * wide, wide)]
            found.append(remote(source, target, end_send.at[slot, part], end_receive.at[slot, part], place.sibling()))
        return found

    def close(slot):
        wide = width_of(slot)
        count = ends[slot].shape[0]
        for core in range(2):

            @on_core(place, core)
            def _():
                for copy in end_copies(core, slot):
                    copy.start()
                for part in range(finals[slot].shape[1] // wide):
                    ends[slot][:, (2 * part + core) * wide : (2 * part + core + 1) * wide] = finals[slot][
                        core * count : (core + 1) * count, part * wide : (part + 1) * wide
                    ]

    qkv_units = list(range(1, 1 + sizes.n_qkv))
    out_unit = 1 + sizes.n_qkv
    up_units = list(range(out_unit + 1, down_unit))
    down_units = list(range(down_unit, count))
    ready, born = [], {}
    state = {"beat": 0}

    def offer(unit):
        leaving[unit].start_sibling()
        ready.append(unit)

    def scatter_beat():
        beat = state["beat"]
        state["beat"] += 1
        fresh = [unit for unit in ready if unit not in born][:1]
        for unit in fresh:
            born[unit] = beat
        for unit in ready:
            if unit not in born or (beat - born[unit]) % LAG:
                continue
            stage = (beat - born[unit]) // LAG
            if stage > 3:
                continue
            leaving[unit].step(stage, final(unit))
            if stage == 3:
                done.append(unit)
                slot = spots[unit][0]
                if all(other in done for other in range(count) if spots[other][0] == slot):
                    close(slot)

    done = []

    meet(place)
    for core in range(2):

        @on_core(place, core)
        def _():
            for copy in raw_copies(core):
                copy.start()

    start_rows(0)
    for core in range(2):

        @on_core(place, core)
        def _():
            place_own(core)

    arriving[0].step(0)
    arriving[1].step(0)
    gather_beat(0)
    start_rows(1)
    layer.prepare(lengths, item_map, me)
    for beat in range(1, 3 * LAG + 2):
        gather_beat(beat)
    whole(0)
    rows_arrived(0)
    layer.small_lines()
    layer.norm_first()
    for beat in range(3 * LAG + 2, 3 * LAG + 5):
        gather_beat(beat)
    whole(*qkv_units)
    layer.project(0)
    layer.project(1)
    beat = 3 * LAG + 5
    pairs = HEADS // 2
    for low in range(0, pairs, 2):
        layer.attend(low, low + 2)
        gather_beat(beat)
        beat += 1
    whole(out_unit)
    layer.merge()
    layer.norm_second()
    while beat < 3 * LAG + up_units[-1] + 2:
        gather_beat(beat)
        beat += 1
    whole(*up_units)
    for z in range(depth):
        layer.activate(z)
        if z % 2 and beat < count + 3 * LAG:
            gather_beat(beat)
            beat += 1
    rows_arrived(1)
    for index, unit in enumerate(down_units):
        layer.grad_down(index)
        offer(unit)
        if beat < count + 3 * LAG:
            gather_beat(beat)
            beat += 1
        if index:
            scatter_beat()
    while beat < count + 3 * LAG:
        gather_beat(beat)
        beat += 1
        scatter_beat()
    layer.bias_down()
    for index, unit in enumerate(down_units):
        whole(unit)
    for index in range(sizes.n_ff):
        layer.back_active(index)
        if index % 2:
            scatter_beat()
    layer.finish()
    start_rows(2)
    for unit in down_units:
        arriving[unit].sent()
    pl.semaphore_signal(free, inc=1, device_id=place.sibling(), device_id_type=MESH)
    for z in range(depth):
        layer.grad_up(z)
    pl.semaphore_wait(free, 1)
    for unit in up_units:
        offer(unit)
    scatter_beat()
    layer.back_up()
    layer.norm_second_back()
    scatter_beat()
    for unit in up_units:
        arriving[unit].sent()
    layer.grad_out()
    offer(out_unit)
    layer.back_out()
    scatter_beat()
    for low in range(0, pairs, 2):
        layer.attend_back(low, low + 1)
        scatter_beat()
        layer.attend_back(low + 1, low + 2)
        if low:
            scatter_beat()
    for i in range(depth // 2):
        layer.grad_qkv(i)
    for unit in qkv_units:
        offer(unit)
    scatter_beat()
    layer.back_qkv()
    layer.norm_first_back()
    start_rows(3)
    layer.grad_small()
    offer(0)
    while len(done) < count:
        scatter_beat()
    for unit in [0, *qkv_units, out_unit]:
        arriving[unit].sent()
    for unit in leaving:
        unit.sent()
    for slot in range(5):
        for core in range(2):

            @on_core(place, core)
            def _():
                for copy in end_copies(core, slot):
                    copy.wait_send()
                for copy in end_copies(1 - core, slot):
                    copy.wait_recv()

    for core in range(2):

        @on_core(place, core)
        def _():
            for copy in raw_copies(core):
                copy.wait_send()

    rows_sent(0)
    rows_sent(1)
    for which in (2, 3):
        rows_arrived(which)
        rows_sent(which)


def write_kernel(
    sizes, end_small, end_qkv, end_out, end_up, end_down, result, input_grad, steps,
    o_table, o_qkv, o_out, o_up, o_down, o_result, o_input, o_lines,
):
    for source, target in (
        (end_qkv, o_qkv), (end_out, o_out), (end_up, o_up), (end_down, o_down), (result, o_result), (input_grad, o_input),
    ):
        target[...] = source[...]
    hot = (steps[...] == iota((sizes.items, o_table.shape[1]), 1)).astype(BF16)
    o_table[...] = dot(end_small[:, 0 : sizes.items].astype(BF16), hot, 1, 0)
    own = sizes.own
    eye = (iota((own, own), 0) == iota((own, own), 1)).astype(F32)
    lines = lax.dot_general(
        end_small[:, sizes.small :], eye, (((0,), (0,)), ((), ())), precision=lax.Precision.HIGHEST, preferred_element_type=F32
    )
    o_lines[...] = lines[0 : o_lines.shape[0]]


def row_by_row(
    inputs, time_table, w_qkv, w_out, w_up, w_down, norm_gains, norm_shifts, biases, up_bias,
    timesteps, item_map, lengths, cotangent,
):
    groups = lax.axis_size("seq")
    local, width = inputs.shape[1], inputs.shape[2]
    length = local * groups
    ff, items = w_down.shape[0], timesteps.shape[0]
    depth = lax.axis_size("dp") // 2
    sizes = Sizes(width, ff, lax.axis_size("dp") * groups, depth, items)
    half, rows, small, per = sizes.half, sizes.rows, sizes.small, sizes.n_ff

    vectors = jnp.concatenate((norm_gains, norm_shifts, biases, up_bias.reshape(per, -1)), axis=0)
    vectors = jnp.pad(vectors, ((0, 16 - vectors.shape[0]), (0, 0)))
    steps = timesteps.reshape(items, 1)
    shapes = sizes.weights()
    own_shapes = sizes.own_shapes()
    final_shapes = [(rows, small), (rows * 3, half), (rows, half), (rows * per, half), (rows, ff // 2)]
    row_shape = (groups, local, width)
    unit_sems = pltpu.SemaphoreType.DMA((sizes.units, depth + 3))
    smem = pl.BlockSpec(memory_space=pltpu.SMEM)
    scratch = (
        [pltpu.VMEM(shape, BF16) for shape in shapes]
        + [pltpu.VMEM(shapes[slot], BF16) for slot in (0, 3, 4)]
        + [pltpu.VMEM(shape, F32) for shape in own_shapes]
        + [pltpu.VMEM((r, c // 2), F32) for r, c in own_shapes]
        + [pltpu.VMEM(shape, F32) for shape in final_shapes]
        + [
            pltpu.VMEM((*sizes.chips, rows, small), BF16),
            pltpu.VMEM((per, *sizes.chips, rows, half), BF16),
            pltpu.VMEM((*sizes.chips, rows, small), BF16),
            pltpu.VMEM((sizes.units - 1, *sizes.chips, rows, half), BF16),
            pltpu.VMEM(row_shape, BF16),
            pltpu.VMEM(row_shape, BF16),
        ]
        + [
            pltpu.VMEM((length, width), F32),
            pltpu.VMEM((length, width), BF16),
            pltpu.VMEM((length, 3 * width), BF16),
            pltpu.VMEM((length, width), BF16),
            pltpu.VMEM((length, 2 * HEAD_DIM), F32),
            pltpu.VMEM((length, width), F32),
            pltpu.VMEM((length, width), BF16),
            pltpu.VMEM((length, ff), BF16),
            pltpu.VMEM((length, ff), BF16),
            pltpu.VMEM(row_shape, BF16),
            pltpu.VMEM((length, width), F32),
            pltpu.VMEM((length, width), BF16),
            pltpu.VMEM((length, length), F32),
            pltpu.VMEM((length, small), BF16),
            pltpu.VMEM((16, width), F32),
            pltpu.VMEM((1, 3 * width), F32),
            pltpu.VMEM((1, ff), F32),
            pltpu.VMEM((width // per, width), BF16),
            pltpu.VMEM((16, width), F32),
            pltpu.VMEM((1, ff), F32),
        ]
        + [unit_sems] * 4
        + [pltpu.SemaphoreType.DMA((5, per))] * 2
        + [pltpu.SemaphoreType.DMA((4, groups - 1))] * 2
        + [pltpu.SemaphoreType.DMA((4,))]
        + [pltpu.SemaphoreType.DMA((5, per))] * 2
        + [pltpu.SemaphoreType.REGULAR]
    )
    row_type = jax.ShapeDtypeStruct(row_shape, BF16)
    landed = pl.pallas_call(
        functools.partial(layer_kernel, sizes),
        out_shape=tuple(jax.ShapeDtypeStruct(shape, F32) for shape in own_shapes) + (row_type, row_type),
        in_specs=[ANY, ANY] + [VMEM] * 7 + [smem] * 2,
        out_specs=(VMEM,) * 5 + (ANY, ANY),
        scratch_shapes=scratch,
        compiler_params=pltpu.CompilerParams(collective_id=0, has_side_effects=True, vmem_limit_bytes=VMEM_LIMIT),
    )(inputs, cotangent, time_table.T, w_qkv.T, w_out.T, w_up.T, w_down.T, vectors, steps, lengths, item_map)
    steps_count = time_table.shape[0]
    own_types = [jax.ShapeDtypeStruct(shape, F32) for shape in own_shapes[1:]]
    line_count = 8 + per
    written = pl.pallas_call(
        functools.partial(write_kernel, sizes),
        out_shape=(
            jax.ShapeDtypeStruct((sizes.own, steps_count), F32),
            *own_types,
            row_type,
            row_type,
            jax.ShapeDtypeStruct((line_count, sizes.own), F32),
        ),
        in_specs=[VMEM] * 8,
        out_specs=(VMEM,) * 8,
    )(*landed, steps)
    table, qkv, out, up, down, result, input_grad, lines = written
    return (
        result,
        input_grad,
        table.T,
        qkv.T,
        out.T,
        up.T,
        down.T,
        lines[0:2],
        lines[2:4],
        lines[4:8],
        lines[8:].reshape(1, -1),
    )


def on_device(*arrays):
    inputs, w_out, w_down, timesteps = arrays[0], arrays[3], arrays[5], arrays[10]
    width, ff = inputs.shape[2], w_down.shape[0]
    own = w_out.shape[1]
    fits = (
        lax.axis_size("seq") == 4
        and inputs.shape[0] == 4
        and lax.axis_size("dp") % 4 == 0
        and own % 8 == 0
        and ff % width == 0
        and width % 256 == 0
        and timesteps.shape[0] <= 128
    )
    return row_by_row(*arrays) if fits else spread_out(*arrays)


def solution(mesh):
    return jax.shard_map(
        on_device,
        mesh=mesh,
        in_specs=(
            P(None, ("dp", "seq"), None),
            P(None, ("dp", "seq")),
            P(None, ("dp", "seq")),
            P(None, ("dp", "seq")),
            P(None, ("dp", "seq")),
            P(None, ("dp", "seq")),
            P(None, ("dp", "seq")),
            P(None, ("dp", "seq")),
            P(None, ("dp", "seq")),
            P(None, ("dp", "seq")),
            P(),
            P("dp"),
            P("dp", None),
            P(None, ("dp", "seq"), None),
        ),
        out_specs=(
            P(None, ("dp", "seq"), None),
            P(None, ("dp", "seq"), None),
            P(None, ("dp", "seq")),
            P(None, ("dp", "seq")),
            P(None, ("dp", "seq")),
            P(None, ("dp", "seq")),
            P(None, ("dp", "seq")),
            P(None, ("dp", "seq")),
            P(None, ("dp", "seq")),
            P(None, ("dp", "seq")),
            P(None, ("dp", "seq")),
        ),
        check_vma=False,
    )
```

```python
import functools

import jax
import jax.numpy as jnp
from jax import lax
from jax.experimental import pallas as pl
from jax.experimental.pallas import tpu as pltpu
from jax.sharding import PartitionSpec as P

HEADS = 12
HEAD_DIM = 64


EPS = 1e-05


def norm_rows(field, gain, offset):
    mean = jnp.mean(field, axis=-1, keepdims=True)
    centred = field - mean
    spread = jnp.mean(centred * centred, axis=-1, keepdims=True)
    return centred * lax.rsqrt(spread + EPS) * gain + offset


def gelu_exact(field):
    return jax.nn.gelu(field, approximate=False)


def scores_block(query_part, keys, query_segment, key_segment, scale):
    raw = scale * jnp.einsum("qhd,khd->hqk", query_part, keys, preferred_element_type=jnp.float32)
    keep = query_segment[None, :, None] == key_segment[None, None, :]
    return jnp.where(keep, raw, -1e30)


def attend_forward(queries, keys, values, segment, scale):
    score = scores_block(queries, keys, segment, segment, scale)
    top = jnp.max(score, axis=-1, keepdims=True)
    expo = jnp.exp(score - top)
    denom = jnp.sum(expo, axis=-1, keepdims=True)
    probs = (expo / denom).astype(jnp.bfloat16)
    results = jnp.einsum("hqk,khd->qhd", probs, values, preferred_element_type=jnp.float32).astype(
        jnp.bfloat16
    )
    log_totals = [top + jnp.log(denom)]
    return (results, log_totals)


def attend_backward(queries, keys, values, segment, log_totals, grad_out, scale):
    length = queries.shape[0]
    block = min(512, length)
    grad_keys = jnp.zeros(keys.shape, jnp.float32)
    grad_values = jnp.zeros(values.shape, jnp.float32)
    grad_queries = []
    for index, begin in enumerate(range(0, length, block)):
        score = scores_block(queries, keys, segment, segment, scale)
        probs = jnp.exp(score - log_totals[index])
        grad_values = jnp.einsum(
            "hqk,qhd->khd", probs.astype(jnp.bfloat16), grad_out, preferred_element_type=jnp.float32
        )
        grad_probs = jnp.einsum(
            "qhd,khd->hqk", grad_out, values, preferred_element_type=jnp.float32
        )
        centre = jnp.sum(probs * grad_probs, axis=-1, keepdims=True)
        grad_score = (probs * (grad_probs - centre)).astype(jnp.bfloat16)
        grad_queries.append(
            (
                scale
                * jnp.einsum("hqk,khd->qhd", grad_score, keys, preferred_element_type=jnp.float32)
            ).astype(jnp.bfloat16)
        )
        grad_keys = scale * jnp.einsum(
            "hqk,qhd->khd", grad_score, queries, preferred_element_type=jnp.float32
        )
    return (grad_queries[0], grad_keys.astype(jnp.bfloat16), grad_values.astype(jnp.bfloat16))


def spread_out(
    inputs,
    time_table,
    w_qkv,
    w_out,
    w_up,
    w_down,
    norm_gains,
    norm_shifts,
    biases,
    up_bias,
    timesteps,
    item_map,
    lengths,
    cotangent,
):
    micro = inputs.shape[0]
    local = inputs.shape[1]
    width = inputs.shape[2]
    groups = lax.axis_size("seq")
    data_count = lax.axis_size("dp")
    seq_len = local * groups
    items_row = lengths.shape[1]
    heads_dev = HEADS // groups
    group_width = width // groups
    scale = HEAD_DIM ** (-0.5)
    my_start = lax.axis_index("seq") * local
    places = jnp.arange(seq_len, dtype=jnp.int32)
    slot_index = jnp.arange(items_row, dtype=jnp.int32)
    step_index = jnp.arange(time_table.shape[0], dtype=jnp.int32)
    totals = None
    results = []
    input_grads = []
    for index in range(micro):
        gathered = (
            lax.all_gather(time_table, ("dp", "seq"), axis=1, tiled=True),
            lax.all_gather(w_qkv, ("dp", "seq"), axis=1, tiled=True),
            lax.all_gather(w_out, ("dp", "seq"), axis=1, tiled=True),
            lax.all_gather(w_up, ("dp", "seq"), axis=1, tiled=True),
            lax.all_gather(w_down, ("dp", "seq"), axis=1, tiled=True),
            lax.all_gather(norm_gains, ("dp", "seq"), axis=1, tiled=True),
            lax.all_gather(norm_shifts, ("dp", "seq"), axis=1, tiled=True),
            lax.all_gather(biases, ("dp", "seq"), axis=1, tiled=True),
            lax.all_gather(up_bias, ("dp", "seq"), axis=1, tiled=True),
        )
        (
            full_table,
            full_qkv,
            full_out,
            full_up,
            full_down,
            full_gains,
            full_shifts,
            full_biases,
            full_up_bias,
        ) = gathered
        gains = full_gains.astype(jnp.float32)
        offsets = full_shifts.astype(jnp.float32)
        bias_rows = full_biases.astype(jnp.float32)
        up_row = full_up_bias.astype(jnp.float32)[0]
        if totals is None:
            totals = [jnp.zeros(a.shape, jnp.float32) for a in gathered]
        ends = jnp.cumsum(lengths[index])
        segment = jnp.sum((ends[None, :] <= places[:, None]).astype(jnp.int32), axis=1)
        my_segment = lax.dynamic_slice_in_dim(segment, my_start, local)
        slot_steps = jnp.take(timesteps, item_map[index * items_row : (index + 1) * items_row])
        token_slot = (my_segment[:, None] == slot_index[None, :]).astype(jnp.bfloat16)
        step_hot = (slot_steps[:, None] == step_index[None, :]).astype(jnp.bfloat16)
        slot_rows = jnp.dot(step_hot, full_table, preferred_element_type=jnp.float32).astype(
            jnp.bfloat16
        )
        embedded = inputs[index].astype(jnp.float32) + jnp.dot(
            token_slot, slot_rows, preferred_element_type=jnp.float32
        )
        first_normed = norm_rows(embedded, gains[0], offsets[0]).astype(jnp.bfloat16)
        projected = jnp.dot(first_normed, full_qkv, preferred_element_type=jnp.float32)
        queries = (projected[:, 0:width] + bias_rows[0]).astype(jnp.bfloat16)
        keys = projected[:, width : 2 * width].astype(jnp.bfloat16)
        values = (projected[:, 2 * width : 3 * width] + bias_rows[1]).astype(jnp.bfloat16)
        head_queries, head_keys, head_values = (
            lax.all_to_all(
                queries.reshape(local, groups, group_width),
                "seq",
                split_axis=1,
                concat_axis=0,
                tiled=True,
            ),
            lax.all_to_all(
                keys.reshape(local, groups, group_width),
                "seq",
                split_axis=1,
                concat_axis=0,
                tiled=True,
            ),
            lax.all_to_all(
                values.reshape(local, groups, group_width),
                "seq",
                split_axis=1,
                concat_axis=0,
                tiled=True,
            ),
        )
        head_queries = head_queries.reshape(seq_len, heads_dev, HEAD_DIM)
        head_keys = head_keys.reshape(seq_len, heads_dev, HEAD_DIM)
        head_values = head_values.reshape(seq_len, heads_dev, HEAD_DIM)
        head_out, log_totals = attend_forward(head_queries, head_keys, head_values, segment, scale)
        attended = lax.all_to_all(
            head_out.reshape(seq_len, 1, group_width),
            "seq",
            split_axis=0,
            concat_axis=1,
            tiled=True,
        ).reshape(local, width)
        mid = (
            embedded
            + jnp.dot(attended, full_out, preferred_element_type=jnp.float32)
            + bias_rows[2]
        )
        second_normed = norm_rows(mid, gains[1], offsets[1]).astype(jnp.bfloat16)
        inner = jnp.dot(second_normed, full_up, preferred_element_type=jnp.float32) + up_row
        activated = gelu_exact(inner).astype(jnp.bfloat16)
        results.append(
            (
                mid
                + jnp.dot(activated, full_down, preferred_element_type=jnp.float32)
                + bias_rows[3]
            ).astype(jnp.bfloat16)
        )
        grad_output = cotangent[index]
        grad_down = jnp.einsum(
            "tf,td->fd", activated, grad_output, preferred_element_type=jnp.float32
        )
        bias_down = jnp.sum(grad_output.astype(jnp.float32), axis=0)
        grad_act = jnp.einsum(
            "td,fd->tf", grad_output, full_down, preferred_element_type=jnp.float32
        )
        unused, gelu_pull = jax.vjp(gelu_exact, inner)
        grad_inner = gelu_pull(grad_act)[0].astype(jnp.bfloat16)
        grad_up = jnp.einsum(
            "td,tf->df", second_normed, grad_inner, preferred_element_type=jnp.float32
        )
        grad_up_bias = jnp.sum(grad_inner.astype(jnp.float32), axis=0)
        upstream = jnp.einsum("tf,df->td", grad_inner, full_up, preferred_element_type=jnp.float32)
        unused, norm_pull = jax.vjp(norm_rows, mid, gains[1], offsets[1])
        back_mid, gain_second, shift_second = norm_pull(upstream)
        grad_mid = grad_output.astype(jnp.float32) + back_mid
        grad_branch = grad_mid.astype(jnp.bfloat16)
        grad_out_weight = jnp.einsum(
            "te,td->ed", attended, grad_branch, preferred_element_type=jnp.float32
        )
        bias_attend = jnp.sum(grad_branch.astype(jnp.float32), axis=0)
        grad_attended = jnp.einsum(
            "td,ed->te", grad_branch, full_out, preferred_element_type=jnp.float32
        ).astype(jnp.bfloat16)
        head_grad = lax.all_to_all(
            grad_attended.reshape(local, groups, group_width),
            "seq",
            split_axis=1,
            concat_axis=0,
            tiled=True,
        ).reshape(seq_len, heads_dev, HEAD_DIM)
        grad_q_heads, grad_k_heads, grad_v_heads = attend_backward(
            head_queries, head_keys, head_values, segment, log_totals, head_grad, scale
        )
        grad_queries, grad_keys, grad_values = (
            lax.all_to_all(
                grad_q_heads.reshape(seq_len, 1, group_width),
                "seq",
                split_axis=0,
                concat_axis=1,
                tiled=True,
            ),
            lax.all_to_all(
                grad_k_heads.reshape(seq_len, 1, group_width),
                "seq",
                split_axis=0,
                concat_axis=1,
                tiled=True,
            ),
            lax.all_to_all(
                grad_v_heads.reshape(seq_len, 1, group_width),
                "seq",
                split_axis=0,
                concat_axis=1,
                tiled=True,
            ),
        )
        grad_projected = jnp.concatenate(
            (
                grad_queries.reshape(local, width),
                grad_keys.reshape(local, width),
                grad_values.reshape(local, width),
            ),
            axis=1,
        )
        grad_qkv = jnp.einsum(
            "td,tc->dc", first_normed, grad_projected, preferred_element_type=jnp.float32
        )
        bias_query = jnp.sum(grad_queries.reshape(local, width).astype(jnp.float32), axis=0)
        bias_value = jnp.sum(grad_values.reshape(local, width).astype(jnp.float32), axis=0)
        upstream_first = jnp.einsum(
            "tc,dc->td", grad_projected, full_qkv, preferred_element_type=jnp.float32
        )
        unused, first_pull = jax.vjp(norm_rows, embedded, gains[0], offsets[0])
        back_first, gain_first, shift_first = first_pull(upstream_first)
        grad_embedded = grad_mid + back_first
        input_grads.append(grad_embedded.astype(jnp.bfloat16))
        slot_sums = jnp.einsum(
            "ts,td->sd",
            token_slot.astype(jnp.float32),
            grad_embedded,
            precision=lax.Precision.HIGHEST,
        )
        grad_table = jnp.einsum(
            "si,sd->id", step_hot.astype(jnp.float32), slot_sums, precision=lax.Precision.HIGHEST
        )
        grad_gains = jnp.stack((gain_first, gain_second), axis=0)
        grad_shifts = jnp.stack((shift_first, shift_second), axis=0)
        grad_biases = jnp.stack((bias_query, bias_value, bias_attend, bias_down), axis=0)
        grad_up_row = grad_up_bias[None, :]
        fresh = (
            grad_table,
            grad_qkv,
            grad_out_weight,
            grad_up,
            grad_down,
            grad_gains,
            grad_shifts,
            grad_biases,
            grad_up_row,
        )
        totals = [a + b for a, b in zip(totals, fresh)]

    def spread(grad):
        return grad.reshape(
            grad.shape[0], data_count, groups, grad.shape[1] // (data_count * groups)
        )

    parts = [spread(a) for a in totals]
    folded = (
        lax.all_to_all(
            parts[0].astype(jnp.bfloat16), "seq", split_axis=2, concat_axis=2, tiled=True
        ).astype(jnp.float32),
        lax.all_to_all(
            parts[1].astype(jnp.bfloat16), "seq", split_axis=2, concat_axis=2, tiled=True
        ).astype(jnp.float32),
        lax.all_to_all(
            parts[2].astype(jnp.bfloat16), "seq", split_axis=2, concat_axis=2, tiled=True
        ).astype(jnp.float32),
        lax.all_to_all(
            parts[3].astype(jnp.bfloat16), "seq", split_axis=2, concat_axis=2, tiled=True
        ).astype(jnp.float32),
        lax.all_to_all(
            parts[4].astype(jnp.bfloat16), "seq", split_axis=2, concat_axis=2, tiled=True
        ).astype(jnp.float32),
        lax.all_to_all(
            parts[5].astype(jnp.bfloat16), "seq", split_axis=2, concat_axis=2, tiled=True
        ).astype(jnp.float32),
        lax.all_to_all(
            parts[6].astype(jnp.bfloat16), "seq", split_axis=2, concat_axis=2, tiled=True
        ).astype(jnp.float32),
        lax.all_to_all(
            parts[7].astype(jnp.bfloat16), "seq", split_axis=2, concat_axis=2, tiled=True
        ).astype(jnp.float32),
        lax.all_to_all(
            parts[8].astype(jnp.bfloat16), "seq", split_axis=2, concat_axis=2, tiled=True
        ).astype(jnp.float32),
    )
    merged = [jnp.sum(f, axis=2, keepdims=True) for f in folded]
    owners = (
        lax.psum_scatter(merged[0], "dp", scatter_dimension=1, tiled=True),
        lax.psum_scatter(merged[1], "dp", scatter_dimension=1, tiled=True),
        lax.psum_scatter(merged[2], "dp", scatter_dimension=1, tiled=True),
        lax.psum_scatter(merged[3], "dp", scatter_dimension=1, tiled=True),
        lax.psum_scatter(merged[4], "dp", scatter_dimension=1, tiled=True),
        lax.psum_scatter(merged[5], "dp", scatter_dimension=1, tiled=True),
        lax.psum_scatter(merged[6], "dp", scatter_dimension=1, tiled=True),
        lax.psum_scatter(merged[7], "dp", scatter_dimension=1, tiled=True),
        lax.psum_scatter(merged[8], "dp", scatter_dimension=1, tiled=True),
    )
    owned = [o.reshape(o.shape[0], o.shape[3]) for o in owners]
    return (
        jnp.stack(results, axis=0),
        jnp.stack(input_grads, axis=0),
        owned[0],
        owned[1],
        owned[2],
        owned[3],
        owned[4],
        owned[5],
        owned[6],
        owned[7],
        owned[8],
    )


F32 = jnp.float32
BF16 = jnp.bfloat16
MESH = pl.DeviceIdType.MESH
VMEM_LIMIT = 63 << 20
VMEM = pl.BlockSpec(memory_space=pltpu.VMEM)
ANY = pl.BlockSpec(memory_space=pl.ANY)
ALL = slice(None)
class Place:
    def __init__(self):
        row, column = lax.axis_index("dp"), lax.axis_index("seq")
        self.at = {"z": row // 2, "y": row % 2, "x": column // 2}
        self.core = column % 2
        self.column = column
        self.depth = lax.axis_size("dp") // 2

    def device(self, core=None, **moved):
        at = {**self.at, **moved}
        core = self.core if core is None else core
        return (at["z"] * 2 + at["y"], at["x"] * 2 + core)

    def other(self, axis):
        return 1 - self.at[axis]

    def around(self, step):
        return (self.at["z"] + step) % self.depth

    def steps(self):
        upper = self.at["z"] // (self.depth // 2)
        return [step + upper * (self.depth - 2 * step) for step in range(1, self.depth)]

    def sibling(self):
        return self.device(core=1 - self.core)

    def partners(self):
        found = [self.sibling(), self.device(x=self.other("x")), self.device(y=self.other("y"))]
        found.append(self.device(core=1 - self.core, x=self.other("x")))
        found += [self.device(z=self.around(step)) for step in range(1, self.depth)]
        return found


def greet(place):
    barrier = pltpu.get_barrier_semaphore()
    for partner in place.partners():
        pl.semaphore_signal(barrier, inc=1, device_id=partner, device_id_type=MESH)


def meet(place):
    pl.semaphore_wait(pltpu.get_barrier_semaphore(), len(place.partners()))


def remote(source, target, send, receive, device):
    return pltpu.make_async_remote_copy(
        src_ref=source,
        dst_ref=target,
        send_sem=send,
        recv_sem=receive,
        device_id=device,
        device_id_type=MESH,
    )


def on_core(place, core):
    return pl.when(place.core == core)


class Route:
    def __init__(self, place, unit, kinds, view, send, receive):
        self.place, self.unit, self.kinds, self.view = place, unit, kinds, view
        self.send, self.receive = send, receive

    def kind(self, core):
        found = self.kinds[core][self.unit]
        return found < 2, "yx"[found % 2], "xy"[found % 2]

    def part(self, core, **moved):
        at = {**self.place.at, **moved}
        return self.view(at["z"], at["y"], at["x"], core)

    def copy(self, slot, source, target, device):
        return remote(source, target, self.send.at[slot], self.receive.at[slot], device)

    def over(self, axis):
        return self.place.device(**{axis: self.place.other(axis)})

    def on_each_core(self, act):
        for core in range(2):

            @on_core(self.place, core)
            def _():
                act(core)


class Gather(Route):
    def copies(self, core, name):
        place, depth = self.place, self.place.depth
        z_first, late, early = self.kind(core)
        spread = ALL if z_first else place.at["z"]
        if name == "z":
            block = self.part(core) if z_first else self.part(core, x=ALL, y=ALL)
            return [self.copy(0, block, block, place.device(z=place.around(step))) for step in place.steps()]
        if name == "sibling":
            block = self.part(core, z=ALL, y=ALL, x=ALL)
            return [self.copy(3, block, block, place.sibling())]
        moved = {early: place.other(early)} if name == "diagonal" else {}
        block = self.part(core, z=spread, **moved)
        return [self.copy(1 if name == "early" else 2, block, block, self.over(early if name == "early" else late))]

    def together(self, core, slot):
        z_first, late, early = self.kind(core)
        if slot == 0:
            moved = {} if z_first else {"x": ALL, "y": ALL}
            moved["z"] = pl.ds(0, self.place.depth - 1)
        elif slot == 3:
            moved = {"z": ALL, "y": ALL, "x": ALL}
        else:
            moved = {"z": ALL} if z_first else {}
            if slot == 2:
                moved[early] = ALL
        block = self.part(core, **moved)
        return self.copy(slot, block, block, self.place.sibling())

    def stages(self, core):
        if self.kind(core)[0]:
            return [((), ("z",)), ((0,), ("early", "late")), ((1,), ("diagonal",)), ((2,), ("sibling",))]
        return [((), ("early", "late")), ((1,), ("diagonal",)), ((2,), ("z",)), ((0,), ("sibling",))]

    def step(self, stage):
        def act(core):
            waits, starts = self.stages(core)[stage]
            for slot in waits:
                self.together(core, slot).wait_recv()
            for name in starts:
                for copy in self.copies(core, name):
                    copy.start()

        self.on_each_core(act)

    def sibling_arrived(self):
        self.on_each_core(lambda core: self.together(1 - core, 3).wait_recv())

    def sent(self):
        def act(core):
            for slot in range(4):
                self.together(core, slot).wait_send()

        self.on_each_core(act)


class Scatter(Route):
    def __init__(self, place, unit, kinds, view, first, landings, send, receive):
        super().__init__(place, unit, kinds, view, send, receive)
        self.first, self.landings = first, landings

    def sibling_copy(self, core):
        theirs = self.part(1 - core, z=ALL, y=ALL, x=ALL)
        return self.copy(3, theirs, self.first, self.place.sibling())

    def target(self, core, name):
        z_first, late, early = self.kind(core)
        if name == "z" and not z_first:
            return self.part(core, x=ALL, y=ALL)
        moved = {early: self.place.other(early)} if name == "diagonal" else {}
        if name != "z" and z_first:
            moved["z"] = ALL
        return self.part(core, **moved)

    def copies(self, core, name):
        place, depth = self.place, self.place.depth
        z_first, late, early = self.kind(core)
        z_land, diagonal, direct, near = self.landings(z_first)
        if name == "z":
            found = []
            rest = {} if z_first else {"x": ALL, "y": ALL}
            for step in place.steps():
                gone = self.part(core, z=place.around(step), **rest)
                landing = z_land.at[step - 1]
                found.append((self.copy(0, gone, landing, place.device(z=place.around(step))), landing))
            return found
        moved = {"z": ALL} if z_first else {}
        if name != "near":
            moved[late] = place.other(late)
        if name != "direct":
            moved[early] = place.other(early)
        slot, landing = {"direct": (1, direct), "near": (1, near), "diagonal": (2, diagonal)}[name]
        gone = self.part(core, **moved)
        return [(self.copy(slot, gone, landing, self.over(early if name == "near" else late)), landing)]

    def together(self, core, slot):
        z_first, late, early = self.kind(core)
        if slot == 0:
            moved = {} if z_first else {"x": ALL, "y": ALL}
            moved["z"] = pl.ds(0, self.place.depth - 1)
        else:
            moved = {"z": ALL} if z_first else {}
            if slot == 1:
                moved[early] = ALL
        block = self.part(core, **moved)
        return self.copy(slot, block, block, self.place.sibling())

    def stages(self, core):
        if self.kind(core)[0]:
            return [((), ("diagonal", "direct")), (("diagonal",), ("near",)), (("near", "direct"), ("z",)), (("z",), ())]
        return [((), ("z",)), (("z",), ("diagonal", "direct")), (("diagonal",), ("near",)), (("near", "direct"), ())]

    def start_sibling(self):
        self.on_each_core(lambda core: self.sibling_copy(core).start())

    def step(self, stage, result):
        def act(core):
            waits, starts = self.stages(core)[stage]
            if stage == 0:
                self.sibling_copy(core).wait_recv()
                mine = self.part(core, z=ALL, y=ALL, x=ALL)
                mine[...] = (mine[...].astype(F32) + self.first[...].astype(F32)).astype(BF16)
            if waits:
                self.together(core, {"z": 0, "near": 1, "diagonal": 2}[waits[0]]).wait_recv()
                target = self.target(core, waits[0])
                total = target[...].astype(F32)
                z_land, diagonal, direct, near = self.landings(self.kind(core)[0])
                came = {"near": near, "direct": direct, "diagonal": diagonal}
                for name in waits:
                    if name == "z":
                        for step in range(1, self.place.depth):
                            total = total + z_land[step - 1].astype(F32)
                    else:
                        total = total + came[name][...].astype(F32)
                if stage == 3:
                    result(core)[...] = total
                else:
                    target[...] = total.astype(BF16)
            for name in starts:
                for copy, _ in self.copies(core, name):
                    copy.start()

        self.on_each_core(act)

    def sent(self):
        def act(core):
            self.sibling_copy(core).wait_send()
            for slot in range(3):
                self.together(core, slot).wait_send()

        self.on_each_core(act)


GATHER_KINDS = (
    (2, 0, 0, 0, 2, 0, 0, 0, 0, 0, 2, 1, 3),
    (0, 1, 0, 1, 0, 1, 0, 1, 2, 1, 0, 0, 0),
)
SCATTER_KINDS = (
    (0, 0, 1, 0, 0, 0, 3, 0, 2, 0, 0, 2, 2),
    (0, 0, 2, 1, 0, 0, 1, 1, 0, 1, 0, 3, 1),
)
SCHEDULE = (
    2632, 2600, 2201, 2624, 2633, 2612, 0, 2616, 2608, 2604, 2628, 2601, 2620, 2625, 2613, 2644, 2602, 2648, 2617,
    2626, 2609, 2614, 2640, 2605, 2606, 2610, 2618, 2200, 2301, 2627, 2621, 2629, 2603, 2634, 2607, 2615, 2636, 2401,
    2400, 2611, 2403, 2641, 2300, 100, 200, 400, 2622, 2402, 1400, 1401, 1502, 2630, 2642, 2645, 2649, 2619, 1503,
    2635, 2623, 2406, 1504, 1501, 2404, 1500, 1505, 2631, 300, 2637, 2646, 2408, 2650, 2407, 2405, 1603, 1703, 2512,
    1601, 1701, 800, 2638, 2643, 2510, 2748, 2647, 1602, 1702, 2651, 2639, 2740, 2511, 1600, 2411, 1700, 2410, 2412,
    2509, 2409, 1803, 2744, 1801, 2741, 1901, 2736, 1800, 1903, 1802, 1900, 1902, 2507, 2506, 500, 2737, 2728, 2505,
    2724, 600, 2742, 2749, 2729, 700, 900, 2738, 2508, 2720, 2504, 1000, 2202, 2004, 2002, 2716, 2732, 2730, 2005,
    2725, 2745, 2750, 2001, 2003, 2717, 2000, 2100, 2101, 2502, 2721, 2718, 2501, 2746, 2751, 1100, 2708, 2704, 2733,
    1200, 1300, 2500, 2705, 2743, 2503, 2700, 2719, 2712, 2734, 2731, 2709, 2706, 2701, 2722, 2735, 2713, 2203, 2702,
    2710, 2726, 2714, 2747, 2723, 2739, 2727, 2302, 2711, 2707, 2703, 2715, 2303,
)


class Sizes:
    def __init__(self, width, ff, devices, depth, items):
        self.width, self.ff, self.devices, self.depth, self.items = width, ff, devices, depth, items
        self.half = width // 2
        self.own = width // devices
        self.rows = 2 * self.own
        self.n_qkv, self.n_ff = 3, ff // width
        self.small = 128
        self.units = 1 + self.n_qkv + 1 + 2 * self.n_ff
        self.chips = (depth, 2, 2)

    def weights(self):
        return [
            (*self.chips, self.rows, 2 * self.small),
            (*self.chips, self.n_qkv, self.rows, self.width),
            (*self.chips, self.rows, self.width),
            (*self.chips, self.n_ff, self.rows, self.width),
            (*self.chips, self.rows, self.ff),
        ]

    def own_shapes(self):
        widths = [2 * self.small, self.width, self.width, self.width, self.ff]
        return [(self.own * n, w) for n, w in zip((1, self.n_qkv, 1, self.n_ff, 1), widths)]

    def raw_places(self):
        shapes = [(slot, part, rows) for slot, rows, parts in (
            (0, self.own, 1), (1, self.n_qkv * self.own, 1), (2, self.own, 1),
            (3, self.n_ff * self.own, 1), (4, self.own, self.n_ff),
        ) for part in range(parts)]
        begin, found = 0, []
        for slot, part, rows in shapes:
            found.append([slot, part, rows, (begin, 0)])
            begin += rows
        tops = [begin, begin]
        for entry in found:
            side = 0 if entry[0] in (1, 2, 3) else 1
            entry.append((tops[side], side * self.half))
            entry.append(self.small if entry[0] == 0 else self.half)
            tops[side] += entry[2]
        return found, max(tops)

    def views(self, refs):
        small, qkv, out, up, down = refs
        half = self.half

        def columns(core, base=0, width=half):
            return pl.ds(base + core * width, width)

        found = [lambda z, y, x, core: small.at[z, y, x, :, columns(core, 0, self.small)]]
        for unit in range(self.n_qkv):
            found.append(lambda z, y, x, core, unit=unit: qkv.at[z, y, x, unit, :, columns(core)])
        found.append(out if callable(out) else lambda z, y, x, core: out.at[z, y, x, :, columns(core)])
        for unit in range(self.n_ff):
            found.append(lambda z, y, x, core, unit=unit: up.at[z, y, x, unit, :, columns(core)])
        for unit in range(self.n_ff):
            found.append(lambda z, y, x, core, unit=unit: down.at[z, y, x, :, columns(core, unit * self.width)])
        return found


def dot(a, b, ca, cb):
    return lax.dot_general(a, b, (((ca,), (cb,)), ((), ())), preferred_element_type=F32)


def iota(shape, axis):
    return lax.broadcasted_iota(jnp.int32, shape, axis)


def normalized(field):
    mean = jnp.mean(field, axis=-1, keepdims=True)
    centred = field - mean
    spread = jnp.mean(centred * centred, axis=-1, keepdims=True)
    rs = lax.rsqrt(spread + EPS)
    return centred * rs, rs


def loop(count, body):
    lax.fori_loop(0, count, lambda i, c: (body(i), c)[1], 0)


def span(i, size):
    return pl.ds(pl.multiple_of(i * size, size), size)


def flat(block, columns):
    return block.reshape(-1, columns)


TILE = 128


class Layer:
    def __init__(self, sizes, weights, grads, row_x, row_cot, scratch):
        self.s = sizes
        self.small, self.qkv_w, self.out_w, self.up_w, self.down_w = weights
        self.g_small, self.g_qkv, self.g_out, self.g_up, self.g_down = grads
        self.row_x, self.row_cot = row_x, row_cot
        (
            self.embedded, self.first, self.qkv, self.attended, self.log_total, self.mid, self.second,
            self.active, self.slope, self.result, self.total, self.bias, self.token_hot,
            self.lines, self.qkv_bias, self.up_row, self.spread, self.grad_lines, self.up_sum, self.turned,
        ) = scratch
        self.length = self.embedded.shape[0]


    def prepare(self, lengths, item_map, me):
        n, wide = self.length, self.s.small
        half = n // 2
        count = lengths.shape[1]
        sizes = [lengths[me, slot] for slot in range(count)]
        ends = [sizes[0]]
        for slot in range(1, count - 1):
            ends.append(ends[-1] + sizes[slot])
        items = [item_map[me * count + slot] for slot in range(count)]
        begin = ends[-1]
        for slot in range(count - 2, -1, -1):
            begin = jnp.where(sizes[slot] == half, ends[slot] - sizes[slot], begin)

        def position(index):
            moved = index + begin
            return jnp.where(moved >= n, moved - n, moved)

        def segment(index):
            return sum((position(index) >= end).astype(jnp.int32) for end in ends)

        columns = segment(iota((1, half), 1) + half)

        def masks(i):
            rows = segment(iota((TILE, 1), 0) + i * TILE + half)
            self.bias[span(i, TILE), :] = jnp.where(rows == columns, 0.0, -1e30)

        def hots(i):
            index = iota((TILE, 1), 0) + i * TILE
            rows = segment(index)
            item = jnp.full((TILE, 1), items[-1], jnp.int32)
            for slot in range(count - 1):
                item = jnp.where(rows == slot, items[slot], item)
            self.token_hot[span(i, TILE), :] = (item == iota((TILE, wide), 1)).astype(BF16)
            self.turned[span(i, TILE), :] = (position(index) == iota((TILE, n), 1)).astype(BF16)

        loop(half // TILE, masks)
        loop(n // TILE, hots)
        own, per = self.s.own, self.s.n_ff
        part = self.spread.shape[0]
        row, column = iota((part, 1), 0), iota((1, self.s.width), 1)
        same = (row // own == column // (per * own)) & (row % own == column % own)
        self.spread[...] = same.astype(BF16)

    def small_lines(self):
        s = self.s
        eye = (iota((16, s.small), 0) == iota((16, s.small), 1)).astype(BF16)
        lines = dot(eye, flat(self.small[:, :, :, :, s.small :], s.small), 1, 1)
        self.lines[...] = lines
        zero = jnp.zeros((1, s.width), F32)
        self.qkv_bias[...] = jnp.concatenate([lines[4:5], zero, lines[5:6]], axis=1)
        part = self.spread.shape[0]
        turn = (iota((1, s.width), 1) // s.own) % s.n_ff
        picked = turn == iota((s.n_ff, 1), 0)
        for tile in range(s.n_ff):
            seen = lines[8 : 8 + s.n_ff, tile * part : (tile + 1) * part].astype(BF16)
            moved = dot(seen, self.spread[...], 1, 0)
            self.up_row[:, tile * s.width : (tile + 1) * s.width] = jnp.sum(
                jnp.where(picked, moved, 0.0), axis=0, keepdims=True
            )
        self.grad_lines[...] = jnp.zeros_like(self.grad_lines)
        self.up_sum[...] = jnp.zeros_like(self.up_sum)

    def norm_first(self):
        gain, shift = self.lines[0:1, :], self.lines[2:3, :]
        items = flat(self.small[:, :, :, :, 0 : self.s.small], self.s.small)

        def body(i):
            field = dot(self.turned[span(i, TILE), :], flat(self.row_x[...], self.s.width), 1, 0)
            field = field + dot(self.token_hot[span(i, TILE), :], items, 1, 1)
            self.embedded[span(i, TILE), :] = field
            n, _ = normalized(field)
            self.first[span(i, TILE), :] = (n * gain + shift).astype(BF16)

        loop(self.length // TILE, body)

    def project(self, i):
        width = 2 * self.qkv_w.shape[1] * self.qkv_w.shape[2] * self.qkv_w.shape[3] * self.s.rows
        weight = flat(self.qkv_w[2 * i : 2 * i + 2], self.s.width)
        lanes = slice(i * width, (i + 1) * width)
        self.qkv[:, lanes] = (dot(self.first[...], weight, 1, 1) + self.qkv_bias[:, lanes]).astype(BF16)

    def heads(self, base, pair):
        return pl.ds(base + pair * 2 * HEAD_DIM, 2 * HEAD_DIM)

    def attend(self, pair):
        width, half = self.s.width, self.length // 2
        lane = iota((1, 2 * HEAD_DIM), 1)
        mine = [lane < HEAD_DIM, lane >= HEAD_DIM]
        scale = HEAD_DIM ** (-0.5)
        for part in range(2):
            rows = slice(part * half, (part + 1) * half)
            queries = self.qkv[rows, self.heads(0, pair)] * jnp.asarray(scale, BF16)
            keys = self.qkv[rows, self.heads(width, pair)]
            values = self.qkv[rows, self.heads(2 * width, pair)]
            logs = self.log_total[rows, :]
            found = []
            for head in range(2):
                one = jnp.where(mine[head], queries, jnp.zeros_like(queries))
                score = dot(one, keys, 1, 1)
                if part:
                    score = score + self.bias[...]
                top = jnp.max(score, axis=-1, keepdims=True)
                expo = jnp.exp(score - top)
                denom = jnp.sum(expo, axis=-1, keepdims=True)
                probs = (expo * (1.0 / denom)).astype(BF16)
                found.append(dot(probs, values, 1, 0))
                logs = jnp.where(lane == 2 * pair + head, top + jnp.log(denom), logs)
            self.log_total[rows, :] = logs
            self.attended[rows, self.heads(0, pair)] = jnp.where(mine[0], found[0], found[1]).astype(BF16)

    def merge(self):
        width = self.s.width
        for i in range(2):
            weight = flat(self.out_w[2 * i : 2 * i + 2], width)
            lanes = slice(i * weight.shape[0], (i + 1) * weight.shape[0])
            self.mid[:, lanes] = self.embedded[:, lanes] + dot(self.attended[...], weight, 1, 1) + self.lines[6:7, lanes]

    def norm_second(self):
        gain, shift = self.lines[1:2, :], self.lines[3:4, :]

        def body(i):
            n, _ = normalized(self.mid[span(i, TILE), :])
            self.second[span(i, TILE), :] = (n * gain + shift).astype(BF16)

        loop(self.length // TILE, body)

    def activate(self, z):
        half = self.s.ff // (2 * self.s.depth)
        for y in range(2):
            lanes = slice((2 * z + y) * half, (2 * z + y + 1) * half)
            weight = flat(self.up_w[z, y], self.s.width)
            inner = dot(self.second[...], weight, 1, 1) + self.up_row[:, lanes]
            mass = 0.5 + 0.5 * lax.erf(inner * (0.5**0.5))
            self.active[:, lanes] = (inner * mass).astype(BF16)
            bell = jnp.exp(-0.5 * inner * inner) * 0.3989422804014327
            self.slope[:, lanes] = (mass + inner * bell).astype(BF16)

    def finish(self):
        width = self.s.width
        for i in range(2):
            weight = flat(self.down_w[2 * i : 2 * i + 2], self.s.ff)
            lanes = slice(i * weight.shape[0], (i + 1) * weight.shape[0])
            field = self.mid[:, lanes] + dot(self.active[...], weight, 1, 1) + self.lines[7:8, lanes]
            field = dot(self.turned[...], field.astype(BF16), 0, 0).astype(BF16)
            self.result[:, :, lanes] = field.reshape(self.result.shape[0], -1, field.shape[1])


    def turn_cotangent(self):
        half = self.s.half
        for part in range(2):
            lanes = slice(part * half, (part + 1) * half)
            moved = dot(self.turned[...], flat(self.row_cot[:, :, lanes], half), 1, 0).astype(BF16)
            self.row_cot[:, :, lanes] = moved.reshape(self.row_cot.shape[0], -1, half)
        self.grad_lines[7:8, :] = jnp.sum(self.cotangent().astype(F32), axis=0, keepdims=True)

    def cotangent(self):
        return flat(self.row_cot[...], self.s.width)

    def grad_down(self, unit):
        width = self.s.width
        lanes = slice(unit * width, (unit + 1) * width)
        grad = dot(self.cotangent(), self.active[:, lanes], 0, 0).astype(BF16)
        self.g_down[:, :, :, :, lanes] = grad.reshape(*self.s.chips, self.s.rows, width)

    def back_active(self, unit):
        width = self.s.width
        for part in range(2):
            lanes = slice(unit * width + part * width // 2, unit * width + (part + 1) * width // 2)
            weight = flat(self.down_w[:, :, :, :, lanes], width // 2)
            grad = dot(self.cotangent(), weight, 1, 0)
            inner = (self.slope[:, lanes].astype(F32) * grad).astype(BF16)
            self.slope[:, lanes] = inner
            self.up_sum[:, lanes] = jnp.sum(inner.astype(F32), axis=0, keepdims=True)

    def grad_up(self, z):
        half = self.s.ff // (2 * self.s.depth)
        for y in range(2):
            lanes = slice((2 * z + y) * half, (2 * z + y + 1) * half)
            grad = dot(self.slope[:, lanes], self.second[...], 0, 0).astype(BF16)
            self.g_up[z, y] = grad.reshape(2, self.s.n_ff, self.s.rows, self.s.width)

    def back_up(self):
        half = self.s.half
        for part in range(2):
            lanes = slice(part * half, (part + 1) * half)
            weight = flat(self.up_w[:, :, :, :, :, lanes], half)
            self.total[:, lanes] = dot(self.slope[...], weight, 1, 0)

    def norm_second_back(self):
        gain = self.lines[1:2, :]
        zero = jnp.zeros((1, self.s.width), F32)

        def body(i, sums):
            upstream = self.total[span(i, TILE), :]
            n, rs = normalized(self.mid[span(i, TILE), :])
            u = upstream * gain
            back = rs * (u - jnp.mean(u, axis=-1, keepdims=True) - n * jnp.mean(u * n, axis=-1, keepdims=True))
            grad = self.row_cot[i].astype(F32) + back
            self.mid[span(i, TILE), :] = grad
            low = grad.astype(BF16)
            self.row_x[i] = low
            fresh = (upstream * n, upstream, low.astype(F32))
            return tuple(a + jnp.sum(b, axis=0, keepdims=True) for a, b in zip(sums, fresh))

        sums = lax.fori_loop(0, self.length // TILE, body, (zero, zero, zero))
        self.grad_lines[1:2, :] = sums[0]
        self.grad_lines[3:4, :] = sums[1]
        self.grad_lines[6:7, :] = sums[2]

    def grad_out(self):
        grad = dot(flat(self.row_x[...], self.s.width), self.attended[...], 0, 0).astype(BF16)
        self.g_out[...] = grad.reshape(*self.s.chips, self.s.rows, self.s.width)

    def back_out(self):
        weight = flat(self.out_w[...], self.s.width)
        self.attended[...] = dot(flat(self.row_x[...], self.s.width), weight, 1, 0).astype(BF16)

    def attend_back(self, pair):
        width, half = self.s.width, self.length // 2
        lane = iota((1, 2 * HEAD_DIM), 1)
        mine = [lane < HEAD_DIM, lane >= HEAD_DIM]
        scale = HEAD_DIM ** (-0.5)
        for part in range(2):
            rows = slice(part * half, (part + 1) * half)
            queries = self.qkv[rows, self.heads(0, pair)]
            keys = self.qkv[rows, self.heads(width, pair)]
            values = self.qkv[rows, self.heads(2 * width, pair)]
            grads = self.attended[rows, self.heads(0, pair)]
            scaled = queries * jnp.asarray(scale, BF16)
            logs = self.log_total[rows, :]
            found = []
            for head in range(2):
                one = jnp.where(mine[head], scaled, jnp.zeros_like(scaled))
                own = jnp.where(mine[head], grads, jnp.zeros_like(grads))
                log = jnp.sum(jnp.where(lane == 2 * pair + head, logs, 0.0), axis=-1, keepdims=True)
                score = dot(one, keys, 1, 1)
                if part:
                    score = score + self.bias[...]
                probs = jnp.exp(score - log)
                grad_probs = dot(own, values, 1, 1)
                centre = jnp.sum(probs * grad_probs, axis=-1, keepdims=True)
                grad_score = (probs * (grad_probs - centre)).astype(BF16)
                found.append(
                    (
                        scale * dot(grad_score, keys, 1, 0),
                        scale * dot(grad_score, queries, 0, 0),
                        dot(probs.astype(BF16), grads, 0, 0),
                    )
                )
            for slot in range(3):
                both = jnp.where(mine[0], found[0][slot], found[1][slot])
                self.qkv[rows, self.heads(slot * width, pair)] = both.astype(BF16)

    def grad_qkv(self, i):
        width, half = self.s.width, self.s.half
        span_z = 2 * self.qkv_w.shape[1] * self.qkv_w.shape[2] * self.qkv_w.shape[3] * self.s.rows
        lanes = slice(i * span_z, (i + 1) * span_z)
        for part in range(2):
            columns = slice(part * half, (part + 1) * half)
            grad = dot(self.qkv[:, lanes], self.first[:, columns], 0, 0).astype(BF16)
            self.g_qkv[2 * i : 2 * i + 2, :, :, 0 : self.s.n_qkv, :, columns] = grad.reshape(
                2, 2, 2, self.s.n_qkv, self.s.rows, half
            )

    def back_qkv(self):
        half = self.s.half
        for part in range(2):
            lanes = slice(part * half, (part + 1) * half)
            weight = flat(self.qkv_w[:, :, :, :, :, lanes], half)
            self.total[:, lanes] = dot(self.qkv[...], weight, 1, 0)

    def norm_first_back(self):
        gain = self.lines[0:1, :]
        width = self.s.width
        zero = jnp.zeros((1, width), F32)

        def body(i, sums):
            upstream = self.total[span(i, TILE), :]
            n, rs = normalized(self.embedded[span(i, TILE), :])
            u = upstream * gain
            back = rs * (u - jnp.mean(u, axis=-1, keepdims=True) - n * jnp.mean(u * n, axis=-1, keepdims=True))
            grad = self.mid[span(i, TILE), :] + back
            self.row_x[i] = grad.astype(BF16)
            projected = self.qkv[span(i, TILE), :].astype(F32)
            fresh = (upstream * n, upstream, projected[:, 0:width], projected[:, 2 * width :])
            return tuple(a + jnp.sum(b, axis=0, keepdims=True) for a, b in zip(sums, fresh))

        sums = lax.fori_loop(0, self.length // TILE, body, (zero,) * 4)
        self.grad_lines[0:1, :] = sums[0]
        self.grad_lines[2:3, :] = sums[1]
        self.grad_lines[4:5, :] = sums[2]
        self.grad_lines[5:6, :] = sums[3]

    def turn_input_grad(self):
        half = self.s.half
        for part in range(2):
            lanes = slice(part * half, (part + 1) * half)
            moved = dot(self.turned[...], flat(self.row_x[:, :, lanes], half), 0, 0).astype(BF16)
            self.row_cot[:, :, lanes] = moved.reshape(self.row_cot.shape[0], -1, half)

    def grad_small(self):
        s = self.s
        part = self.spread.shape[0]
        turn = (iota((1, s.width), 1) // s.own) % s.n_ff
        picked = turn == iota((s.n_ff, 1), 0)
        for tile in range(s.n_ff):
            seen = self.up_sum[:, tile * s.width : (tile + 1) * s.width]
            moved = dot(jnp.where(picked, seen, 0.0).astype(BF16), self.spread[...], 1, 1)
            self.grad_lines[8 : 8 + s.n_ff, tile * part : (tile + 1) * part] = moved
        eye = (iota((16, s.small), 0) == iota((16, s.small), 1)).astype(BF16)
        lines = dot(self.grad_lines[...].astype(BF16), eye, 0, 0).astype(BF16)
        self.g_small[:, :, :, :, s.small :] = lines.reshape(*s.chips, s.rows, s.small)
        sums = dot(flat(self.row_x[...], s.width), self.token_hot[...], 0, 0).astype(BF16)
        self.g_small[:, :, :, :, 0 : s.small] = sums.reshape(*s.chips, s.rows, s.small)


def layer_kernel(
    sizes, inputs, cotangent, table, qkv, out, up, down, gains, shifts, biases, up_bias, steps, lengths, item_map,
    end_small, end_qkv, end_out, end_up, end_down, result, input_grad,
    w_small, w_qkv, w_out, w_up, w_down, g_small, g_up, g_down,
    raw_table, raw_qkv, raw_out, raw_up, raw_down,
    f_small, f_qkv, f_out, f_up, f_down,
    first_small, first, pool_small, pool, row_x, row_cot, *rest,
):
    scratch, sems = rest[:20], rest[20:]
    (
        loads, send, receive, back_receive, raw_send, raw_receive, row_send, row_receive, row_local,
        end_send, end_receive, end_local,
    ) = sems
    place = Place()
    half, depth = sizes.half, sizes.depth
    me = place.column
    groups = inputs.shape[0]
    weights = [w_small, w_qkv, w_out, w_up, w_down]
    finals = [f_small, f_qkv, f_out, f_up, f_down]
    ends = [end_small, end_qkv, end_out, end_up, end_down]
    grad_out = w_up.at[:, :, :, sizes.n_qkv]
    layer = Layer(sizes, weights, [g_small, w_up, grad_out, g_up, g_down], row_x, row_cot, scratch)

    def width_of(slot):
        return sizes.small if slot == 0 else half

    raws = [
        pltpu.make_async_copy(source, target, loads.at[i])
        for i, (source, target) in enumerate(
            ((table, raw_table), (qkv, raw_qkv), (out, raw_out), (up, raw_up), (down, raw_down))
        )
    ]
    for copy in raws:
        copy.start()
    greet(place)
    lane = iota((1, sizes.small), 1)
    columns = jnp.zeros((sizes.own, sizes.small), F32)
    begin = 0
    for ref in (gains, shifts, biases):
        count = ref.shape[0]
        picked = (iota((count, sizes.small), 1) == iota((count, sizes.small), 0) + begin).astype(BF16)
        columns = columns + dot(ref[...], picked, 0, 0)
        begin += count
    for part in range(sizes.n_ff):
        piece = up_bias[:, part * sizes.own : (part + 1) * sizes.own]
        columns = columns + dot(piece, (lane == begin + part).astype(BF16), 0, 0)
    pieces = []
    for slot, part, count, (row, column), (far_row, far_column), wide in sizes.raw_places()[0]:
        here = layer.total.at[pl.ds(row, count), pl.ds(column, 2 * wide)]
        there = layer.total.at[pl.ds(far_row, count), pl.ds(far_column, wide)]
        pieces.append((slot, part, here, there, wide))
    own_small = pieces[0][2]
    raws[0].wait()
    hot = (iota((table.shape[1], sizes.items), 0) == steps[...]).astype(BF16)
    own_small[:, 0 : sizes.small] = jnp.zeros((sizes.own, sizes.small), F32)
    own_small[:, 0 : sizes.items] = dot(raw_table[...], hot, 1, 0)
    own_small[:, sizes.small :] = columns
    for copy in raws[1:]:
        copy.wait()
    for slot, part, here, _, _ in pieces[1:]:
        source = (raw_qkv, raw_out, raw_up, raw_down)[slot - 1]
        here[...] = source[:, part * sizes.width : (part + 1) * sizes.width].astype(F32)

    rows = [(inputs, row_x), (cotangent, row_cot), (layer.result, result), (row_cot, input_grad)]

    def row_copies(which):
        source, target = rows[which]
        found = []
        for step in range(1, groups):
            peer = (me + step) % groups
            device = (lax.axis_index("dp"), peer)
            found.append(remote(source.at[peer], target.at[me], row_send.at[which], row_receive.at[which], device))
        return found

    def row_local_copy(which):
        source, target = rows[which]
        return pltpu.make_async_copy(source.at[me], target.at[me], row_local.at[which])

    def start_rows(which):
        for copy in [*row_copies(which), row_local_copy(which)]:
            copy.start()

    def rows_together(which):
        source, target = (ref.at[pl.ds(0, groups - 1)] for ref in rows[which])
        return remote(source, target, row_send.at[which], row_receive.at[which], place.sibling())

    def rows_arrived(which):
        rows_together(which).wait_recv()
        row_local_copy(which).wait()

    def rows_sent(which):
        rows_together(which).wait_send()

    def raw_copies(core, slots=range(5)):
        return [
            remote(
                here.at[:, pl.ds((1 - core) * wide, wide)], there, raw_send.at[i], raw_receive.at[i], place.sibling()
            )
            for i, (slot, _, here, there, wide) in enumerate(pieces)
            if slot in slots
        ]

    def place_own(slot):
        z, y, x = (place.at[a] for a in "zyx")
        for core in range(2):

            @on_core(place, core)
            def _():
                for copy in raw_copies(core, [slot]):
                    copy.wait()
                for _, part, mine, theirs, wide in [piece for piece in pieces if piece[0] == slot]:
                    here, there = mine[:, core * wide : (core + 1) * wide], theirs[...]
                    block = jnp.concatenate([here, there] if core == 0 else [there, here], axis=0).astype(BF16)
                    lanes = pl.ds((2 * part + core) * wide, wide)
                    if weights[slot].ndim == 6:
                        for unit in range(weights[slot].shape[3]):
                            weights[slot][z, y, x, unit, :, lanes] = block[unit * sizes.rows : (unit + 1) * sizes.rows]
                    else:
                        weights[slot][z, y, x, :, lanes] = block

    arriving = [
        Gather(place, unit, GATHER_KINDS, view, send.at[unit], receive.at[unit])
        for unit, view in enumerate(sizes.views(weights))
    ]

    spots = [(0, 0)] + [(1, u) for u in range(sizes.n_qkv)] + [(2, 0)]
    spots += [(3, u) for u in range(sizes.n_ff)] + [(4, u) for u in range(sizes.n_ff)]
    views = sizes.views([g_small, w_up, lambda z, y, x, core: w_up.at[z, y, x, sizes.n_qkv, :, pl.ds(core * half, half)], g_up, g_down])
    def landings(unit, z_first):
        here = (lambda *i: pool_small.at[i]) if unit == 0 else (lambda *i: pool.at[(unit - 1, *i)])
        some = pl.ds(0, depth - 1)
        if z_first:
            return here(some, 1, 1), here(ALL, 0, 0), here(ALL, 0, 1), here(ALL, 1, 0)
        return here(some), here(depth - 1, 0, 0), here(depth - 1, 0, 1), here(depth - 1, 1, 0)

    def send_row(unit):
        slot, part = spots[unit]
        return sizes.units + part if slot == 4 else unit

    leaving = [
        Scatter(
            place, unit, SCATTER_KINDS, view, first_small if unit == 0 else first.at[unit - 1],
            functools.partial(landings, unit), send.at[send_row(unit)], back_receive.at[unit],
        )
        for unit, view in enumerate(views)
    ]

    def final(unit):
        slot, part = spots[unit]
        if slot == 4:
            return lambda core: finals[slot].at[:, pl.ds(part * half, half)]
        return lambda core: finals[slot].at[pl.ds(part * sizes.rows, sizes.rows), :]

    def end_copies(core, slot):
        wide = width_of(slot)
        count = ends[slot].shape[0]
        found = []
        for part in range(finals[slot].shape[1] // wide):
            at = slot + part
            columns = pl.ds(part * wide, wide)
            target = ends[slot].at[:, pl.ds((2 * part + core) * wide, wide)]
            gone = finals[slot].at[pl.ds((1 - core) * count, count), columns]
            kept = finals[slot].at[pl.ds(core * count, count), columns]
            found.append(
                (
                    remote(gone, target, end_send.at[at], end_receive.at[at], place.sibling()),
                    pltpu.make_async_copy(kept, target, end_local.at[at]),
                )
            )
        return found

    def close(slot):
        for core in range(2):

            @on_core(place, core)
            def _():
                for pair in end_copies(core, slot):
                    for copy in pair:
                        copy.start()

    done, placed, cleared = [], [], []

    def clear(unit):
        if unit not in cleared:
            cleared.append(unit)
            arriving[unit].sent()

    def offer(unit):
        if spots[unit][0] != 4:
            clear(unit)
        leaving[unit].start_sibling()

    def gather_step(unit, stage):
        slot = spots[unit][0]
        if slot not in placed:
            placed.append(slot)
            place_own(slot)
        arriving[unit].step(stage)

    def scatter_step(unit, stage):
        leaving[unit].step(stage, final(unit))
        if stage == 3:
            done.append(unit)
            slot = spots[unit][0]
            if all(other in done for other in range(sizes.units) if spots[other][0] == slot):
                close(slot)

    def merge():
        layer.merge()
        layer.norm_second()

    def gathered_up():
        for unit, (slot, _) in enumerate(spots):
            if slot == 3:
                clear(unit)

    def end_input_grad():
        layer.norm_first_back()
        layer.turn_input_grad()

    acts = (
        lambda _: layer.prepare(lengths, item_map, me),
        lambda _: layer.small_lines(),
        lambda _: layer.norm_first(),
        lambda _: merge(),
        lambda _: layer.turn_cotangent(),
        lambda _: layer.finish(),
        lambda _: layer.back_up(),
        lambda _: layer.norm_second_back(),
        lambda _: gathered_up(),
        lambda _: layer.grad_out(),
        lambda _: layer.back_out(),
        lambda _: layer.back_qkv(),
        lambda _: end_input_grad(),
        lambda _: layer.grad_small(),
        layer.project,
        layer.attend,
        layer.activate,
        layer.grad_down,
        layer.back_active,
        layer.grad_up,
        layer.attend_back,
        layer.grad_qkv,
        start_rows,
        rows_arrived,
        lambda n: arriving[n].sibling_arrived(),
        offer,
        lambda n: gather_step(n // 4, n % 4),
        lambda n: scatter_step(n // 4, n % 4),
    )

    meet(place)
    for core in range(2):

        @on_core(place, core)
        def _():
            for copy in raw_copies(core):
                copy.start()

    for step in SCHEDULE:
        acts[step // 100](step % 100)

    for unit in range(sizes.units):
        clear(unit)
        leaving[unit].sent()
    for slot in range(5):
        for core in range(2):

            @on_core(place, core)
            def _():
                for away, kept in end_copies(core, slot):
                    away.wait_send()
                    kept.wait()
                for coming, _ in end_copies(1 - core, slot):
                    coming.wait_recv()

    for which in range(4):
        rows_sent(which)


def write_kernel(
    sizes, end_qkv, end_out, end_up, end_down, result, input_grad, end_small, steps,
    o_qkv, o_out, o_up, o_down, o_result, o_input, o_table, o_gains, o_shifts, o_biases, o_up_bias, *scratch,
):
    buffers, sems = scratch[:6], scratch[6]
    sources = (end_qkv, end_out, end_up, end_down, result, input_grad)
    targets = (o_qkv, o_out, o_up, o_down, o_result, o_input)
    loads = [pltpu.make_async_copy(a, b, sems.at[0, i]) for i, (a, b) in enumerate(zip(sources, buffers))]
    stores = [pltpu.make_async_copy(a, b, sems.at[1, i]) for i, (a, b) in enumerate(zip(buffers, targets))]
    for load in loads:
        load.start()
    for load, store in zip(loads, stores):
        load.wait()
        store.start()
    hot = (iota((o_table.shape[1], sizes.items), 0) == steps[...]).astype(BF16)
    o_table[...] = dot(end_small[:, 0 : sizes.items].astype(BF16), hot, 1, 1)
    own = sizes.own
    exact = functools.partial(
        lax.dot_general, precision=lax.Precision.HIGHEST, preferred_element_type=F32
    )
    eye = (iota((own, own), 0) == iota((own, own), 1)).astype(F32)
    lines = exact(end_small[:, sizes.small :], eye, (((0,), (0,)), ((), ())))
    begin = 0
    for ref in (o_gains, o_shifts, o_biases):
        ref[...] = lines[begin : begin + ref.shape[0]]
        begin += ref.shape[0]
    total = jnp.zeros(o_up_bias.shape, F32)
    for part in range(sizes.n_ff):
        moved = (iota((own, own * sizes.n_ff), 0) + part * own == iota((own, own * sizes.n_ff), 1)).astype(F32)
        total = total + exact(lines[begin + part : begin + part + 1], moved, (((1,), (0,)), ((), ())))
    o_up_bias[...] = total
    for store in stores:
        store.wait()


def row_by_row(
    inputs, time_table, w_qkv, w_out, w_up, w_down, norm_gains, norm_shifts, biases, up_bias,
    timesteps, item_map, lengths, cotangent,
):
    groups = lax.axis_size("seq")
    local, width = inputs.shape[1], inputs.shape[2]
    length = local * groups
    ff, items = w_down.shape[0], timesteps.shape[0]
    depth = lax.axis_size("dp") // 2
    sizes = Sizes(width, ff, lax.axis_size("dp") * groups, depth, items)
    half, rows, small, per = sizes.half, sizes.rows, sizes.small, sizes.n_ff

    steps = timesteps.reshape(1, items)
    shapes = sizes.weights()
    own_shapes = sizes.own_shapes()
    final_shapes = [(rows, small), (rows * 3, half), (rows, half), (rows * per, half), (rows, ff // 2)]
    row_shape = (groups, local, width)
    unit_sems = pltpu.SemaphoreType.DMA((sizes.units, 4))
    parts = len(sizes.raw_places()[0])
    smem = pl.BlockSpec(memory_space=pltpu.SMEM)
    scratch = (
        [pltpu.VMEM(shape, BF16) for shape in shapes]
        + [pltpu.VMEM(shapes[slot], BF16) for slot in (0, 3, 4)]
        + [pltpu.VMEM(tuple(reversed(ref.shape)), BF16) for ref in (time_table, w_qkv, w_out, w_up, w_down)]
        + [pltpu.VMEM(shape, F32) for shape in final_shapes]
        + [
            pltpu.VMEM((*sizes.chips, rows, small), BF16),
            pltpu.VMEM((sizes.units - 1, *sizes.chips, rows, half), BF16),
            pltpu.VMEM((*sizes.chips, rows, small), BF16),
            pltpu.VMEM((sizes.units - 1, *sizes.chips, rows, half), BF16),
            pltpu.VMEM(row_shape, BF16),
            pltpu.VMEM(row_shape, BF16),
        ]
        + [
            pltpu.VMEM((length, width), F32),
            pltpu.VMEM((length, width), BF16),
            pltpu.VMEM((length, 3 * width), BF16),
            pltpu.VMEM((length, width), BF16),
            pltpu.VMEM((length, 2 * HEAD_DIM), F32),
            pltpu.VMEM((length, width), F32),
            pltpu.VMEM((length, width), BF16),
            pltpu.VMEM((length, ff), BF16),
            pltpu.VMEM((length, ff), BF16),
            pltpu.VMEM(row_shape, BF16),
            pltpu.VMEM((length, width), F32),
            pltpu.VMEM((length // 2, length // 2), F32),
            pltpu.VMEM((length, small), BF16),
            pltpu.VMEM((16, width), F32),
            pltpu.VMEM((1, 3 * width), F32),
            pltpu.VMEM((1, ff), F32),
            pltpu.VMEM((width // per, width), BF16),
            pltpu.VMEM((16, width), F32),
            pltpu.VMEM((1, ff), F32),
            pltpu.VMEM((length, length), BF16),
        ]
        + [pltpu.SemaphoreType.DMA((5,))]
        + [pltpu.SemaphoreType.DMA((sizes.units + per, 4)), unit_sems, unit_sems]
        + [pltpu.SemaphoreType.DMA((parts,))] * 2
        + [pltpu.SemaphoreType.DMA((4,))] * 3
        + [pltpu.SemaphoreType.DMA((parts,))] * 3
    )
    row_type = jax.ShapeDtypeStruct(row_shape, BF16)
    landed = pl.pallas_call(
        functools.partial(layer_kernel, sizes),
        out_shape=tuple(jax.ShapeDtypeStruct(shape, F32) for shape in own_shapes) + (row_type, row_type),
        in_specs=[ANY] * 7 + [VMEM] * 5 + [smem] * 2,
        out_specs=(ANY,) * 7,
        scratch_shapes=scratch,
        compiler_params=pltpu.CompilerParams(collective_id=0, has_side_effects=True, vmem_limit_bytes=VMEM_LIMIT),
    )(
        inputs, cotangent, time_table.T, w_qkv.T, w_out.T, w_up.T, w_down.T, norm_gains, norm_shifts, biases, up_bias,
        steps, lengths, item_map,
    )
    end_small, *rest = landed
    moved = [jax.ShapeDtypeStruct(a.shape, a.dtype) for a in rest]
    written = pl.pallas_call(
        functools.partial(write_kernel, sizes),
        out_shape=(
            *moved,
            jax.ShapeDtypeStruct((sizes.own, time_table.shape[0]), F32),
            *(jax.ShapeDtypeStruct(a.shape, F32) for a in (norm_gains, norm_shifts, biases, up_bias)),
        ),
        in_specs=[ANY] * 6 + [VMEM] * 2,
        out_specs=(ANY,) * 6 + (VMEM,) * 5,
        scratch_shapes=[pltpu.VMEM(a.shape, a.dtype) for a in rest] + [pltpu.SemaphoreType.DMA((2, 6))],
    )(*rest, end_small, steps)
    qkv, out, up, down, result, input_grad, table, *small_grads = written
    return (result, input_grad, table.T, qkv.T, out.T, up.T, down.T, *small_grads)


def steps_of(sizes):
    pairs = HEADS // 2
    counts = [1] * 14
    counts += [sizes.depth // 2, pairs, sizes.depth, sizes.n_ff, sizes.n_ff, sizes.depth, pairs, sizes.depth // 2]
    counts += [4, 4, sizes.units, sizes.units, 4 * sizes.units, 4 * sizes.units]
    return [100 * kind + i for kind, count in enumerate(counts) for i in range(count)]


def on_device(*arrays):
    inputs, w_out, w_down, timesteps = arrays[0], arrays[3], arrays[5], arrays[10]
    width, ff = inputs.shape[2], w_down.shape[0]
    groups, data_count = lax.axis_size("seq"), lax.axis_size("dp")
    sizes = Sizes(width, ff, groups * data_count, data_count // 2, timesteps.shape[0])
    fits = (
        groups == 4
        and inputs.shape[0] == groups
        and data_count % 4 == 0
        and w_out.shape[1] % 8 == 0
        and ff % width == 0
        and width % 256 == 0
        and timesteps.shape[0] <= sizes.small
        and sizes.raw_places()[1] <= inputs.shape[1] * groups
        and steps_of(sizes) == sorted(SCHEDULE)
    )
    return row_by_row(*arrays) if fits else spread_out(*arrays)


def solution(mesh):
    return jax.shard_map(
        on_device,
        mesh=mesh,
        in_specs=(
            P(None, ("dp", "seq"), None),
            P(None, ("dp", "seq")),
            P(None, ("dp", "seq")),
            P(None, ("dp", "seq")),
            P(None, ("dp", "seq")),
            P(None, ("dp", "seq")),
            P(None, ("dp", "seq")),
            P(None, ("dp", "seq")),
            P(None, ("dp", "seq")),
            P(None, ("dp", "seq")),
            P(),
            P("dp"),
            P("dp", None),
            P(None, ("dp", "seq"), None),
        ),
        out_specs=(
            P(None, ("dp", "seq"), None),
            P(None, ("dp", "seq"), None),
            P(None, ("dp", "seq")),
            P(None, ("dp", "seq")),
            P(None, ("dp", "seq")),
            P(None, ("dp", "seq")),
            P(None, ("dp", "seq")),
            P(None, ("dp", "seq")),
            P(None, ("dp", "seq")),
            P(None, ("dp", "seq")),
            P(None, ("dp", "seq")),
        ),
        check_vma=False,
    )
```

```python
import functools

import jax
import jax.numpy as jnp
from jax import lax
from jax.experimental import pallas as pl
from jax.experimental.pallas import tpu as pltpu
from jax.sharding import PartitionSpec as P

HEADS = 12
HEAD_DIM = 64


EPS = 1e-05


def norm_rows(field, gain, offset):
    mean = jnp.mean(field, axis=-1, keepdims=True)
    centred = field - mean
    spread = jnp.mean(centred * centred, axis=-1, keepdims=True)
    return centred * lax.rsqrt(spread + EPS) * gain + offset


def gelu_exact(field):
    return jax.nn.gelu(field, approximate=False)


def scores_block(query_part, keys, query_segment, key_segment, scale):
    raw = scale * jnp.einsum("qhd,khd->hqk", query_part, keys, preferred_element_type=jnp.float32)
    keep = query_segment[None, :, None] == key_segment[None, None, :]
    return jnp.where(keep, raw, -1e30)


def attend_forward(queries, keys, values, segment, scale):
    score = scores_block(queries, keys, segment, segment, scale)
    top = jnp.max(score, axis=-1, keepdims=True)
    expo = jnp.exp(score - top)
    denom = jnp.sum(expo, axis=-1, keepdims=True)
    probs = (expo / denom).astype(jnp.bfloat16)
    results = jnp.einsum("hqk,khd->qhd", probs, values, preferred_element_type=jnp.float32).astype(
        jnp.bfloat16
    )
    log_totals = [top + jnp.log(denom)]
    return (results, log_totals)


def attend_backward(queries, keys, values, segment, log_totals, grad_out, scale):
    length = queries.shape[0]
    block = min(512, length)
    grad_keys = jnp.zeros(keys.shape, jnp.float32)
    grad_values = jnp.zeros(values.shape, jnp.float32)
    grad_queries = []
    for index, begin in enumerate(range(0, length, block)):
        score = scores_block(queries, keys, segment, segment, scale)
        probs = jnp.exp(score - log_totals[index])
        grad_values = jnp.einsum(
            "hqk,qhd->khd", probs.astype(jnp.bfloat16), grad_out, preferred_element_type=jnp.float32
        )
        grad_probs = jnp.einsum(
            "qhd,khd->hqk", grad_out, values, preferred_element_type=jnp.float32
        )
        centre = jnp.sum(probs * grad_probs, axis=-1, keepdims=True)
        grad_score = (probs * (grad_probs - centre)).astype(jnp.bfloat16)
        grad_queries.append(
            (
                scale
                * jnp.einsum("hqk,khd->qhd", grad_score, keys, preferred_element_type=jnp.float32)
            ).astype(jnp.bfloat16)
        )
        grad_keys = scale * jnp.einsum(
            "hqk,qhd->khd", grad_score, queries, preferred_element_type=jnp.float32
        )
    return (grad_queries[0], grad_keys.astype(jnp.bfloat16), grad_values.astype(jnp.bfloat16))


def spread_out(
    inputs,
    time_table,
    w_qkv,
    w_out,
    w_up,
    w_down,
    norm_gains,
    norm_shifts,
    biases,
    up_bias,
    timesteps,
    item_map,
    lengths,
    cotangent,
):
    micro = inputs.shape[0]
    local = inputs.shape[1]
    width = inputs.shape[2]
    groups = lax.axis_size("seq")
    data_count = lax.axis_size("dp")
    seq_len = local * groups
    items_row = lengths.shape[1]
    heads_dev = HEADS // groups
    group_width = width // groups
    scale = HEAD_DIM ** (-0.5)
    my_start = lax.axis_index("seq") * local
    places = jnp.arange(seq_len, dtype=jnp.int32)
    slot_index = jnp.arange(items_row, dtype=jnp.int32)
    step_index = jnp.arange(time_table.shape[0], dtype=jnp.int32)
    totals = None
    results = []
    input_grads = []
    for index in range(micro):
        gathered = (
            lax.all_gather(time_table, ("dp", "seq"), axis=1, tiled=True),
            lax.all_gather(w_qkv, ("dp", "seq"), axis=1, tiled=True),
            lax.all_gather(w_out, ("dp", "seq"), axis=1, tiled=True),
            lax.all_gather(w_up, ("dp", "seq"), axis=1, tiled=True),
            lax.all_gather(w_down, ("dp", "seq"), axis=1, tiled=True),
            lax.all_gather(norm_gains, ("dp", "seq"), axis=1, tiled=True),
            lax.all_gather(norm_shifts, ("dp", "seq"), axis=1, tiled=True),
            lax.all_gather(biases, ("dp", "seq"), axis=1, tiled=True),
            lax.all_gather(up_bias, ("dp", "seq"), axis=1, tiled=True),
        )
        (
            full_table,
            full_qkv,
            full_out,
            full_up,
            full_down,
            full_gains,
            full_shifts,
            full_biases,
            full_up_bias,
        ) = gathered
        gains = full_gains.astype(jnp.float32)
        offsets = full_shifts.astype(jnp.float32)
        bias_rows = full_biases.astype(jnp.float32)
        up_row = full_up_bias.astype(jnp.float32)[0]
        if totals is None:
            totals = [jnp.zeros(a.shape, jnp.float32) for a in gathered]
        ends = jnp.cumsum(lengths[index])
        segment = jnp.sum((ends[None, :] <= places[:, None]).astype(jnp.int32), axis=1)
        my_segment = lax.dynamic_slice_in_dim(segment, my_start, local)
        slot_steps = jnp.take(timesteps, item_map[index * items_row : (index + 1) * items_row])
        token_slot = (my_segment[:, None] == slot_index[None, :]).astype(jnp.bfloat16)
        step_hot = (slot_steps[:, None] == step_index[None, :]).astype(jnp.bfloat16)
        slot_rows = jnp.dot(step_hot, full_table, preferred_element_type=jnp.float32).astype(
            jnp.bfloat16
        )
        embedded = inputs[index].astype(jnp.float32) + jnp.dot(
            token_slot, slot_rows, preferred_element_type=jnp.float32
        )
        first_normed = norm_rows(embedded, gains[0], offsets[0]).astype(jnp.bfloat16)
        projected = jnp.dot(first_normed, full_qkv, preferred_element_type=jnp.float32)
        queries = (projected[:, 0:width] + bias_rows[0]).astype(jnp.bfloat16)
        keys = projected[:, width : 2 * width].astype(jnp.bfloat16)
        values = (projected[:, 2 * width : 3 * width] + bias_rows[1]).astype(jnp.bfloat16)
        head_queries, head_keys, head_values = (
            lax.all_to_all(
                queries.reshape(local, groups, group_width),
                "seq",
                split_axis=1,
                concat_axis=0,
                tiled=True,
            ),
            lax.all_to_all(
                keys.reshape(local, groups, group_width),
                "seq",
                split_axis=1,
                concat_axis=0,
                tiled=True,
            ),
            lax.all_to_all(
                values.reshape(local, groups, group_width),
                "seq",
                split_axis=1,
                concat_axis=0,
                tiled=True,
            ),
        )
        head_queries = head_queries.reshape(seq_len, heads_dev, HEAD_DIM)
        head_keys = head_keys.reshape(seq_len, heads_dev, HEAD_DIM)
        head_values = head_values.reshape(seq_len, heads_dev, HEAD_DIM)
        head_out, log_totals = attend_forward(head_queries, head_keys, head_values, segment, scale)
        attended = lax.all_to_all(
            head_out.reshape(seq_len, 1, group_width),
            "seq",
            split_axis=0,
            concat_axis=1,
            tiled=True,
        ).reshape(local, width)
        mid = (
            embedded
            + jnp.dot(attended, full_out, preferred_element_type=jnp.float32)
            + bias_rows[2]
        )
        second_normed = norm_rows(mid, gains[1], offsets[1]).astype(jnp.bfloat16)
        inner = jnp.dot(second_normed, full_up, preferred_element_type=jnp.float32) + up_row
        activated = gelu_exact(inner).astype(jnp.bfloat16)
        results.append(
            (
                mid
                + jnp.dot(activated, full_down, preferred_element_type=jnp.float32)
                + bias_rows[3]
            ).astype(jnp.bfloat16)
        )
        grad_output = cotangent[index]
        grad_down = jnp.einsum(
            "tf,td->fd", activated, grad_output, preferred_element_type=jnp.float32
        )
        bias_down = jnp.sum(grad_output.astype(jnp.float32), axis=0)
        grad_act = jnp.einsum(
            "td,fd->tf", grad_output, full_down, preferred_element_type=jnp.float32
        )
        unused, gelu_pull = jax.vjp(gelu_exact, inner)
        grad_inner = gelu_pull(grad_act)[0].astype(jnp.bfloat16)
        grad_up = jnp.einsum(
            "td,tf->df", second_normed, grad_inner, preferred_element_type=jnp.float32
        )
        grad_up_bias = jnp.sum(grad_inner.astype(jnp.float32), axis=0)
        upstream = jnp.einsum("tf,df->td", grad_inner, full_up, preferred_element_type=jnp.float32)
        unused, norm_pull = jax.vjp(norm_rows, mid, gains[1], offsets[1])
        back_mid, gain_second, shift_second = norm_pull(upstream)
        grad_mid = grad_output.astype(jnp.float32) + back_mid
        grad_branch = grad_mid.astype(jnp.bfloat16)
        grad_out_weight = jnp.einsum(
            "te,td->ed", attended, grad_branch, preferred_element_type=jnp.float32
        )
        bias_attend = jnp.sum(grad_branch.astype(jnp.float32), axis=0)
        grad_attended = jnp.einsum(
            "td,ed->te", grad_branch, full_out, preferred_element_type=jnp.float32
        ).astype(jnp.bfloat16)
        head_grad = lax.all_to_all(
            grad_attended.reshape(local, groups, group_width),
            "seq",
            split_axis=1,
            concat_axis=0,
            tiled=True,
        ).reshape(seq_len, heads_dev, HEAD_DIM)
        grad_q_heads, grad_k_heads, grad_v_heads = attend_backward(
            head_queries, head_keys, head_values, segment, log_totals, head_grad, scale
        )
        grad_queries, grad_keys, grad_values = (
            lax.all_to_all(
                grad_q_heads.reshape(seq_len, 1, group_width),
                "seq",
                split_axis=0,
                concat_axis=1,
                tiled=True,
            ),
            lax.all_to_all(
                grad_k_heads.reshape(seq_len, 1, group_width),
                "seq",
                split_axis=0,
                concat_axis=1,
                tiled=True,
            ),
            lax.all_to_all(
                grad_v_heads.reshape(seq_len, 1, group_width),
                "seq",
                split_axis=0,
                concat_axis=1,
                tiled=True,
            ),
        )
        grad_projected = jnp.concatenate(
            (
                grad_queries.reshape(local, width),
                grad_keys.reshape(local, width),
                grad_values.reshape(local, width),
            ),
            axis=1,
        )
        grad_qkv = jnp.einsum(
            "td,tc->dc", first_normed, grad_projected, preferred_element_type=jnp.float32
        )
        bias_query = jnp.sum(grad_queries.reshape(local, width).astype(jnp.float32), axis=0)
        bias_value = jnp.sum(grad_values.reshape(local, width).astype(jnp.float32), axis=0)
        upstream_first = jnp.einsum(
            "tc,dc->td", grad_projected, full_qkv, preferred_element_type=jnp.float32
        )
        unused, first_pull = jax.vjp(norm_rows, embedded, gains[0], offsets[0])
        back_first, gain_first, shift_first = first_pull(upstream_first)
        grad_embedded = grad_mid + back_first
        input_grads.append(grad_embedded.astype(jnp.bfloat16))
        slot_sums = jnp.einsum(
            "ts,td->sd",
            token_slot.astype(jnp.float32),
            grad_embedded,
            precision=lax.Precision.HIGHEST,
        )
        grad_table = jnp.einsum(
            "si,sd->id", step_hot.astype(jnp.float32), slot_sums, precision=lax.Precision.HIGHEST
        )
        grad_gains = jnp.stack((gain_first, gain_second), axis=0)
        grad_shifts = jnp.stack((shift_first, shift_second), axis=0)
        grad_biases = jnp.stack((bias_query, bias_value, bias_attend, bias_down), axis=0)
        grad_up_row = grad_up_bias[None, :]
        fresh = (
            grad_table,
            grad_qkv,
            grad_out_weight,
            grad_up,
            grad_down,
            grad_gains,
            grad_shifts,
            grad_biases,
            grad_up_row,
        )
        totals = [a + b for a, b in zip(totals, fresh)]

    def spread(grad):
        return grad.reshape(
            grad.shape[0], data_count, groups, grad.shape[1] // (data_count * groups)
        )

    parts = [spread(a) for a in totals]
    folded = (
        lax.all_to_all(
            parts[0].astype(jnp.bfloat16), "seq", split_axis=2, concat_axis=2, tiled=True
        ).astype(jnp.float32),
        lax.all_to_all(
            parts[1].astype(jnp.bfloat16), "seq", split_axis=2, concat_axis=2, tiled=True
        ).astype(jnp.float32),
        lax.all_to_all(
            parts[2].astype(jnp.bfloat16), "seq", split_axis=2, concat_axis=2, tiled=True
        ).astype(jnp.float32),
        lax.all_to_all(
            parts[3].astype(jnp.bfloat16), "seq", split_axis=2, concat_axis=2, tiled=True
        ).astype(jnp.float32),
        lax.all_to_all(
            parts[4].astype(jnp.bfloat16), "seq", split_axis=2, concat_axis=2, tiled=True
        ).astype(jnp.float32),
        lax.all_to_all(
            parts[5].astype(jnp.bfloat16), "seq", split_axis=2, concat_axis=2, tiled=True
        ).astype(jnp.float32),
        lax.all_to_all(
            parts[6].astype(jnp.bfloat16), "seq", split_axis=2, concat_axis=2, tiled=True
        ).astype(jnp.float32),
        lax.all_to_all(
            parts[7].astype(jnp.bfloat16), "seq", split_axis=2, concat_axis=2, tiled=True
        ).astype(jnp.float32),
        lax.all_to_all(
            parts[8].astype(jnp.bfloat16), "seq", split_axis=2, concat_axis=2, tiled=True
        ).astype(jnp.float32),
    )
    merged = [jnp.sum(f, axis=2, keepdims=True) for f in folded]
    owners = (
        lax.psum_scatter(merged[0], "dp", scatter_dimension=1, tiled=True),
        lax.psum_scatter(merged[1], "dp", scatter_dimension=1, tiled=True),
        lax.psum_scatter(merged[2], "dp", scatter_dimension=1, tiled=True),
        lax.psum_scatter(merged[3], "dp", scatter_dimension=1, tiled=True),
        lax.psum_scatter(merged[4], "dp", scatter_dimension=1, tiled=True),
        lax.psum_scatter(merged[5], "dp", scatter_dimension=1, tiled=True),
        lax.psum_scatter(merged[6], "dp", scatter_dimension=1, tiled=True),
        lax.psum_scatter(merged[7], "dp", scatter_dimension=1, tiled=True),
        lax.psum_scatter(merged[8], "dp", scatter_dimension=1, tiled=True),
    )
    owned = [o.reshape(o.shape[0], o.shape[3]) for o in owners]
    return (
        jnp.stack(results, axis=0),
        jnp.stack(input_grads, axis=0),
        owned[0],
        owned[1],
        owned[2],
        owned[3],
        owned[4],
        owned[5],
        owned[6],
        owned[7],
        owned[8],
    )


F32 = jnp.float32
BF16 = jnp.bfloat16
MESH = pl.DeviceIdType.MESH
VMEM_LIMIT = 63 << 20
VMEM = pl.BlockSpec(memory_space=pltpu.VMEM)
ANY = pl.BlockSpec(memory_space=pl.ANY)
ALL = slice(None)
class Place:
    def __init__(self):
        row, column = lax.axis_index("dp"), lax.axis_index("seq")
        self.at = {"z": row // 2, "y": row % 2, "x": column // 2}
        self.core = column % 2
        self.column = column
        self.depth = lax.axis_size("dp") // 2

    def device(self, core=None, **moved):
        at = {**self.at, **moved}
        core = self.core if core is None else core
        return (at["z"] * 2 + at["y"], at["x"] * 2 + core)

    def other(self, axis):
        return 1 - self.at[axis]

    def around(self, step):
        return (self.at["z"] + step) % self.depth

    def steps(self):
        upper = self.at["z"] // (self.depth // 2)
        return [step + upper * (self.depth - 2 * step) for step in range(1, self.depth)]

    def sibling(self):
        return self.device(core=1 - self.core)

    def partners(self):
        found = [self.sibling(), self.device(x=self.other("x")), self.device(y=self.other("y"))]
        found.append(self.device(core=1 - self.core, x=self.other("x")))
        found += [self.device(z=self.around(step)) for step in range(1, self.depth)]
        return found


def greet(place):
    barrier = pltpu.get_barrier_semaphore()
    for partner in place.partners():
        pl.semaphore_signal(barrier, inc=1, device_id=partner, device_id_type=MESH)


def meet(place):
    pl.semaphore_wait(pltpu.get_barrier_semaphore(), len(place.partners()))


def remote(source, target, send, receive, device):
    return pltpu.make_async_remote_copy(
        src_ref=source,
        dst_ref=target,
        send_sem=send,
        recv_sem=receive,
        device_id=device,
        device_id_type=MESH,
    )


def on_core(place, core):
    return pl.when(place.core == core)


class Route:
    def __init__(self, place, unit, kinds, view, send, receive):
        self.place, self.unit, self.kinds, self.view = place, unit, kinds, view
        self.send, self.receive = send, receive

    def kind(self, core):
        found = self.kinds[core][self.unit]
        return found < 2, "yx"[found % 2], "xy"[found % 2]

    def part(self, core, **moved):
        at = {**self.place.at, **moved}
        return self.view(at["z"], at["y"], at["x"], core)

    def copy(self, slot, source, target, device):
        return remote(source, target, self.send.at[slot], self.receive.at[slot], device)

    def over(self, axis):
        return self.place.device(**{axis: self.place.other(axis)})

    def on_each_core(self, act):
        for core in range(2):

            @on_core(self.place, core)
            def _():
                act(core)


class Gather(Route):
    def copies(self, core, name):
        place, depth = self.place, self.place.depth
        z_first, late, early = self.kind(core)
        spread = ALL if z_first else place.at["z"]
        if name == "z":
            block = self.part(core) if z_first else self.part(core, x=ALL, y=ALL)
            return [self.copy(0, block, block, place.device(z=place.around(step))) for step in place.steps()]
        if name == "sibling":
            block = self.part(core, z=ALL, y=ALL, x=ALL)
            return [self.copy(3, block, block, place.sibling())]
        moved = {early: place.other(early)} if name == "diagonal" else {}
        block = self.part(core, z=spread, **moved)
        return [self.copy(1 if name == "early" else 2, block, block, self.over(early if name == "early" else late))]

    def together(self, core, slot):
        z_first, late, early = self.kind(core)
        if slot == 0:
            moved = {} if z_first else {"x": ALL, "y": ALL}
            moved["z"] = pl.ds(0, self.place.depth - 1)
        elif slot == 3:
            moved = {"z": ALL, "y": ALL, "x": ALL}
        else:
            moved = {"z": ALL} if z_first else {}
            if slot == 2:
                moved[early] = ALL
        block = self.part(core, **moved)
        return self.copy(slot, block, block, self.place.sibling())

    def stages(self, core):
        if self.kind(core)[0]:
            return [((), ("z",)), ((0,), ("early", "late")), ((1,), ("diagonal",)), ((2,), ("sibling",))]
        return [((), ("early", "late")), ((1,), ("diagonal",)), ((2,), ("z",)), ((0,), ("sibling",))]

    def step(self, stage):
        def act(core):
            waits, starts = self.stages(core)[stage]
            for slot in waits:
                self.together(core, slot).wait_recv()
            for name in starts:
                for copy in self.copies(core, name):
                    copy.start()

        self.on_each_core(act)

    def sibling_arrived(self):
        self.on_each_core(lambda core: self.together(1 - core, 3).wait_recv())

    def sent(self):
        def act(core):
            for slot in range(4):
                self.together(core, slot).wait_send()

        self.on_each_core(act)


class Scatter(Route):
    def __init__(self, place, unit, kinds, view, first, landings, send, receive):
        super().__init__(place, unit, kinds, view, send, receive)
        self.first, self.landings = first, landings

    def sibling_copy(self, core):
        theirs = self.part(1 - core, z=ALL, y=ALL, x=ALL)
        return self.copy(3, theirs, self.first, self.place.sibling())

    def target(self, core, name):
        z_first, late, early = self.kind(core)
        if name == "z" and not z_first:
            return self.part(core, x=ALL, y=ALL)
        moved = {early: self.place.other(early)} if name == "diagonal" else {}
        if name != "z" and z_first:
            moved["z"] = ALL
        return self.part(core, **moved)

    def copies(self, core, name):
        place, depth = self.place, self.place.depth
        z_first, late, early = self.kind(core)
        z_land, diagonal, direct, near = self.landings(z_first)
        if name == "z":
            found = []
            rest = {} if z_first else {"x": ALL, "y": ALL}
            for step in place.steps():
                gone = self.part(core, z=place.around(step), **rest)
                landing = z_land.at[step - 1]
                found.append((self.copy(0, gone, landing, place.device(z=place.around(step))), landing))
            return found
        moved = {"z": ALL} if z_first else {}
        if name != "near":
            moved[late] = place.other(late)
        if name != "direct":
            moved[early] = place.other(early)
        slot, landing = {"direct": (1, direct), "near": (1, near), "diagonal": (2, diagonal)}[name]
        gone = self.part(core, **moved)
        return [(self.copy(slot, gone, landing, self.over(early if name == "near" else late)), landing)]

    def together(self, core, slot):
        z_first, late, early = self.kind(core)
        if slot == 0:
            moved = {} if z_first else {"x": ALL, "y": ALL}
            moved["z"] = pl.ds(0, self.place.depth - 1)
        else:
            moved = {"z": ALL} if z_first else {}
            if slot == 1:
                moved[early] = ALL
        block = self.part(core, **moved)
        return self.copy(slot, block, block, self.place.sibling())

    def stages(self, core):
        if self.kind(core)[0]:
            return [((), ("diagonal", "direct")), (("diagonal",), ("near",)), (("near", "direct"), ("z",)), (("z",), ())]
        return [((), ("z",)), (("z",), ("diagonal", "direct")), (("diagonal",), ("near",)), (("near", "direct"), ())]

    def start_sibling(self):
        self.on_each_core(lambda core: self.sibling_copy(core).start())

    def step(self, stage, result):
        def act(core):
            waits, starts = self.stages(core)[stage]
            if stage == 0:
                self.sibling_copy(core).wait_recv()
                mine = self.part(core, z=ALL, y=ALL, x=ALL)
                mine[...] = (mine[...].astype(F32) + self.first[...].astype(F32)).astype(BF16)
            if waits:
                self.together(core, {"z": 0, "near": 1, "diagonal": 2}[waits[0]]).wait_recv()
                target = self.target(core, waits[0])
                total = target[...].astype(F32)
                z_land, diagonal, direct, near = self.landings(self.kind(core)[0])
                came = {"near": near, "direct": direct, "diagonal": diagonal}
                for name in waits:
                    if name == "z":
                        for step in range(1, self.place.depth):
                            total = total + z_land[step - 1].astype(F32)
                    else:
                        total = total + came[name][...].astype(F32)
                if stage == 3:
                    result(core)[...] = total
                else:
                    target[...] = total.astype(BF16)
            for name in starts:
                for copy, _ in self.copies(core, name):
                    copy.start()

        self.on_each_core(act)

    def sent(self):
        def act(core):
            self.sibling_copy(core).wait_send()
            for slot in range(3):
                self.together(core, slot).wait_send()

        self.on_each_core(act)


GATHER_KINDS = (
    (2, 0, 0, 0, 2, 0, 0, 0, 0, 0, 2, 1, 3),
    (0, 1, 0, 1, 0, 1, 0, 1, 2, 1, 0, 0, 0),
)
SCATTER_KINDS = (
    (0, 0, 1, 0, 0, 0, 3, 0, 2, 0, 0, 0, 2),
    (0, 0, 2, 1, 0, 0, 1, 1, 0, 1, 0, 3, 1),
)
SCHEDULE = (
    2600, 2604, 2201, 2601, 0, 2608, 2612, 2632, 2616, 2605, 2609, 2613, 2602, 2606, 2620, 2617, 2648, 2614, 2624,
    2200, 2640, 2621, 2607, 2610, 2628, 2401, 2603, 2400, 2618, 2649, 100, 2636, 2615, 2629, 2403, 2611, 2633, 2625,
    2641, 2301, 400, 2644, 2300, 200, 2630, 2634, 2402, 2622, 1400, 1401, 1504, 2626, 1503, 1505, 2619, 2635, 1502,
    2637, 2650, 1500, 2631, 2404, 2408, 1501, 2642, 2627, 2645, 2623, 2407, 300, 2638, 2406, 2405, 1602, 1601, 1600,
    2646, 2651, 1702, 2511, 1700, 2509, 1701, 2639, 1603, 2643, 2744, 2647, 2409, 2736, 1703, 2412, 2510, 2411, 2512,
    2410, 1802, 1800, 1801, 1900, 2748, 1902, 1901, 1803, 2745, 2737, 1903, 800, 2507, 2740, 2506, 500, 2724, 2728,
    2508, 600, 700, 2732, 2741, 900, 1000, 2729, 2738, 2504, 2003, 2725, 2202, 2000, 2742, 2749, 2746, 2716, 2004,
    2002, 2001, 2005, 2733, 2750, 2505, 2100, 2101, 2502, 2726, 2720, 2501, 2717, 2743, 2503, 2708, 2730, 1100, 2721,
    2712, 1200, 1300, 2500, 2700, 2734, 2713, 2704, 2718, 2722, 2701, 2727, 2705, 2302, 2203, 2714, 2751, 2709, 2731,
    2747, 2706, 2702, 2710, 2715, 2723, 2735, 2719, 2739, 2303, 2707, 2711, 2703,
)


class Sizes:
    def __init__(self, width, ff, devices, depth, items):
        self.width, self.ff, self.devices, self.depth, self.items = width, ff, devices, depth, items
        self.half = width // 2
        self.own = width // devices
        self.rows = 2 * self.own
        self.n_qkv, self.n_ff = 3, ff // width
        self.small = 128
        self.units = 1 + self.n_qkv + 1 + 2 * self.n_ff
        self.chips = (depth, 2, 2)

    def weights(self):
        return [
            (*self.chips, self.rows, 2 * self.small),
            (*self.chips, self.n_qkv, self.rows, self.width),
            (*self.chips, self.rows, self.width),
            (*self.chips, self.n_ff, self.rows, self.width),
            (*self.chips, self.rows, self.ff),
        ]

    def own_shapes(self):
        widths = [2 * self.small, self.width, self.width, self.width, self.ff]
        return [(self.own * n, w) for n, w in zip((1, self.n_qkv, 1, self.n_ff, 1), widths)]

    def raw_places(self):
        shapes = [(slot, part, rows) for slot, rows, parts in (
            (0, self.own, 1), (1, self.n_qkv * self.own, 1), (2, self.own, 1),
            (3, self.n_ff * self.own, 1), (4, self.own, self.n_ff),
        ) for part in range(parts)]
        begin, found = 0, []
        for slot, part, rows in shapes:
            found.append([slot, part, rows, (begin, 0)])
            begin += rows
        tops = [begin, begin]
        for entry in found:
            side = 0 if entry[0] in (1, 2, 3) else 1
            entry.append((tops[side], side * self.half))
            entry.append(self.small if entry[0] == 0 else self.half)
            tops[side] += entry[2]
        return found, max(tops)

    def views(self, refs):
        small, qkv, out, up, down = refs
        half = self.half

        def columns(core, base=0, width=half):
            return pl.ds(base + core * width, width)

        found = [lambda z, y, x, core: small.at[z, y, x, :, columns(core, 0, self.small)]]
        for unit in range(self.n_qkv):
            found.append(lambda z, y, x, core, unit=unit: qkv.at[z, y, x, unit, :, columns(core)])
        found.append(out if callable(out) else lambda z, y, x, core: out.at[z, y, x, :, columns(core)])
        for unit in range(self.n_ff):
            found.append(lambda z, y, x, core, unit=unit: up.at[z, y, x, unit, :, columns(core)])
        for unit in range(self.n_ff):
            found.append(lambda z, y, x, core, unit=unit: down.at[z, y, x, :, columns(core, unit * self.width)])
        return found


def dot(a, b, ca, cb):
    return lax.dot_general(a, b, (((ca,), (cb,)), ((), ())), preferred_element_type=F32)


def iota(shape, axis):
    return lax.broadcasted_iota(jnp.int32, shape, axis)


def normalized(field):
    mean = jnp.mean(field, axis=-1, keepdims=True)
    centred = field - mean
    spread = jnp.mean(centred * centred, axis=-1, keepdims=True)
    rs = lax.rsqrt(spread + EPS)
    return centred * rs, rs


def loop(count, body):
    lax.fori_loop(0, count, lambda i, c: (body(i), c)[1], 0)


def span(i, size):
    return pl.ds(pl.multiple_of(i * size, size), size)


def flat(block, columns):
    return block.reshape(-1, columns)


TILE = 128


class Layer:
    def __init__(self, sizes, weights, grads, row_x, row_cot, scratch):
        self.s = sizes
        self.small, self.qkv_w, self.out_w, self.up_w, self.down_w = weights
        self.g_small, self.g_qkv, self.g_out, self.g_up, self.g_down = grads
        self.row_x, self.row_cot = row_x, row_cot
        (
            self.embedded, self.first, self.qkv, self.attended, self.log_total, self.mid, self.second,
            self.active, self.slope, self.result, self.total, self.bias, self.token_hot,
            self.lines, self.qkv_bias, self.up_row, self.spread, self.grad_lines, self.up_sum, self.turned,
        ) = scratch
        self.length = self.embedded.shape[0]


    def prepare(self, lengths, item_map, me):
        n, wide = self.length, self.s.small
        half = n // 2
        count = lengths.shape[1]
        sizes = [lengths[me, slot] for slot in range(count)]
        ends = [sizes[0]]
        for slot in range(1, count - 1):
            ends.append(ends[-1] + sizes[slot])
        items = [item_map[me * count + slot] for slot in range(count)]
        begin = ends[-1]
        for slot in range(count - 2, -1, -1):
            begin = jnp.where(sizes[slot] == half, ends[slot] - sizes[slot], begin)

        def position(index):
            moved = index + begin
            return jnp.where(moved >= n, moved - n, moved)

        def segment(index):
            return sum((position(index) >= end).astype(jnp.int32) for end in ends)

        columns = segment(iota((1, half), 1) + half)

        def masks(i):
            rows = segment(iota((TILE, 1), 0) + i * TILE + half)
            self.bias[span(i, TILE), :] = jnp.where(rows == columns, 0.0, -1e30)

        def hots(i):
            index = iota((TILE, 1), 0) + i * TILE
            rows = segment(index)
            item = jnp.full((TILE, 1), items[-1], jnp.int32)
            for slot in range(count - 1):
                item = jnp.where(rows == slot, items[slot], item)
            self.token_hot[span(i, TILE), :] = (item == iota((TILE, wide), 1)).astype(BF16)
            self.turned[span(i, TILE), :] = (position(index) == iota((TILE, n), 1)).astype(BF16)

        loop(half // TILE, masks)
        loop(n // TILE, hots)
        own, per = self.s.own, self.s.n_ff
        part = self.spread.shape[0]
        row, column = iota((part, 1), 0), iota((1, self.s.width), 1)
        same = (row // own == column // (per * own)) & (row % own == column % own)
        self.spread[...] = same.astype(BF16)

    def small_lines(self):
        s = self.s
        eye = (iota((16, s.small), 0) == iota((16, s.small), 1)).astype(BF16)
        lines = dot(eye, flat(self.small[:, :, :, :, s.small :], s.small), 1, 1)
        self.lines[...] = lines
        zero = jnp.zeros((1, s.width), F32)
        self.qkv_bias[...] = jnp.concatenate([lines[4:5], zero, lines[5:6]], axis=1)
        part = self.spread.shape[0]
        turn = (iota((1, s.width), 1) // s.own) % s.n_ff
        picked = turn == iota((s.n_ff, 1), 0)
        for tile in range(s.n_ff):
            seen = lines[8 : 8 + s.n_ff, tile * part : (tile + 1) * part].astype(BF16)
            moved = dot(seen, self.spread[...], 1, 0)
            self.up_row[:, tile * s.width : (tile + 1) * s.width] = jnp.sum(
                jnp.where(picked, moved, 0.0), axis=0, keepdims=True
            )
        self.grad_lines[...] = jnp.zeros_like(self.grad_lines)
        self.up_sum[...] = jnp.zeros_like(self.up_sum)

    def norm_first(self):
        gain, shift = self.lines[0:1, :], self.lines[2:3, :]
        items = flat(self.small[:, :, :, :, 0 : self.s.small], self.s.small)

        def body(i):
            field = dot(self.turned[span(i, TILE), :], flat(self.row_x[...], self.s.width), 1, 0)
            field = field + dot(self.token_hot[span(i, TILE), :], items, 1, 1)
            self.embedded[span(i, TILE), :] = field
            n, _ = normalized(field)
            self.first[span(i, TILE), :] = (n * gain + shift).astype(BF16)

        loop(self.length // TILE, body)

    def project(self, i):
        width = 2 * self.qkv_w.shape[1] * self.qkv_w.shape[2] * self.qkv_w.shape[3] * self.s.rows
        weight = flat(self.qkv_w[2 * i : 2 * i + 2], self.s.width)
        lanes = slice(i * width, (i + 1) * width)
        self.qkv[:, lanes] = (dot(self.first[...], weight, 1, 1) + self.qkv_bias[:, lanes]).astype(BF16)

    def heads(self, base, pair):
        return pl.ds(base + pair * 2 * HEAD_DIM, 2 * HEAD_DIM)

    def attend(self, pair):
        width, half = self.s.width, self.length // 2
        lane = iota((1, 2 * HEAD_DIM), 1)
        mine = [lane < HEAD_DIM, lane >= HEAD_DIM]
        scale = HEAD_DIM ** (-0.5)
        for part in range(2):
            rows = slice(part * half, (part + 1) * half)
            queries = self.qkv[rows, self.heads(0, pair)] * jnp.asarray(scale, BF16)
            keys = self.qkv[rows, self.heads(width, pair)]
            values = self.qkv[rows, self.heads(2 * width, pair)]
            logs = self.log_total[rows, :]
            found = []
            for head in range(2):
                one = jnp.where(mine[head], queries, jnp.zeros_like(queries))
                score = dot(one, keys, 1, 1)
                if part:
                    score = score + self.bias[...]
                top = jnp.max(score, axis=-1, keepdims=True)
                expo = jnp.exp(score - top)
                denom = jnp.sum(expo, axis=-1, keepdims=True)
                probs = (expo * (1.0 / denom)).astype(BF16)
                found.append(dot(probs, values, 1, 0))
                logs = jnp.where(lane == 2 * pair + head, top + jnp.log(denom), logs)
            self.log_total[rows, :] = logs
            self.attended[rows, self.heads(0, pair)] = jnp.where(mine[0], found[0], found[1]).astype(BF16)

    def merge(self):
        width = self.s.width
        for i in range(2):
            weight = flat(self.out_w[2 * i : 2 * i + 2], width)
            lanes = slice(i * weight.shape[0], (i + 1) * weight.shape[0])
            self.mid[:, lanes] = self.embedded[:, lanes] + dot(self.attended[...], weight, 1, 1) + self.lines[6:7, lanes]

    def norm_second(self):
        gain, shift = self.lines[1:2, :], self.lines[3:4, :]

        def body(i):
            n, _ = normalized(self.mid[span(i, TILE), :])
            self.second[span(i, TILE), :] = (n * gain + shift).astype(BF16)

        loop(self.length // TILE, body)

    def activate(self, z):
        half = self.s.ff // (2 * self.s.depth)
        for y in range(2):
            lanes = slice((2 * z + y) * half, (2 * z + y + 1) * half)
            weight = flat(self.up_w[z, y], self.s.width)
            inner = dot(self.second[...], weight, 1, 1) + self.up_row[:, lanes]
            mass = 0.5 + 0.5 * lax.erf(inner * (0.5**0.5))
            self.active[:, lanes] = (inner * mass).astype(BF16)
            bell = jnp.exp(-0.5 * inner * inner) * 0.3989422804014327
            self.slope[:, lanes] = (mass + inner * bell).astype(BF16)

    def finish(self):
        width = self.s.width
        for i in range(2):
            weight = flat(self.down_w[2 * i : 2 * i + 2], self.s.ff)
            lanes = slice(i * weight.shape[0], (i + 1) * weight.shape[0])
            field = self.mid[:, lanes] + dot(self.active[...], weight, 1, 1) + self.lines[7:8, lanes]
            field = dot(self.turned[...], field.astype(BF16), 0, 0).astype(BF16)
            self.result[:, :, lanes] = field.reshape(self.result.shape[0], -1, field.shape[1])


    def turn_cotangent(self):
        half = self.s.half
        for part in range(2):
            lanes = slice(part * half, (part + 1) * half)
            moved = dot(self.turned[...], flat(self.row_cot[:, :, lanes], half), 1, 0).astype(BF16)
            self.row_cot[:, :, lanes] = moved.reshape(self.row_cot.shape[0], -1, half)
        self.grad_lines[7:8, :] = jnp.sum(self.cotangent().astype(F32), axis=0, keepdims=True)

    def cotangent(self):
        return flat(self.row_cot[...], self.s.width)

    def grad_down(self, unit):
        width = self.s.width
        lanes = slice(unit * width, (unit + 1) * width)
        grad = dot(self.cotangent(), self.active[:, lanes], 0, 0).astype(BF16)
        self.g_down[:, :, :, :, lanes] = grad.reshape(*self.s.chips, self.s.rows, width)

    def back_active(self, unit):
        width = self.s.width
        for part in range(2):
            lanes = slice(unit * width + part * width // 2, unit * width + (part + 1) * width // 2)
            weight = flat(self.down_w[:, :, :, :, lanes], width // 2)
            grad = dot(self.cotangent(), weight, 1, 0)
            inner = (self.slope[:, lanes].astype(F32) * grad).astype(BF16)
            self.slope[:, lanes] = inner
            self.up_sum[:, lanes] = jnp.sum(inner.astype(F32), axis=0, keepdims=True)

    def grad_up(self, z):
        half = self.s.ff // (2 * self.s.depth)
        for y in range(2):
            lanes = slice((2 * z + y) * half, (2 * z + y + 1) * half)
            grad = dot(self.slope[:, lanes], self.second[...], 0, 0).astype(BF16)
            self.g_up[z, y] = grad.reshape(2, self.s.n_ff, self.s.rows, self.s.width)

    def back_up(self):
        half = self.s.half
        for part in range(2):
            lanes = slice(part * half, (part + 1) * half)
            weight = flat(self.up_w[:, :, :, :, :, lanes], half)
            self.total[:, lanes] = dot(self.slope[...], weight, 1, 0)

    def norm_second_back(self):
        gain = self.lines[1:2, :]
        zero = jnp.zeros((1, self.s.width), F32)

        def body(i, sums):
            upstream = self.total[span(i, TILE), :]
            n, rs = normalized(self.mid[span(i, TILE), :])
            u = upstream * gain
            back = rs * (u - jnp.mean(u, axis=-1, keepdims=True) - n * jnp.mean(u * n, axis=-1, keepdims=True))
            grad = self.row_cot[i].astype(F32) + back
            self.mid[span(i, TILE), :] = grad
            low = grad.astype(BF16)
            self.row_x[i] = low
            fresh = (upstream * n, upstream, low.astype(F32))
            return tuple(a + jnp.sum(b, axis=0, keepdims=True) for a, b in zip(sums, fresh))

        sums = lax.fori_loop(0, self.length // TILE, body, (zero, zero, zero))
        self.grad_lines[1:2, :] = sums[0]
        self.grad_lines[3:4, :] = sums[1]
        self.grad_lines[6:7, :] = sums[2]

    def grad_out(self):
        grad = dot(flat(self.row_x[...], self.s.width), self.attended[...], 0, 0).astype(BF16)
        self.g_out[...] = grad.reshape(*self.s.chips, self.s.rows, self.s.width)

    def back_out(self):
        weight = flat(self.out_w[...], self.s.width)
        self.attended[...] = dot(flat(self.row_x[...], self.s.width), weight, 1, 0).astype(BF16)

    def attend_back(self, pair):
        width, half = self.s.width, self.length // 2
        lane = iota((1, 2 * HEAD_DIM), 1)
        mine = [lane < HEAD_DIM, lane >= HEAD_DIM]
        scale = HEAD_DIM ** (-0.5)
        for part in range(2):
            rows = slice(part * half, (part + 1) * half)
            queries = self.qkv[rows, self.heads(0, pair)]
            keys = self.qkv[rows, self.heads(width, pair)]
            values = self.qkv[rows, self.heads(2 * width, pair)]
            grads = self.attended[rows, self.heads(0, pair)]
            scaled = queries * jnp.asarray(scale, BF16)
            logs = self.log_total[rows, :]
            found = []
            for head in range(2):
                one = jnp.where(mine[head], scaled, jnp.zeros_like(scaled))
                own = jnp.where(mine[head], grads, jnp.zeros_like(grads))
                log = jnp.sum(jnp.where(lane == 2 * pair + head, logs, 0.0), axis=-1, keepdims=True)
                score = dot(one, keys, 1, 1)
                if part:
                    score = score + self.bias[...]
                probs = jnp.exp(score - log)
                grad_probs = dot(own, values, 1, 1)
                centre = jnp.sum(probs * grad_probs, axis=-1, keepdims=True)
                grad_score = (probs * (grad_probs - centre)).astype(BF16)
                found.append(
                    (
                        scale * dot(grad_score, keys, 1, 0),
                        scale * dot(grad_score, queries, 0, 0),
                        dot(probs.astype(BF16), grads, 0, 0),
                    )
                )
            for slot in range(3):
                both = jnp.where(mine[0], found[0][slot], found[1][slot])
                self.qkv[rows, self.heads(slot * width, pair)] = both.astype(BF16)

    def grad_qkv(self, i):
        width, half = self.s.width, self.s.half
        span_z = 2 * self.qkv_w.shape[1] * self.qkv_w.shape[2] * self.qkv_w.shape[3] * self.s.rows
        lanes = slice(i * span_z, (i + 1) * span_z)
        for part in range(2):
            columns = slice(part * half, (part + 1) * half)
            grad = dot(self.qkv[:, lanes], self.first[:, columns], 0, 0).astype(BF16)
            self.g_qkv[2 * i : 2 * i + 2, :, :, 0 : self.s.n_qkv, :, columns] = grad.reshape(
                2, 2, 2, self.s.n_qkv, self.s.rows, half
            )

    def back_qkv(self):
        half = self.s.half
        for part in range(2):
            lanes = slice(part * half, (part + 1) * half)
            weight = flat(self.qkv_w[:, :, :, :, :, lanes], half)
            self.total[:, lanes] = dot(self.qkv[...], weight, 1, 0)

    def norm_first_back(self):
        gain = self.lines[0:1, :]
        width = self.s.width
        zero = jnp.zeros((1, width), F32)

        def body(i, sums):
            upstream = self.total[span(i, TILE), :]
            n, rs = normalized(self.embedded[span(i, TILE), :])
            u = upstream * gain
            back = rs * (u - jnp.mean(u, axis=-1, keepdims=True) - n * jnp.mean(u * n, axis=-1, keepdims=True))
            grad = self.mid[span(i, TILE), :] + back
            self.row_x[i] = grad.astype(BF16)
            projected = self.qkv[span(i, TILE), :].astype(F32)
            fresh = (upstream * n, upstream, projected[:, 0:width], projected[:, 2 * width :])
            return tuple(a + jnp.sum(b, axis=0, keepdims=True) for a, b in zip(sums, fresh))

        sums = lax.fori_loop(0, self.length // TILE, body, (zero,) * 4)
        self.grad_lines[0:1, :] = sums[0]
        self.grad_lines[2:3, :] = sums[1]
        self.grad_lines[4:5, :] = sums[2]
        self.grad_lines[5:6, :] = sums[3]

    def turn_input_grad(self):
        half = self.s.half
        for part in range(2):
            lanes = slice(part * half, (part + 1) * half)
            moved = dot(self.turned[...], flat(self.row_x[:, :, lanes], half), 0, 0).astype(BF16)
            self.row_cot[:, :, lanes] = moved.reshape(self.row_cot.shape[0], -1, half)

    def grad_small(self):
        s = self.s
        part = self.spread.shape[0]
        turn = (iota((1, s.width), 1) // s.own) % s.n_ff
        picked = turn == iota((s.n_ff, 1), 0)
        for tile in range(s.n_ff):
            seen = self.up_sum[:, tile * s.width : (tile + 1) * s.width]
            moved = dot(jnp.where(picked, seen, 0.0).astype(BF16), self.spread[...], 1, 1)
            self.grad_lines[8 : 8 + s.n_ff, tile * part : (tile + 1) * part] = moved
        eye = (iota((16, s.small), 0) == iota((16, s.small), 1)).astype(BF16)
        lines = dot(self.grad_lines[...].astype(BF16), eye, 0, 0).astype(BF16)
        self.g_small[:, :, :, :, s.small :] = lines.reshape(*s.chips, s.rows, s.small)
        sums = dot(flat(self.row_x[...], s.width), self.token_hot[...], 0, 0).astype(BF16)
        self.g_small[:, :, :, :, 0 : s.small] = sums.reshape(*s.chips, s.rows, s.small)


def layer_kernel(
    sizes, inputs, cotangent, table, qkv, out, up, down, gains, shifts, biases, up_bias, steps, lengths, item_map,
    end_small, end_qkv, end_out, end_up, end_down, result, input_grad,
    w_small, w_qkv, w_out, w_up, w_down, g_small, g_up, g_down,
    raw_table, raw_qkv, raw_out, raw_up, raw_down,
    f_small, f_qkv, f_out, f_up, f_down,
    first_small, first, pool_small, pool, row_x, row_cot, *rest,
):
    scratch, sems = rest[:20], rest[20:]
    (
        loads, send, receive, back_receive, raw_send, raw_receive, row_send, row_receive, row_local,
        end_send, end_receive, end_local,
    ) = sems
    place = Place()
    half, depth = sizes.half, sizes.depth
    me = place.column
    groups = inputs.shape[0]
    weights = [w_small, w_qkv, w_out, w_up, w_down]
    finals = [f_small, f_qkv, f_out, f_up, f_down]
    ends = [end_small, end_qkv, end_out, end_up, end_down]
    grad_out = w_up.at[:, :, :, sizes.n_qkv]
    layer = Layer(sizes, weights, [g_small, w_up, grad_out, g_up, g_down], row_x, row_cot, scratch)

    def width_of(slot):
        return sizes.small if slot == 0 else half

    raws = [
        pltpu.make_async_copy(source, target, loads.at[i])
        for i, (source, target) in enumerate(
            ((table, raw_table), (qkv, raw_qkv), (out, raw_out), (up, raw_up), (down, raw_down))
        )
    ]
    for copy in raws:
        copy.start()
    greet(place)
    lane = iota((1, sizes.small), 1)
    columns = jnp.zeros((sizes.own, sizes.small), F32)
    begin = 0
    for ref in (gains, shifts, biases):
        count = ref.shape[0]
        picked = (iota((count, sizes.small), 1) == iota((count, sizes.small), 0) + begin).astype(BF16)
        columns = columns + dot(ref[...], picked, 0, 0)
        begin += count
    for part in range(sizes.n_ff):
        piece = up_bias[:, part * sizes.own : (part + 1) * sizes.own]
        columns = columns + dot(piece, (lane == begin + part).astype(BF16), 0, 0)
    pieces = []
    for slot, part, count, (row, column), (far_row, far_column), wide in sizes.raw_places()[0]:
        here = layer.total.at[pl.ds(row, count), pl.ds(column, 2 * wide)]
        there = layer.total.at[pl.ds(far_row, count), pl.ds(far_column, wide)]
        pieces.append((slot, part, here, there, wide))
    own_small = pieces[0][2]
    raws[0].wait()
    hot = (iota((table.shape[1], sizes.items), 0) == steps[...]).astype(BF16)
    own_small[:, 0 : sizes.small] = jnp.zeros((sizes.own, sizes.small), F32)
    own_small[:, 0 : sizes.items] = dot(raw_table[...], hot, 1, 0)
    own_small[:, sizes.small :] = columns
    for copy in raws[1:]:
        copy.wait()
    for slot, part, here, _, _ in pieces[1:]:
        source = (raw_qkv, raw_out, raw_up, raw_down)[slot - 1]
        here[...] = source[:, part * sizes.width : (part + 1) * sizes.width].astype(F32)

    rows = [(inputs, row_x), (cotangent, row_cot), (layer.result, result), (row_cot, input_grad)]

    def row_copies(which):
        source, target = rows[which]
        found = []
        for step in range(1, groups):
            peer = (me + step) % groups
            device = (lax.axis_index("dp"), peer)
            found.append(remote(source.at[peer], target.at[me], row_send.at[which], row_receive.at[which], device))
        return found

    def row_local_copy(which):
        source, target = rows[which]
        return pltpu.make_async_copy(source.at[me], target.at[me], row_local.at[which])

    def start_rows(which):
        for copy in [*row_copies(which), row_local_copy(which)]:
            copy.start()

    def rows_together(which):
        source, target = (ref.at[pl.ds(0, groups - 1)] for ref in rows[which])
        return remote(source, target, row_send.at[which], row_receive.at[which], place.sibling())

    def rows_arrived(which):
        rows_together(which).wait_recv()
        row_local_copy(which).wait()

    def rows_sent(which):
        rows_together(which).wait_send()

    def raw_copies(core, slots=range(5)):
        return [
            remote(
                here.at[:, pl.ds((1 - core) * wide, wide)], there, raw_send.at[i], raw_receive.at[i], place.sibling()
            )
            for i, (slot, _, here, there, wide) in enumerate(pieces)
            if slot in slots
        ]

    def place_own(slot):
        z, y, x = (place.at[a] for a in "zyx")
        for core in range(2):

            @on_core(place, core)
            def _():
                for copy in raw_copies(core, [slot]):
                    copy.wait()
                for _, part, mine, theirs, wide in [piece for piece in pieces if piece[0] == slot]:
                    here, there = mine[:, core * wide : (core + 1) * wide], theirs[...]
                    block = jnp.concatenate([here, there] if core == 0 else [there, here], axis=0).astype(BF16)
                    lanes = pl.ds((2 * part + core) * wide, wide)
                    if weights[slot].ndim == 6:
                        for unit in range(weights[slot].shape[3]):
                            weights[slot][z, y, x, unit, :, lanes] = block[unit * sizes.rows : (unit + 1) * sizes.rows]
                    else:
                        weights[slot][z, y, x, :, lanes] = block

    arriving = [
        Gather(place, unit, GATHER_KINDS, view, send.at[unit], receive.at[unit])
        for unit, view in enumerate(sizes.views(weights))
    ]

    spots = [(0, 0)] + [(1, u) for u in range(sizes.n_qkv)] + [(2, 0)]
    spots += [(3, u) for u in range(sizes.n_ff)] + [(4, u) for u in range(sizes.n_ff)]
    views = sizes.views([g_small, w_up, lambda z, y, x, core: w_up.at[z, y, x, sizes.n_qkv, :, pl.ds(core * half, half)], g_up, g_down])
    def landings(unit, z_first):
        here = (lambda *i: pool_small.at[i]) if unit == 0 else (lambda *i: pool.at[(unit - 1, *i)])
        some = pl.ds(0, depth - 1)
        if z_first:
            return here(some, 1, 1), here(ALL, 0, 0), here(ALL, 0, 1), here(ALL, 1, 0)
        return here(some), here(depth - 1, 0, 0), here(depth - 1, 0, 1), here(depth - 1, 1, 0)

    def send_row(unit):
        slot, part = spots[unit]
        return sizes.units + part if slot == 4 else unit

    leaving = [
        Scatter(
            place, unit, SCATTER_KINDS, view, first_small if unit == 0 else first.at[unit - 1],
            functools.partial(landings, unit), send.at[send_row(unit)], back_receive.at[unit],
        )
        for unit, view in enumerate(views)
    ]

    def final(unit):
        slot, part = spots[unit]
        if slot == 4:
            return lambda core: finals[slot].at[:, pl.ds(part * half, half)]
        return lambda core: finals[slot].at[pl.ds(part * sizes.rows, sizes.rows), :]

    def end_copies(core, slot):
        wide = width_of(slot)
        count = ends[slot].shape[0]
        found = []
        for part in range(finals[slot].shape[1] // wide):
            at = slot + part
            columns = pl.ds(part * wide, wide)
            target = ends[slot].at[:, pl.ds((2 * part + core) * wide, wide)]
            gone = finals[slot].at[pl.ds((1 - core) * count, count), columns]
            kept = finals[slot].at[pl.ds(core * count, count), columns]
            found.append(
                (
                    remote(gone, target, end_send.at[at], end_receive.at[at], place.sibling()),
                    pltpu.make_async_copy(kept, target, end_local.at[at]),
                )
            )
        return found

    def close(slot):
        for core in range(2):

            @on_core(place, core)
            def _():
                for pair in end_copies(core, slot):
                    for copy in pair:
                        copy.start()

    done, placed, cleared = [], [], []

    def clear(unit):
        if unit not in cleared:
            cleared.append(unit)
            arriving[unit].sent()

    def offer(unit):
        if spots[unit][0] != 4:
            clear(unit)
        leaving[unit].start_sibling()

    def gather_step(unit, stage):
        slot = spots[unit][0]
        if slot not in placed:
            placed.append(slot)
            place_own(slot)
        arriving[unit].step(stage)

    def scatter_step(unit, stage):
        leaving[unit].step(stage, final(unit))
        if stage == 3:
            done.append(unit)
            slot = spots[unit][0]
            if all(other in done for other in range(sizes.units) if spots[other][0] == slot):
                close(slot)

    def merge():
        layer.merge()
        layer.norm_second()

    def gathered_up():
        for unit, (slot, _) in enumerate(spots):
            if slot == 3:
                clear(unit)

    def end_input_grad():
        layer.norm_first_back()
        layer.turn_input_grad()

    acts = (
        lambda _: layer.prepare(lengths, item_map, me),
        lambda _: layer.small_lines(),
        lambda _: layer.norm_first(),
        lambda _: merge(),
        lambda _: layer.turn_cotangent(),
        lambda _: layer.finish(),
        lambda _: layer.back_up(),
        lambda _: layer.norm_second_back(),
        lambda _: gathered_up(),
        lambda _: layer.grad_out(),
        lambda _: layer.back_out(),
        lambda _: layer.back_qkv(),
        lambda _: end_input_grad(),
        lambda _: layer.grad_small(),
        layer.project,
        layer.attend,
        layer.activate,
        layer.grad_down,
        layer.back_active,
        layer.grad_up,
        layer.attend_back,
        layer.grad_qkv,
        start_rows,
        rows_arrived,
        lambda n: arriving[n].sibling_arrived(),
        offer,
        lambda n: gather_step(n // 4, n % 4),
        lambda n: scatter_step(n // 4, n % 4),
    )

    meet(place)
    for core in range(2):

        @on_core(place, core)
        def _():
            for copy in raw_copies(core):
                copy.start()

    for step in SCHEDULE:
        acts[step // 100](step % 100)

    for unit in range(sizes.units):
        clear(unit)
        leaving[unit].sent()
    for slot in range(5):
        for core in range(2):

            @on_core(place, core)
            def _():
                for away, kept in end_copies(core, slot):
                    away.wait_send()
                    kept.wait()
                for coming, _ in end_copies(1 - core, slot):
                    coming.wait_recv()

    for which in range(4):
        rows_sent(which)


def write_kernel(
    sizes, end_qkv, end_out, end_up, end_down, result, input_grad, end_small, steps,
    o_qkv, o_out, o_up, o_down, o_result, o_input, o_table, o_gains, o_shifts, o_biases, o_up_bias, *scratch,
):
    buffers, sems = scratch[:6], scratch[6]
    sources = (end_qkv, end_out, end_up, end_down, result, input_grad)
    targets = (o_qkv, o_out, o_up, o_down, o_result, o_input)
    loads = [pltpu.make_async_copy(a, b, sems.at[0, i]) for i, (a, b) in enumerate(zip(sources, buffers))]
    stores = [pltpu.make_async_copy(a, b, sems.at[1, i]) for i, (a, b) in enumerate(zip(buffers, targets))]
    for load in loads:
        load.start()
    for load, store in zip(loads, stores):
        load.wait()
        store.start()
    hot = (iota((o_table.shape[1], sizes.items), 0) == steps[...]).astype(BF16)
    o_table[...] = dot(end_small[:, 0 : sizes.items].astype(BF16), hot, 1, 1)
    own = sizes.own
    exact = functools.partial(
        lax.dot_general, precision=lax.Precision.HIGHEST, preferred_element_type=F32
    )
    eye = (iota((own, own), 0) == iota((own, own), 1)).astype(F32)
    lines = exact(end_small[:, sizes.small :], eye, (((0,), (0,)), ((), ())))
    begin = 0
    for ref in (o_gains, o_shifts, o_biases):
        ref[...] = lines[begin : begin + ref.shape[0]]
        begin += ref.shape[0]
    total = jnp.zeros(o_up_bias.shape, F32)
    for part in range(sizes.n_ff):
        moved = (iota((own, own * sizes.n_ff), 0) + part * own == iota((own, own * sizes.n_ff), 1)).astype(F32)
        total = total + exact(lines[begin + part : begin + part + 1], moved, (((1,), (0,)), ((), ())))
    o_up_bias[...] = total
    for store in stores:
        store.wait()


def row_by_row(
    inputs, time_table, w_qkv, w_out, w_up, w_down, norm_gains, norm_shifts, biases, up_bias,
    timesteps, item_map, lengths, cotangent,
):
    groups = lax.axis_size("seq")
    local, width = inputs.shape[1], inputs.shape[2]
    length = local * groups
    ff, items = w_down.shape[0], timesteps.shape[0]
    depth = lax.axis_size("dp") // 2
    sizes = Sizes(width, ff, lax.axis_size("dp") * groups, depth, items)
    half, rows, small, per = sizes.half, sizes.rows, sizes.small, sizes.n_ff

    steps = timesteps.reshape(1, items)
    shapes = sizes.weights()
    own_shapes = sizes.own_shapes()
    final_shapes = [(rows, small), (rows * 3, half), (rows, half), (rows * per, half), (rows, ff // 2)]
    row_shape = (groups, local, width)
    unit_sems = pltpu.SemaphoreType.DMA((sizes.units, 4))
    parts = len(sizes.raw_places()[0])
    smem = pl.BlockSpec(memory_space=pltpu.SMEM)
    scratch = (
        [pltpu.VMEM(shape, BF16) for shape in shapes]
        + [pltpu.VMEM(shapes[slot], BF16) for slot in (0, 3, 4)]
        + [pltpu.VMEM(tuple(reversed(ref.shape)), BF16) for ref in (time_table, w_qkv, w_out, w_up, w_down)]
        + [pltpu.VMEM(shape, F32) for shape in final_shapes]
        + [
            pltpu.VMEM((*sizes.chips, rows, small), BF16),
            pltpu.VMEM((sizes.units - 1, *sizes.chips, rows, half), BF16),
            pltpu.VMEM((*sizes.chips, rows, small), BF16),
            pltpu.VMEM((sizes.units - 1, *sizes.chips, rows, half), BF16),
            pltpu.VMEM(row_shape, BF16),
            pltpu.VMEM(row_shape, BF16),
        ]
        + [
            pltpu.VMEM((length, width), F32),
            pltpu.VMEM((length, width), BF16),
            pltpu.VMEM((length, 3 * width), BF16),
            pltpu.VMEM((length, width), BF16),
            pltpu.VMEM((length, 2 * HEAD_DIM), F32),
            pltpu.VMEM((length, width), F32),
            pltpu.VMEM((length, width), BF16),
            pltpu.VMEM((length, ff), BF16),
            pltpu.VMEM((length, ff), BF16),
            pltpu.VMEM(row_shape, BF16),
            pltpu.VMEM((length, width), F32),
            pltpu.VMEM((length // 2, length // 2), F32),
            pltpu.VMEM((length, small), BF16),
            pltpu.VMEM((16, width), F32),
            pltpu.VMEM((1, 3 * width), F32),
            pltpu.VMEM((1, ff), F32),
            pltpu.VMEM((width // per, width), BF16),
            pltpu.VMEM((16, width), F32),
            pltpu.VMEM((1, ff), F32),
            pltpu.VMEM((length, length), BF16),
        ]
        + [pltpu.SemaphoreType.DMA((5,))]
        + [pltpu.SemaphoreType.DMA((sizes.units + per, 4)), unit_sems, unit_sems]
        + [pltpu.SemaphoreType.DMA((parts,))] * 2
        + [pltpu.SemaphoreType.DMA((4,))] * 3
        + [pltpu.SemaphoreType.DMA((parts,))] * 3
    )
    row_type = jax.ShapeDtypeStruct(row_shape, BF16)
    landed = pl.pallas_call(
        functools.partial(layer_kernel, sizes),
        out_shape=tuple(jax.ShapeDtypeStruct(shape, F32) for shape in own_shapes) + (row_type, row_type),
        in_specs=[ANY] * 7 + [VMEM] * 5 + [smem] * 2,
        out_specs=(ANY,) * 7,
        scratch_shapes=scratch,
        compiler_params=pltpu.CompilerParams(collective_id=0, has_side_effects=True, vmem_limit_bytes=VMEM_LIMIT),
    )(
        inputs, cotangent, time_table.T, w_qkv.T, w_out.T, w_up.T, w_down.T, norm_gains, norm_shifts, biases, up_bias,
        steps, lengths, item_map,
    )
    end_small, *rest = landed
    moved = [jax.ShapeDtypeStruct(a.shape, a.dtype) for a in rest]
    written = pl.pallas_call(
        functools.partial(write_kernel, sizes),
        out_shape=(
            *moved,
            jax.ShapeDtypeStruct((sizes.own, time_table.shape[0]), F32),
            *(jax.ShapeDtypeStruct(a.shape, F32) for a in (norm_gains, norm_shifts, biases, up_bias)),
        ),
        in_specs=[ANY] * 6 + [VMEM] * 2,
        out_specs=(ANY,) * 6 + (VMEM,) * 5,
        scratch_shapes=[pltpu.VMEM(a.shape, a.dtype) for a in rest] + [pltpu.SemaphoreType.DMA((2, 6))],
    )(*rest, end_small, steps)
    qkv, out, up, down, result, input_grad, table, *small_grads = written
    return (result, input_grad, table.T, qkv.T, out.T, up.T, down.T, *small_grads)


def steps_of(sizes):
    pairs = HEADS // 2
    counts = [1] * 14
    counts += [sizes.depth // 2, pairs, sizes.depth, sizes.n_ff, sizes.n_ff, sizes.depth, pairs, sizes.depth // 2]
    counts += [4, 4, sizes.units, sizes.units, 4 * sizes.units, 4 * sizes.units]
    return [100 * kind + i for kind, count in enumerate(counts) for i in range(count)]


def on_device(*arrays):
    inputs, w_out, w_down, timesteps = arrays[0], arrays[3], arrays[5], arrays[10]
    width, ff = inputs.shape[2], w_down.shape[0]
    groups, data_count = lax.axis_size("seq"), lax.axis_size("dp")
    sizes = Sizes(width, ff, groups * data_count, data_count // 2, timesteps.shape[0])
    fits = (
        groups == 4
        and inputs.shape[0] == groups
        and data_count % 4 == 0
        and w_out.shape[1] % 8 == 0
        and ff % width == 0
        and width % 256 == 0
        and timesteps.shape[0] <= sizes.small
        and sizes.raw_places()[1] <= inputs.shape[1] * groups
        and steps_of(sizes) == sorted(SCHEDULE)
    )
    return row_by_row(*arrays) if fits else spread_out(*arrays)


def solution(mesh):
    return jax.shard_map(
        on_device,
        mesh=mesh,
        in_specs=(
            P(None, ("dp", "seq"), None),
            P(None, ("dp", "seq")),
            P(None, ("dp", "seq")),
            P(None, ("dp", "seq")),
            P(None, ("dp", "seq")),
            P(None, ("dp", "seq")),
            P(None, ("dp", "seq")),
            P(None, ("dp", "seq")),
            P(None, ("dp", "seq")),
            P(None, ("dp", "seq")),
            P(),
            P("dp"),
            P("dp", None),
            P(None, ("dp", "seq"), None),
        ),
        out_specs=(
            P(None, ("dp", "seq"), None),
            P(None, ("dp", "seq"), None),
            P(None, ("dp", "seq")),
            P(None, ("dp", "seq")),
            P(None, ("dp", "seq")),
            P(None, ("dp", "seq")),
            P(None, ("dp", "seq")),
            P(None, ("dp", "seq")),
            P(None, ("dp", "seq")),
            P(None, ("dp", "seq")),
            P(None, ("dp", "seq")),
        ),
        check_vma=False,
    )
```
